32 devices in a mesh: nest: 2 (over core), bin: 16 (over z, y, x).
Axes of the slice: x: 2, y: 2, z: 4, core: 2. Of those that a mesh axis runs over, the one named last changes fastest.
Arguments:
- spectra: float32 [2, 1152, 1024], P('nest', 'bin'), may hold values from 0.05 to 2
- courant: float32 [2, 1152], P(None, 'bin'), may hold values from -0.9 to 0.9
- coupling: bfloat16 [1152, 1152], replicated, may hold values from -0.1875 to 0.1875
- growth: float32 [1152], replicated, may hold values from 0.05 to 0.5
- dissipation: float32 [1152], replicated, may hold values from 0.2 to 2
- wind: float32 [2, 1024], P('nest'), may hold values from 0.5 to 2
- neighbours: int32 [2, 4, 1024], P('nest'), may hold values from 0 to 1023, as said below
- wet_mask: int32 [2, 1024], P('nest'), may hold values from 0 to 1, as said below
- send_list: int32 [2, 256], P('nest'), may hold values from 0 to 1023, as said below
- recv_list: int32 [2, 256], P('nest'), may hold values from 0 to 1023, as said below
- substep_count: int32 [2], P('nest'), may hold values from 1 to 2, as said below
Outputs:
- new_spectra: float32 [2, 1152, 1024], P('nest', 'bin')
The draws below stay inside these ranges and needn't reach their ends.
Inputs may be any that keep to these rules, and one draw needn't show every extreme that they name: `neighbours`: row 0 holds each point's east neighbour, row 1 west, row 2 north, row 3 south, on a periodic grid of 4 rows of 256 points; grid row r holds the point numbers r * 256 to (r + 1) * 256 - 1 in some order. `wet_mask`: exactly 512 points of each nest are sea points. `send_list`: distinct sea points of the nest, none of them in recv_list of the same nest. `recv_list`: distinct sea points of the nest. `substep_count`: some nest takes 2 substeps.
All inputs are finite; a program needn't handle non-finite values.
Results may differ from the reference program's by a relative error of at most 0.0012.
Values sent between devices are 32-bit elements; how exact they have to be, the bound alone decides.
No kernel may reach another device: no remote copies, remote signals or barrier semaphores. Data moves between devices by JAX's collectives and lax.ppermute only.
A program may use at most 64 MiB of HBM per device.

```python
import math
import jax
import jax.numpy as jnp
from jax import lax

K = 1152
SUBSTEPS = 2
SRC = 5
NESTS = 2
POINTS = 1024
GX = 256
GY = 4
WET = 512
NB = 256


def geometry(key, nest_id):
    base_key = jax.random.fold_in(jax.random.fold_in(key, 1237), nest_id)
    key_rows, key_level, key_cols, key_noise, key_pick = jax.random.split(base_key, 5)
    row_keys = jax.random.split(key_rows, GY)
    perms = jax.vmap(lambda row_key: jax.random.permutation(row_key, GX))(row_keys).astype(jnp.int32)
    inverse = jnp.argsort(perms, axis=1, stable=True).astype(jnp.int32)
    cell = (jnp.arange(GY, dtype=jnp.int32)[:, None] * GX + inverse).astype(jnp.int32)
    column = perms.reshape(-1)
    row_of = jnp.repeat(jnp.arange(GY, dtype=jnp.int32), GX)
    east_index = cell[row_of, (column + 1) % GX]
    west_index = cell[row_of, (column + GX - 1) % GX]
    north_index = cell[(row_of + 1) % GY, column]
    south_index = cell[(row_of + GY - 1) % GY, column]
    tables = jnp.stack([east_index, west_index, north_index, south_index]).astype(jnp.int32)
    row_level = jax.random.randint(key_level, (GY,), 0, 4)
    col_level = jax.random.randint(key_cols, (GX,), 0, 4)
    noise = jax.random.randint(key_noise, (POINTS,), 0, 3)
    score = (row_level[row_of] + col_level[column]) * 4 + noise
    order = jnp.argsort(score, stable=True).astype(jnp.int32)
    sea_int = jnp.zeros((POINTS,), jnp.int32).at[order[:WET]].set(1)
    pick = jax.random.randint(key_pick, (POINTS,), 0, 1 << 20)
    pick = jnp.where(sea_int == 1, pick, 1 << 21)
    chosen = jnp.argsort(pick, stable=True).astype(jnp.int32)
    return (tables, sea_int, chosen[:NB], chosen[NB:2 * NB])


def draw_neighbours(key, part):
    return jnp.stack([geometry(key, nest_id)[0] for nest_id in range(NESTS)]).astype(jnp.int32)


def draw_wet_mask(key, part):
    return jnp.stack([geometry(key, nest_id)[1] for nest_id in range(NESTS)]).astype(jnp.int32)


def draw_send_list(key, part):
    return jnp.stack([geometry(key, nest_id)[2] for nest_id in range(NESTS)]).astype(jnp.int32)


def draw_recv_list(key, part):
    return jnp.stack([geometry(key, nest_id)[3] for nest_id in range(NESTS)]).astype(jnp.int32)


def draw_substep_count(key, part):
    base_key = jax.random.fold_in(key, 4421)
    key_big, key_rest = jax.random.split(base_key)
    busiest = jax.random.randint(key_big, (), 0, NESTS)
    others = jax.random.randint(key_rest, (NESTS,), 1, SUBSTEPS + 1)
    return jnp.where(jnp.arange(NESTS) == busiest, SUBSTEPS, others).astype(jnp.int32)


def level_of(rng, extent, pieces, smallest, largest):
    level, own = 1.0, jax.random.fold_in(rng, 6)
    for axis_at, blocks in pieces:
        heights = jnp.exp(jax.random.uniform(jax.random.fold_in(own, axis_at), (blocks,), jnp.float32, smallest / len(pieces), largest / len(pieces)))
        level = level * jnp.repeat(heights, extent[axis_at] // blocks).reshape([-1 if axis == axis_at else 1 for axis in range(len(extent))])
    return level


def centred(stream_key, dims, width, limit, kind=jnp.bfloat16):
    array = width * jax.random.normal(stream_key, dims, jnp.float32)
    return jnp.clip(array, min=-limit, max=limit).astype(kind)


def setup_inputs(seed: int = 0) -> dict:
    seeds = jax.random.split(jax.random.key(seed), 12)
    spectra = jnp.clip(jnp.exp(math.log(2.0) - 3.6888794 * jax.random.uniform(seeds[0], (NESTS, K, POINTS), jnp.float32) ** level_of(seeds[0], (NESTS, K, POINTS), ((0, 2), (1, 16)), -0.2, 0.2)), 0.05, 2.0)
    courant = jnp.clip(jax.random.uniform(seeds[1], (2, K), jnp.float32, -0.9, 0.9) * level_of(seeds[1], (2, K), ((1, 16),), -0.4, 0.0), -0.9, 0.9)
    coupling = centred(seeds[2], (K, K), K ** -0.5, 0.1875)
    growth = jnp.clip(jnp.exp(jax.random.uniform(seeds[3], (K,), jnp.float32, math.log(0.05), math.log(0.5))), 0.05, 0.5)
    dissipation = jnp.clip(jnp.exp(jax.random.uniform(seeds[4], (K,), jnp.float32, math.log(0.2), math.log(2.0))), 0.2, 2.0)
    wind = jnp.clip(0.5 + 1.5 * jax.random.uniform(seeds[5], (NESTS, POINTS), jnp.float32) ** level_of(seeds[5], (NESTS, POINTS), ((0, 2),), -0.2, 0.2), 0.5, 2.0)
    neighbours = draw_neighbours(jax.random.fold_in(seeds[11], 71), 0)
    wet_mask = draw_wet_mask(jax.random.fold_in(seeds[11], 71), 0)
    send_list = draw_send_list(jax.random.fold_in(seeds[11], 71), 0)
    recv_list = draw_recv_list(jax.random.fold_in(seeds[11], 71), 0)
    substep_count = draw_substep_count(jax.random.fold_in(seeds[11], 71), 0)
    return {"spectra": spectra, "courant": courant, "coupling": coupling, "growth": growth, "dissipation": dissipation, "wind": wind, "neighbours": neighbours, "wet_mask": wet_mask, "send_list": send_list, "recv_list": recv_list, "substep_count": substep_count}


source_dt = 0.25
tiny_add = 1e-06

def advect(field, rate, fwd_index, back_index, fwd_next):
    magnitude = jnp.abs(rate)
    forward = rate >= 0.0
    next_cell = field[:, fwd_index]
    prev_cell = field[:, back_index]
    next_next = field[:, fwd_next]
    upwind = jnp.where(forward, field, next_cell)
    downwind = jnp.where(forward, next_cell, field)
    far_upwind = jnp.where(forward, prev_cell, next_next)
    estimate = 0.5 * (upwind + downwind) - 0.5 * magnitude * (downwind - upwind) - (1.0 - magnitude * magnitude) / 6.0 * (downwind - 2.0 * upwind + far_upwind)
    face_value = jnp.clip(estimate, jnp.minimum(upwind, downwind), jnp.maximum(upwind, downwind))
    return field - rate * (face_value - face_value[:, back_index])

def integrate(columns, wind_cols, coupling, growth, dissipation):
    for repeat in range(SRC):
        linear = jnp.dot(coupling, columns.astype(jnp.bfloat16), preferred_element_type=jnp.float32)
        spread = jnp.sqrt(lax.optimization_barrier(jnp.mean(columns * columns, axis=0)) + tiny_add)
        columns = (columns + source_dt * (linear + growth[:, None] * wind_cols[None, :] * columns)) / (1.0 + source_dt * dissipation[:, None] * spread[None, :])
    return columns

def wet_points(sea_int, total):
    position = (jnp.cumsum(sea_int) - 1).astype(jnp.int32)
    target = jnp.where(sea_int == 1, position, total).astype(jnp.int32)
    return jnp.zeros((total,), jnp.int32).at[target].set(jnp.arange(sea_int.shape[0], dtype=jnp.int32), mode='drop')

def reference(spectra, courant, coupling, growth, dissipation, wind, neighbours, wet_mask, send_list, recv_list, substep_count):
    nests = spectra.shape[0]
    bins = spectra.shape[1]
    points = spectra.shape[2]
    sea = wet_mask.astype(jnp.float32)
    east_index = neighbours[:, 0]
    west_index = neighbours[:, 1]
    north_index = neighbours[:, 2]
    south_index = neighbours[:, 3]
    east_next = jnp.take_along_axis(east_index, east_index, axis=1)
    north_next = jnp.take_along_axis(north_index, north_index, axis=1)
    steps_float = substep_count.astype(jnp.float32)

    def propagate(block):
        field, cour = block
        field = field * sea[:, None, :]
        for substep in range(SUBSTEPS):
            incoming = [field[(nest_id + 1) % nests][:, send_list[(nest_id + 1) % nests]] for nest_id in range(nests)]
            updated = []
            for nest_id in range(nests):
                current = field[nest_id].at[:, recv_list[nest_id]].set(incoming[nest_id])
                rates = cour / steps_float[nest_id]
                current = advect(current, rates[0][:, None], east_index[nest_id], west_index[nest_id], east_next[nest_id])
                current = advect(current, rates[1][:, None], north_index[nest_id], south_index[nest_id], north_next[nest_id])
                current = current * sea[nest_id][None, :]
                updated.append(jnp.where(substep < substep_count[nest_id], current, field[nest_id]))
            field = jnp.stack(updated)
        return field
    blocks = spectra.reshape(nests, bins // 8, 8, points).transpose(1, 0, 2, 3)
    cour_blocks = courant.reshape(2, bins // 8, 8).transpose(1, 0, 2)
    moved = lax.map(propagate, (blocks, cour_blocks))
    moved = moved.transpose(1, 0, 2, 3).reshape(nests, bins, points)
    results = []
    for nest_id in range(nests):
        wet_index = wet_points(wet_mask[nest_id], points // 2)
        columns = moved[nest_id][:, wet_index]
        columns = integrate(columns, wind[nest_id][wet_index], coupling, growth, dissipation)
        results.append(jnp.zeros((bins, points), jnp.float32).at[:, wet_index].set(columns))
    return jnp.stack(results)
```

```python
import functools

import jax
import jax.numpy as jnp
from jax import lax
from jax.experimental import pallas as pl
from jax.experimental.pallas import tpu as pltpu
from jax.sharding import PartitionSpec as P

SUBSTEPS = 2
SRC = 5
LANES = 128
SUBLANES = 8

source_dt = 0.25
tiny_add = 1e-06
f32 = jnp.float32
bf16 = jnp.bfloat16


def up_to(value, unit):
    return -(-value // unit) * unit


def grid_shape(points):
    cols_count = min(256, points // 4)
    return points // cols_count, cols_count


def dot(left, right):
    return jnp.dot(left, right, preferred_element_type=f32)


def dot_t(left, right):
    return lax.dot_general(left, right, (((1,), (1,)), ((), ())), preferred_element_type=f32)


def split(values):
    rest = values - values.astype(bf16).astype(f32)
    return jnp.concatenate([values, rest], axis=0).astype(bf16)


def joined(terms):
    half = terms.shape[0] // 2
    return terms[:half] + terms[half:]


def one_hot(rows, index):
    at = lax.broadcasted_iota(jnp.int32, (rows, index.shape[1]), 0)
    return jnp.where(at == index, 1.0, 0.0).astype(bf16)


def column(row):
    size = row.shape[1]
    at = lax.broadcasted_iota(jnp.int32, (size, size), 0)
    across = lax.broadcasted_iota(jnp.int32, (size, size), 1)
    return jnp.sum(jnp.where(at == across, row, 0.0), axis=1, keepdims=True)


def each(count, body):
    if count <= 8:
        for step in range(count):
            body(step)
    else:
        pl.loop(0, count)(body)


def span(start, size):
    if isinstance(start, int):
        return pl.ds(start * size, size)
    return pl.ds(pl.multiple_of(start * size, size), size)


def walk(tables, order):
    rows_count, cols_count, _ = order.shape
    step = one_hot(cols_count, tables[0:1, 0:cols_count])
    across = lax.broadcasted_iota(jnp.int32, (cols_count, cols_count), 1)
    at = lax.broadcasted_iota(jnp.int32, (cols_count, cols_count), 0)
    found = jnp.where(at == 0, 1.0, 0.0)
    bits = (cols_count - 1).bit_length()
    for bit in range(bits):
        moved = dot(step, found.astype(bf16))
        found = jnp.where((across >> bit) & 1 == 1, moved, found)
        if bit < bits - 1:
            step = dot(step, step).astype(bf16)
    order[0] = found.astype(bf16)

    def next_row(row):
        north = tables[2:3, span(row, cols_count)] - (row + 1) * cols_count
        order[row + 1] = dot(one_hot(cols_count, north), order[row]).astype(bf16)

    each(rows_count - 1, next_row)


def sea_matrix(wet, row, cols_count, before, count):
    here = jnp.broadcast_to(wet[0:1, span(row, cols_count)].astype(f32), (SUBLANES, cols_count))
    at = lax.broadcasted_iota(jnp.int32, (cols_count, cols_count), 0)
    across = lax.broadcasted_iota(jnp.int32, (cols_count, cols_count), 1)
    upper = jnp.where(at <= across, 1.0, 0.0).astype(bf16)
    place = dot(here.astype(bf16), upper)[0:1] + before
    place = jnp.where(here[0:1] > 0.0, place - 1.0, -1.0).astype(jnp.int32)
    return one_hot(count, place), before + jnp.sum(here[0:1], axis=1, keepdims=True)


def face_at(cell, onward, curve, weights):
    rate, lean, bend, forward = weights
    estimate = cell + lean * (onward - cell) - bend * curve
    return jnp.clip(estimate, jnp.minimum(cell, onward), jnp.maximum(cell, onward))


def advect_east(cell, weights):
    size = cell.shape[1]
    onward = pltpu.roll(cell, size - 1, 1)
    slope = onward - cell
    bent = slope - pltpu.roll(slope, 1, 1)
    curve = jnp.where(weights[3], bent, pltpu.roll(bent, size - 1, 1))
    face = face_at(cell, onward, curve, weights)
    return cell - weights[0] * (face - pltpu.roll(face, 1, 1))


def rate_weights(courant, which, steps):
    rate = column(courant[which : which + 1, :]) / steps.astype(f32)
    return rate, 0.5 - 0.5 * rate, (1.0 - rate * rate) / 6.0, rate >= 0.0


def advance(field, sea, weights_east, weights_north, scratch):
    rows_count = field.shape[0]
    moved, faces = scratch

    def east(row):
        moved[row] = advect_east(field[row], weights_east)

    each(rows_count, east)

    def face(row):
        ahead, second, behind = ((row + k + rows_count) % rows_count for k in (1, 2, -1))
        cell, onward = moved[row], moved[ahead]
        slope = onward - cell
        curve = jnp.where(
            weights_north[3],
            slope - (cell - moved[behind]),
            (moved[second] - onward) - slope,
        )
        faces[row] = face_at(cell, onward, curve, weights_north)

    each(rows_count, face)

    def north(row):
        behind = (row - 1 + rows_count) % rows_count
        field[row] = (moved[row] - weights_north[0] * (faces[row] - faces[behind])) * sea[row]

    each(rows_count, north)


def propagate_kernel(
    share,
    spectra,
    courant,
    wind,
    tables,
    wet,
    send,
    recv,
    steps,
    spectra_b,
    tables_b,
    wet_b,
    send_b,
    recv_b,
    steps_b,
    pieces,
    order,
    order_b,
    field,
    field_b,
    moved,
    faces,
    sea,
    sea_b,
    out_cols,
):
    rows_count, bins, cols_count = field.shape
    sea_count = out_cols.shape[1]
    listed = send.shape[1]
    walk(tables, order)
    walk(tables_b, order_b)

    def sent(raw, list_ref):
        total = jnp.zeros((2 * bins, listed), f32)

        def add(row, total):
            own = one_hot(cols_count, list_ref[...] - row * cols_count)
            return total + dot(split(raw[:, span(row, cols_count)]), own)

        if rows_count <= 8:
            for row in range(rows_count):
                total = add(row, total)
        else:
            total = lax.fori_loop(0, rows_count, add, total)
        return total.astype(bf16)

    def start(raw, incoming, wet_ref, recv_ref, order_ref, sea_ref, field_ref):
        def place(row):
            into = one_hot(cols_count, recv_ref[...] - row * cols_count)
            taken = dot_t(jnp.ones((SUBLANES, listed), bf16), into)[0:1] > 0.5
            here = wet_ref[0:1, span(row, cols_count)].astype(f32)
            values = jnp.where(
                taken, joined(dot_t(incoming, into)), raw[:, span(row, cols_count)] * here
            )
            field_ref[row] = joined(dot(split(values), order_ref[row]))
            wide = jnp.broadcast_to(here, (SUBLANES, cols_count)).astype(bf16)
            sea_ref[row] = dot(wide, order_ref[row])[0:1]

        each(rows_count, place)

    from_b = sent(spectra_b, send_b)
    from_a = sent(spectra, send)
    start(spectra, from_b, wet, recv, order, sea, field)
    start(spectra_b, from_a, wet_b, recv_b, order_b, sea_b, field_b)
    east_a = rate_weights(courant, 0, steps[...])
    north_a = rate_weights(courant, 1, steps[...])
    advance(field, sea, east_a, north_a, (moved, faces))
    advance(
        field_b,
        sea_b,
        rate_weights(courant, 0, steps_b[...]),
        rate_weights(courant, 1, steps_b[...]),
        (moved, faces),
    )

    def add_b(row, total):
        plain = dot_t(split(field_b[row]), order_b[row]).astype(bf16)
        return total + dot(plain, one_hot(cols_count, send_b[...] - row * cols_count))

    total = jnp.zeros((2 * bins, listed), f32)
    if rows_count <= 8:
        for row in range(rows_count):
            total = add_b(row, total)
    else:
        total = lax.fori_loop(0, rows_count, add_b, total)
    from_b = total.astype(bf16)

    def take(row):
        into = one_hot(cols_count, recv[...] - row * cols_count)
        taken = dot_t(jnp.ones((SUBLANES, listed), bf16), into).astype(bf16)
        taken = dot(taken, order[row])[0:1] > 0.5
        incoming = joined(dot(dot_t(from_b, into).astype(bf16), order[row]))
        old = field[row]
        field_b[row] = old
        field[row] = jnp.where(taken, incoming, old)

    each(rows_count, take)
    advance(field, sea, east_a, north_a, (moved, faces))
    second = steps[...] > 1

    def gather(row, carry):
        total, before = carry
        picks, before = sea_matrix(wet, row, cols_count, before, sea_count)
        last = jnp.where(second, field[row], field_b[row])
        plain = dot_t(split(last), order[row]).astype(bf16)
        blown = jnp.broadcast_to(wind[0:1, span(row, cols_count)], (SUBLANES, cols_count))
        return total + dot_t(jnp.concatenate([plain, split(blown)], axis=0), picks), before

    carry = (jnp.zeros((2 * bins + 2 * SUBLANES, sea_count), f32), jnp.zeros((1, 1), f32))
    if rows_count <= 8:
        for row in range(rows_count):
            carry = gather(row, carry)
    else:
        carry = lax.fori_loop(0, rows_count, gather, carry)
    total = carry[0]
    out_cols[0:bins] = joined(total[: 2 * bins])
    out_cols[bins : bins + SUBLANES] = joined(total[2 * bins :])

    per = LANES // share
    block = bins // (per - 1)
    lane_group = lax.broadcasted_iota(jnp.int32, (block, LANES), 1) // share

    def fold(tile):
        columns = out_cols[:, span(tile, LANES)]
        for j in range(per):
            last = jnp.broadcast_to(columns[bins : bins + 1], (block, LANES))
            piece = pltpu.roll(last, (per - 1 - j) * share, 1)
            for q in range(per - 1):
                part = columns[q * block : (q + 1) * block]
                if q != j:
                    part = pltpu.roll(part, ((q - j) % per) * share, 1)
                piece = jnp.where(lane_group == q, part, piece)
            pieces[tile * per + j] = piece

    each(sea_count // LANES, fold)


def integrate_kernel(share, pieces, coupling, growth, dissipation, out, values, push, drag):
    devices, block, _ = pieces.shape
    per = LANES // share
    size = coupling.shape[0]
    bins = size // devices
    groups = -(-bins // block)

    def rows(device, q):
        start = device * bins + q * block
        return pl.ds(start if isinstance(start, int) else pl.multiple_of(start, bins & -bins), block)

    blown = pltpu.roll(pieces[0, 0:SUBLANES], share, 1)[0:1]

    def unfold(source):
        piece = pieces[source]
        for q in range(groups):
            part = piece if q == 0 else pltpu.roll(piece, LANES - q * share, 1)
            values[rows(source, q)] = part

    each(devices, unfold)

    def rates(chunk):
        here = span(chunk, LANES)
        push[here] = 1.0 + source_dt * (column(growth[0:1, here]) * blown)
        drag[here] = jnp.broadcast_to(source_dt * column(dissipation[0:1, here]), (LANES, LANES))

    each(size // LANES, rates)
    for repeat in range(SRC):
        now = values[0:size]
        linear = dot(coupling[...], now.astype(bf16))
        spread = jnp.sqrt(jnp.mean(now * now, axis=0, keepdims=True) + tiny_add)
        values[0:size] = (now * push[...] + source_dt * linear) / (1.0 + drag[...] * spread)

    lane_group = lax.broadcasted_iota(jnp.int32, (block, LANES), 1) // share

    def fold(target):
        piece = values[rows(target, 0)]
        for q in range(1, groups):
            part = pltpu.roll(values[rows(target, q)], q * share, 1)
            piece = jnp.where(lane_group == q, part, piece)
        out[target] = piece

    each(devices, fold)


def spread_kernel(share, pieces, wet, out, columns):
    devices, block, _ = pieces.shape
    per = LANES // share
    sea_count = devices * share
    points = wet.shape[1]
    rows_count, cols_count = grid_shape(points)
    lane_group = lax.broadcasted_iota(jnp.int32, (block, LANES), 1) // share

    def unfold(tile):
        for q in range(per - 1):
            part = jnp.zeros((block, LANES), f32)
            for j in range(per):
                piece = pieces[tile * per + j]
                if j != q:
                    piece = pltpu.roll(piece, ((j - q) % per) * share, 1)
                part = jnp.where(lane_group == j, piece, part)
            columns[q * block : (q + 1) * block, span(tile, LANES)] = part

    each(sea_count // LANES, unfold)
    terms = split(columns[...])

    def scatter(row, before):
        picks, before = sea_matrix(wet, row, cols_count, before, sea_count)
        out[:, span(row, cols_count)] = joined(dot(terms, picks))
        return before

    before = jnp.zeros((1, 1), f32)
    if rows_count <= 8:
        for row in range(rows_count):
            before = scatter(row, before)
    else:
        lax.fori_loop(0, rows_count, scatter, before)


def call(kernel, out_shape, scratch, operands, flops):
    held = sum(x.size * x.dtype.itemsize for x in operands)
    return pl.pallas_call(
        kernel,
        out_shape=out_shape,
        in_specs=[pl.BlockSpec(memory_space=pltpu.VMEM)] * len(operands),
        out_specs=pl.BlockSpec(memory_space=pltpu.VMEM),
        scratch_shapes=scratch,
        compiler_params=pltpu.CompilerParams(vmem_limit_bytes=min(56 << 20, (24 << 20) + 2 * held)),
        cost_estimate=pl.CostEstimate(flops=flops, bytes_accessed=held, transcendentals=0),
    )(*operands)


def local(
    spectra,
    courant,
    coupling,
    growth,
    dissipation,
    wind,
    neighbours,
    wet_mask,
    send_list,
    recv_list,
    substep_count,
):
    devices = lax.axis_size("bin")
    field = spectra[0]
    bins_here, points = field.shape
    rows_count, cols_count = grid_shape(points)
    sea_count = points // 2
    share = sea_count // devices
    per = LANES // share
    bins = up_to(bins_here, SUBLANES * (per - 1))
    extra = bins - bins_here
    if extra:
        field = jnp.pad(field, ((0, extra), (0, 0)))
        courant = jnp.pad(courant, ((0, 0), (0, extra)))
    own = (field, neighbours[0], wet_mask, send_list, recv_list, substep_count.reshape(1, 1))
    other = [lax.ppermute(x, "nest", [(0, 1), (1, 0)]) for x in own]
    grid = (rows_count, bins, cols_count)
    operands = (own[0], courant, wind, *own[1:], *other)
    pieces = call(
        functools.partial(propagate_kernel, share),
        jax.ShapeDtypeStruct((devices, bins // (per - 1), LANES), f32),
        [
            pltpu.VMEM((rows_count, cols_count, cols_count), bf16),
            pltpu.VMEM((rows_count, cols_count, cols_count), bf16),
            pltpu.VMEM(grid, f32),
            pltpu.VMEM(grid, f32),
            pltpu.VMEM(grid, f32),
            pltpu.VMEM(grid, f32),
            pltpu.VMEM((rows_count, 1, cols_count), f32),
            pltpu.VMEM((rows_count, 1, cols_count), f32),
            pltpu.VMEM((bins + SUBLANES, sea_count), f32),
        ],
        operands,
        10**9,
    )
    pieces = lax.all_to_all(pieces, "bin", split_axis=0, concat_axis=0)
    size = devices * bins_here
    pieces = call(
        functools.partial(integrate_kernel, share),
        jax.ShapeDtypeStruct(pieces.shape, f32),
        [pltpu.VMEM((size + bins, LANES), f32), *[pltpu.VMEM((size, LANES), f32)] * 2],
        (pieces, coupling, growth.reshape(1, size), dissipation.reshape(1, size)),
        10**9,
    )
    pieces = lax.all_to_all(pieces, "bin", split_axis=0, concat_axis=0)
    result = call(
        functools.partial(spread_kernel, share),
        jax.ShapeDtypeStruct((bins, points), f32),
        [pltpu.VMEM((bins, sea_count), f32)],
        (pieces, wet_mask),
        10**8,
    )
    return result[None, :bins_here]


def solution(mesh):
    in_specs = (
        P("nest", "bin", None),
        P(None, "bin"),
        P(),
        P(),
        P(),
        P("nest", None),
        P("nest", None, None),
        P("nest", None),
        P("nest", None),
        P("nest", None),
        P("nest"),
    )
    out_specs = P("nest", "bin", None)
    return jax.shard_map(local, mesh=mesh, in_specs=in_specs, out_specs=out_specs, check_vma=False)
```

```python
import functools
import math

import jax
import jax.numpy as jnp
from jax import lax
from jax.experimental import pallas as pl
from jax.experimental.pallas import tpu as pltpu
from jax.sharding import PartitionSpec as P

SUBSTEPS = 2
SRC = 5
LANES = 128
SUBLANES = 8

source_dt = 0.25
tiny_add = 1e-06
f32 = jnp.float32
bf16 = jnp.bfloat16


def up_to(value, unit):
    return -(-value // unit) * unit


def grid_shape(points):
    cols_count = min(256, points // 4)
    return points // cols_count, cols_count


def dot(left, right):
    return jnp.dot(left, right, preferred_element_type=f32)


def dot_t(left, right):
    return lax.dot_general(left, right, (((1,), (1,)), ((), ())), preferred_element_type=f32)


def split(values):
    rest = values - values.astype(bf16).astype(f32)
    return jnp.concatenate([values, rest], axis=0).astype(bf16)


def joined(terms):
    half = terms.shape[0] // 2
    return terms[:half] + terms[half:]


def one_hot(rows, index):
    at = lax.broadcasted_iota(jnp.int32, (rows, index.shape[1]), 0)
    return jnp.where(at == index, 1.0, 0.0).astype(bf16)


def column(row):
    size = row.shape[1]
    at = lax.broadcasted_iota(jnp.int32, (size, size), 0)
    across = lax.broadcasted_iota(jnp.int32, (size, size), 1)
    return jnp.sum(jnp.where(at == across, row, 0.0), axis=1, keepdims=True)


def each(count, body):
    if count <= 16:
        for step in range(count):
            body(step)
    else:
        pl.loop(0, count)(body)


def total_of(count, shape, term):
    total = jnp.zeros(shape, f32)
    if count <= 16:
        for step in range(count):
            total = total + term(step)
        return total
    return lax.fori_loop(0, count, lambda step, total: total + term(step), total)


def span(start, size):
    if isinstance(start, int):
        return pl.ds(start * size, size)
    return pl.ds(pl.multiple_of(start * size, size), size)


def walk(tables, order):
    rows_count, cols_count, _ = order.shape
    step = one_hot(cols_count, tables[0:1, 0:cols_count])
    across = lax.broadcasted_iota(jnp.int32, (cols_count, cols_count), 1)
    at = lax.broadcasted_iota(jnp.int32, (cols_count, cols_count), 0)
    found = jnp.where(at == 0, 1.0, 0.0)
    bits = (cols_count - 1).bit_length()
    for bit in range(bits):
        moved = dot(step, found.astype(bf16))
        found = jnp.where((across >> bit) & 1 == 1, moved, found)
        if bit < bits - 1:
            step = dot(step, step).astype(bf16)
    order[0] = found.astype(bf16)

    def next_row(row):
        north = tables[2:3, span(row, cols_count)] - (row + 1) * cols_count
        order[row + 1] = dot(one_hot(cols_count, north), order[row]).astype(bf16)

    each(rows_count - 1, next_row)


def down(row):
    wide = jnp.broadcast_to(row.astype(f32), (LANES, row.shape[1]))
    return jnp.transpose(wide).astype(jnp.int32)


def one_hot_across(index, first, count):
    lane = lax.broadcasted_iota(jnp.int32, index.shape, 1)
    tiles = [
        jnp.where(lane + (first + tile * LANES) == index, 1.0, 0.0).astype(bf16)
        for tile in range(count // LANES)
    ]
    return jnp.concatenate(tiles, axis=1)


def eight(row):
    return jnp.broadcast_to(row, (SUBLANES, row.shape[1]))


def face_at(cell, onward, curve, rate):
    estimate = cell + (0.5 - 0.5 * rate) * (onward - cell) - (1.0 - rate * rate) / 6.0 * curve
    return jnp.clip(estimate, jnp.minimum(cell, onward), jnp.maximum(cell, onward))


def advance(field, moved, faces, sea, rate_east, rate_north):
    rows_count, _, cols_count = field.shape

    def east(row):
        cell = field[row]
        onward = pltpu.roll(cell, cols_count - 1, 1)
        slope = onward - cell
        bent = slope - pltpu.roll(slope, 1, 1)
        curve = jnp.where(rate_east >= 0.0, bent, pltpu.roll(bent, cols_count - 1, 1))
        face = face_at(cell, onward, curve, rate_east)
        moved[row] = cell - rate_east * (face - pltpu.roll(face, 1, 1))

    each(rows_count, east)

    def face(row):
        ahead, second, behind = ((row + k + rows_count) % rows_count for k in (1, 2, -1))
        cell, onward = moved[row], moved[ahead]
        slope = onward - cell
        curve = jnp.where(
            rate_north >= 0.0, slope - (cell - moved[behind]), (moved[second] - onward) - slope
        )
        faces[row] = face_at(cell, onward, curve, rate_north)

    each(rows_count, face)

    def north(row):
        behind = (row - 1 + rows_count) % rows_count
        field[row] = (moved[row] - rate_north * (faces[row] - faces[behind])) * sea[row]

    each(rows_count, north)


def landing(row, into, order, lists):
    if into.shape[0] == order.shape[0]:
        return into[row]
    cols_count = order.shape[2]
    here = one_hot_across(down(lists[1:2]), row * cols_count, cols_count)
    return dot(here, order[row]).astype(bf16)


def prepare_kernel(
    spectra_in,
    courant_in,
    tables_in,
    wet_in,
    send_in,
    recv_in,
    steps,
    order,
    base,
    into,
    sea,
    taken,
    rates,
    lists,
    spectra,
    courant,
    tables,
    wet,
    arrived,
):
    copies = [
        pltpu.make_async_copy(source, target, arrived.at[which])
        for which, (source, target) in enumerate(
            (
                (tables_in, tables),
                (send_in, lists.at[0:1]),
                (recv_in, lists.at[1:2]),
                (wet_in, wet),
                (courant_in, courant),
                (spectra_in, spectra),
            )
        )
    ]
    for copy in copies:
        copy.start()
    rows_count, bins, cols_count = base.shape
    listed = lists.shape[1]
    copies[0].wait()
    walk(tables, order)
    for copy in copies[1:]:
        copy.wait()
    recv_down = down(lists[1:2])
    count = steps[0, 0]
    second = jnp.where(count > 1, 1.0, 0.0)

    def place(row):
        own = order[row]
        here = one_hot_across(recv_down, row * cols_count, cols_count)
        if into.shape[0] == rows_count:
            into[row] = dot(here, own).astype(bf16)
        got = dot(jnp.ones((SUBLANES, listed), bf16), here)[0:1]
        taken[row] = dot(eight(got).astype(bf16), own)[0:1] * second
        covered = wet[0:1, span(row, cols_count)].astype(f32)
        sea[row] = dot(eight(covered).astype(bf16), own)[0:1]
        values = spectra[:, span(row, cols_count)] * (covered * (1.0 - got))
        base[row] = joined(dot(split(values), own))

    each(rows_count, place)
    for which in range(2):
        rate = column(courant[which : which + 1, :]) / count.astype(f32)
        rates[which] = jnp.broadcast_to(rate, (bins, cols_count))
        rates[2 + which] = jnp.broadcast_to(rate * second, (bins, cols_count))


def first_kernel(
    base, into, order, sea, rates, lists, spectra_b, send_b, field, outgoing, moved, faces
):
    rows_count, bins, cols_count = base.shape
    listed = lists.shape[1]

    def sent(row):
        own = one_hot(cols_count, send_b[...] - row * cols_count)
        return dot(split(spectra_b[:, span(row, cols_count)]), own)

    incoming = total_of(rows_count, (2 * bins, listed), sent).astype(bf16)

    def take(row):
        field[row] = base[row] + joined(dot(incoming, landing(row, into, order, lists)))

    each(rows_count, take)
    advance(field, moved, faces, sea, rates[0], rates[1])

    def sending(row):
        plain = dot_t(split(field[row]), order[row]).astype(bf16)
        return dot(plain, one_hot(cols_count, lists[0:1] - row * cols_count))

    outgoing[...] = joined(total_of(rows_count, (2 * bins, listed), sending))


def picked(row, ranks, picks, sea_count):
    if picks.shape[0] == ranks.shape[0]:
        return picks[row]
    return one_hot_across(down(ranks[row] - 1.0), 0, sea_count)


def places_kernel(order, sea, wind, ranks, picks, place, blown):
    rows_count, cols_count, _ = order.shape
    sea_count = blown.shape[1]
    at = lax.broadcasted_iota(jnp.int32, (cols_count, cols_count), 0)
    across = lax.broadcasted_iota(jnp.int32, (cols_count, cols_count), 1)
    upper = jnp.where(at <= across, 1.0, 0.0).astype(bf16)

    def number(row, before):
        here = sea[row]
        rank = dot(eight(here).astype(bf16), upper)[0:1] + before
        rank = jnp.where(here > 0.0, rank, 0.0)
        ranks[row] = rank
        if picks.shape[0] == rows_count:
            picks[row] = one_hot_across(down(rank - 1.0), 0, sea_count)
        high = jnp.floor(rank * (1.0 / cols_count))
        digits = jnp.concatenate([eight(high), eight(rank - high * cols_count)], axis=0)
        plain = dot_t(digits.astype(bf16), order[row])
        plain = plain[0:1] * cols_count + plain[SUBLANES : SUBLANES + 1]
        place[0:1, span(row, cols_count)] = plain.astype(jnp.int32)
        return before + jnp.sum(here, axis=1, keepdims=True)

    before = jnp.zeros((1, 1), f32)
    if rows_count <= 16:
        for row in range(rows_count):
            before = number(row, before)
    else:
        lax.fori_loop(0, rows_count, number, before)

    def there(row):
        terms = split(eight(wind[0:1, span(row, cols_count)]))
        by_grid = dot(terms, order[row]).astype(bf16)
        return dot(by_grid, picked(row, ranks, picks, sea_count))

    blown[...] = joined(total_of(rows_count, (2 * SUBLANES, sea_count), there))


def second_kernel(
    share,
    field_in,
    incoming,
    into,
    order,
    lists,
    taken,
    sea,
    rates,
    ranks,
    picks,
    blown,
    pieces,
    field,
    moved,
    faces,
    columns,
):
    rows_count, bins, cols_count = field.shape
    sea_count = blown.shape[1]
    terms = split(incoming[...])

    def take(row):
        got = joined(dot(terms, landing(row, into, order, lists)))
        field[row] = jnp.where(taken[row] > 0.5, got, field_in[row])

    each(rows_count, take)
    advance(field, moved, faces, sea, rates[2], rates[3])

    def at_sea(row):
        return dot(split(field[row]), picked(row, ranks, picks, sea_count))

    columns[...] = joined(total_of(rows_count, (2 * bins, sea_count), at_sea))
    per = LANES // share
    block = bins // (per - 1)
    lane_group = lax.broadcasted_iota(jnp.int32, (block, LANES), 1) // share

    def fold(tile):
        winds = jnp.broadcast_to(blown[0:1, span(tile, LANES)], (block, LANES))
        for j in range(per):
            piece = pltpu.roll(winds, (per - 1 - j) * share, 1)
            for q in range(per - 1):
                part = columns[q * block : (q + 1) * block, span(tile, LANES)]
                if q != j:
                    part = pltpu.roll(part, ((q - j) % per) * share, 1)
                piece = jnp.where(lane_group == q, part, piece)
            pieces[tile * per + j] = piece

    each(sea_count // LANES, fold)


def weights_kernel(devices, bins, coupling_in, weights, coupling, rows, sorted_rows, turned, arrived):
    copy = pltpu.make_async_copy(coupling_in, coupling, arrived)
    copy.start()
    copy.wait()
    size = coupling.shape[0]
    block = rows.shape[0] - size
    groups = sorted_rows.shape[0] // (devices * block)
    at = lax.broadcasted_iota(jnp.int32, (block, LANES), 0)
    rows[size:] = jnp.zeros((block, LANES), f32)

    def sort(tile):
        rows[0:size] = tile
        for q in range(groups):
            if q * block >= bins:
                none = jnp.zeros((devices * block, LANES), f32)
                sorted_rows[q * devices * block : (q + 1) * devices * block] = none
                continue

            def move(device, q=q):
                start = device * bins + q * block
                if not isinstance(start, int):
                    start = pl.multiple_of(start, bins & -bins)
                taken = rows[pl.ds(start, block)]
                if (q + 1) * block > bins:
                    taken = jnp.where(at < bins - q * block, taken, 0.0)
                sorted_rows[span(q * devices + device, block)] = taken

            each(devices, move)
        return sorted_rows[...]

    def turn(tile):
        turned[span(tile, LANES)] = jnp.transpose(sort(coupling[:, span(tile, LANES)].astype(f32)))

    def lay(tile):
        weights[:, span(tile, LANES)] = sort(turned[:, span(tile, LANES)]).astype(bf16)

    each(size // LANES, turn)
    each(weights.shape[1] // LANES, lay)


def integrate_kernel(share, total_bins, pieces, weights, rates, out):
    devices, block, _ = pieces.shape
    groups = LANES // share - 1
    width = devices * block
    turned = jnp.transpose(pieces[...].reshape(width, LANES))
    now = jnp.concatenate([turned[q * share : (q + 1) * share] for q in range(groups)], axis=1)
    wind = turned[groups * share :, 0:1]
    push = 1.0 + source_dt * (rates[0:1] * wind)
    drag = source_dt * rates[1:2]
    for repeat in range(SRC):
        linear = dot(now.astype(bf16), weights[...])
        mean = jnp.sum(now * now, axis=1, keepdims=True) * (1.0 / total_bins)
        spread = jnp.sqrt(mean + tiny_add)
        now = (now * push + source_dt * linear) / (1.0 + drag * spread)
    back = [now[:, q * width : (q + 1) * width] for q in range(groups)]
    back.append(jnp.zeros((share, width), f32))
    out[...] = jnp.transpose(jnp.concatenate(back, axis=0)).reshape(devices, block, LANES)


def spread_kernel(share, pieces, place, out, columns):
    devices, block, _ = pieces.shape
    per = LANES // share
    sea_count = devices * share
    points = place.shape[1]
    rows_count, cols_count = grid_shape(points)
    lane_group = lax.broadcasted_iota(jnp.int32, (block, LANES), 1) // share

    def unfold(tile):
        for q in range(per - 1):
            part = jnp.zeros((block, LANES), f32)
            for j in range(per):
                piece = pieces[tile * per + j]
                if j != q:
                    piece = pltpu.roll(piece, ((j - q) % per) * share, 1)
                part = jnp.where(lane_group == j, piece, part)
            columns[q * block : (q + 1) * block, span(tile, LANES)] = part

    each(sea_count // LANES, unfold)
    terms = split(columns[...])

    def scatter(row):
        picks = one_hot(sea_count, place[0:1, span(row, cols_count)] - 1)
        out[:, span(row, cols_count)] = joined(dot(terms, picks))

    each(rows_count, scatter)


def call(kernel, outs, scratch, operands, flops, apart=(), scalar=None):
    held = sum(x.size * x.dtype.itemsize for x in operands)
    single = not isinstance(outs, list)
    shapes = [jax.ShapeDtypeStruct(*out) for out in ([outs] if single else outs)]
    held += sum(x.size * x.dtype.itemsize for x in shapes)
    own = sum(4 * math.prod(getattr(x, "shape", ())) for x in scratch)
    in_vmem = pl.BlockSpec(memory_space=pltpu.VMEM)
    places = [pl.BlockSpec(memory_space=pltpu.HBM) if x in apart else in_vmem for x in range(len(operands))]
    if scalar is not None:
        places[scalar] = pl.BlockSpec(memory_space=pltpu.SMEM)
    operands = [
        x if which == scalar else pltpu.with_memory_space_constraint(x, places[which].memory_space)
        for which, x in enumerate(operands)
    ]
    return pl.pallas_call(
        kernel,
        out_shape=shapes[0] if single else shapes,
        in_specs=places,
        out_specs=in_vmem if single else [in_vmem] * len(shapes),
        scratch_shapes=scratch,
        compiler_params=pltpu.CompilerParams(vmem_limit_bytes=min(60 << 20, (4 << 20) + held + own)),
        cost_estimate=pl.CostEstimate(flops=flops, bytes_accessed=held, transcendentals=0),
    )(*operands)


def local(
    spectra,
    courant,
    coupling,
    growth,
    dissipation,
    wind,
    neighbours,
    wet_mask,
    send_list,
    recv_list,
    substep_count,
):
    devices = lax.axis_size("bin")
    field = spectra[0]
    bins_here, points = field.shape
    rows_count, cols_count = grid_shape(points)
    sea_count = points // 2
    listed = send_list.shape[1]
    share = sea_count // devices
    groups = LANES // share - 1
    bins = up_to(bins_here, SUBLANES * groups)
    block = bins // groups
    size = devices * bins_here
    extra = bins - bins_here
    rates_in = jnp.stack([growth, dissipation]).reshape(2, devices, bins_here)
    if extra:
        field = jnp.pad(field, ((0, extra), (0, 0)))
        courant = jnp.pad(courant, ((0, 0), (0, extra)))
        rates_in = jnp.pad(rates_in, ((0, 0), (0, 0), (0, extra)))
    rates_in = rates_in.reshape(2, devices, groups, block).swapaxes(1, 2).reshape(2, devices * bins)

    def swap(array):
        return lax.ppermute(array, "nest", [(0, 1), (1, 0)])

    spectra_b, send_b = swap(field), swap(send_list)
    grid = (rows_count, bins, cols_count)
    by_point = (rows_count, cols_count, cols_count)
    row_of = (rows_count, 1, cols_count)
    early = (
        field,
        courant,
        neighbours[0],
        wet_mask,
        send_list,
        recv_list,
        substep_count.reshape(1, 1),
    )
    kept_into = rows_count if points * listed <= 1 << 22 else 1
    order, base, into, sea, taken, rates, lists = call(
        prepare_kernel,
        [
            (by_point, bf16),
            (grid, f32),
            ((kept_into, listed, cols_count), bf16),
            (row_of, f32),
            (row_of, f32),
            ((4, bins, cols_count), f32),
            ((2, listed), jnp.int32),
        ],
        [
            *(pltpu.VMEM(x.shape, x.dtype) for x in early[:4]),
            pltpu.SemaphoreType.DMA((6,)),
        ],
        early,
        10**9,
        range(6),
        6,
    )
    field, outgoing = call(
        first_kernel,
        [(grid, f32), ((bins, listed), f32)],
        [pltpu.VMEM(grid, f32)] * 2,
        (base, into, order, sea, rates, lists, spectra_b, send_b),
        10**9,
    )
    incoming = swap(outgoing)
    kept = rows_count if points * sea_count <= 1 << 22 else 1
    ranks, picks, place, blown = call(
        places_kernel,
        [
            (row_of, f32),
            ((kept, cols_count, sea_count), bf16),
            ((1, points), jnp.int32),
            ((SUBLANES, sea_count), f32),
        ],
        [],
        (order, sea, wind),
        10**9,
    )
    pieces = call(
        functools.partial(second_kernel, share),
        ((devices, block, LANES), f32),
        [*[pltpu.VMEM(grid, f32)] * 3, pltpu.VMEM((bins, sea_count), f32)],
        (field, incoming, into, order, lists, taken, sea, rates, ranks, picks, blown),
        10**9,
    )
    pieces = lax.all_to_all(pieces, "bin", split_axis=0, concat_axis=0)
    weights = call(
        functools.partial(weights_kernel, devices, bins_here),
        ((devices * bins, devices * bins), bf16),
        [
            pltpu.VMEM((size, size), bf16),
            pltpu.VMEM((size + block, LANES), f32),
            pltpu.VMEM((devices * bins, LANES), f32),
            pltpu.VMEM((size, devices * bins), f32),
            pltpu.SemaphoreType.DMA,
        ],
        (coupling,),
        10**9,
        (0,),
    )
    pieces = call(
        functools.partial(integrate_kernel, share, size),
        ((devices, block, LANES), f32),
        [],
        (pieces, weights, rates_in),
        10**9,
    )
    pieces = lax.all_to_all(pieces, "bin", split_axis=0, concat_axis=0)
    result = call(
        functools.partial(spread_kernel, share),
        ((bins, points), f32),
        [pltpu.VMEM((bins, sea_count), f32)],
        (pieces, place),
        10**8,
    )
    return result[None, :bins_here]


def solution(mesh):
    in_specs = (
        P("nest", "bin", None),
        P(None, "bin"),
        P(),
        P(),
        P(),
        P("nest", None),
        P("nest", None, None),
        P("nest", None),
        P("nest", None),
        P("nest", None),
        P("nest"),
    )
    out_specs = P("nest", "bin", None)
    return jax.shard_map(local, mesh=mesh, in_specs=in_specs, out_specs=out_specs, check_vma=False)
```

```python
import functools
import math

import jax
import jax.numpy as jnp
from jax import lax
from jax.experimental import pallas as pl
from jax.experimental.pallas import tpu as pltpu
from jax.sharding import PartitionSpec as P

SUBSTEPS = 2
SRC = 5
LANES = 128
SUBLANES = 8

source_dt = 0.25
tiny_add = 1e-06
f32 = jnp.float32
bf16 = jnp.bfloat16


def up_to(value, unit):
    return -(-value // unit) * unit


def grid_shape(points):
    cols_count = min(256, points // 4)
    return points // cols_count, cols_count


def dot(left, right):
    return jnp.dot(left, right, preferred_element_type=f32)


def dot_t(left, right):
    return lax.dot_general(left, right, (((1,), (1,)), ((), ())), preferred_element_type=f32)


def split(values):
    rest = values - values.astype(bf16).astype(f32)
    return jnp.concatenate([values, rest], axis=0).astype(bf16)


def joined(terms):
    half = terms.shape[0] // 2
    return terms[:half] + terms[half:]


def one_hot(rows, index):
    at = lax.broadcasted_iota(jnp.int32, (rows, index.shape[1]), 0)
    return jnp.where(at == index, 1.0, 0.0).astype(bf16)


def column(row):
    size = row.shape[1]
    at = lax.broadcasted_iota(jnp.int32, (size, size), 0)
    across = lax.broadcasted_iota(jnp.int32, (size, size), 1)
    return jnp.sum(jnp.where(at == across, row, 0.0), axis=1, keepdims=True)


def each(count, body):
    if count <= 16:
        for step in range(count):
            body(step)
    else:
        pl.loop(0, count)(body)


def total_of(count, shape, term):
    total = jnp.zeros(shape, f32)
    if count <= 16:
        for step in range(count):
            total = total + term(step)
        return total
    return lax.fori_loop(0, count, lambda step, total: total + term(step), total)


def span(start, size):
    if isinstance(start, int):
        return pl.ds(start * size, size)
    return pl.ds(pl.multiple_of(start * size, size), size)


def rows_of(start, size):
    return pl.ds(start * size, size)


def walk(tables, order):
    rows_count, cols_count, _ = order.shape
    step = one_hot(cols_count, tables[0:1, 0:cols_count])
    across = lax.broadcasted_iota(jnp.int32, (cols_count, cols_count), 1)
    at = lax.broadcasted_iota(jnp.int32, (cols_count, cols_count), 0)
    found = jnp.where(at == 0, 1.0, 0.0)
    bits = (cols_count - 1).bit_length()
    for bit in range(bits):
        moved = dot(step, found.astype(bf16))
        found = jnp.where((across >> bit) & 1 == 1, moved, found)
        if bit < bits - 1:
            step = dot(step, step).astype(bf16)
    order[0] = found.astype(bf16)

    def next_row(row):
        north = tables[2:3, span(row, cols_count)] - (row + 1) * cols_count
        order[row + 1] = dot(one_hot(cols_count, north), order[row]).astype(bf16)

    each(rows_count - 1, next_row)


def down(row):
    wide = jnp.broadcast_to(row.astype(f32), (LANES, row.shape[1]))
    return jnp.transpose(wide).astype(jnp.int32)


def one_hot_across(index, first, count):
    lane = lax.broadcasted_iota(jnp.int32, index.shape, 1)
    tiles = [
        jnp.where(lane + (first + tile * LANES) == index, 1.0, 0.0).astype(bf16)
        for tile in range(count // LANES)
    ]
    return jnp.concatenate(tiles, axis=1)


def eight(row):
    return jnp.broadcast_to(row, (SUBLANES, row.shape[1]))


def face_at(cell, onward, curve, rate):
    estimate = cell + (0.5 - 0.5 * rate) * (onward - cell) - (1.0 - rate * rate) / 6.0 * curve
    return jnp.clip(estimate, jnp.minimum(cell, onward), jnp.maximum(cell, onward))


def advance(field, moved, faces, sea, rate_east, rate_north):
    rows_count, _, cols_count = field.shape

    def east(row):
        cell = field[row]
        onward = pltpu.roll(cell, cols_count - 1, 1)
        slope = onward - cell
        bent = slope - pltpu.roll(slope, 1, 1)
        curve = jnp.where(rate_east >= 0.0, bent, pltpu.roll(bent, cols_count - 1, 1))
        face = face_at(cell, onward, curve, rate_east)
        moved[row] = cell - rate_east * (face - pltpu.roll(face, 1, 1))

    each(rows_count, east)

    def face(row):
        ahead, second, behind = ((row + k + rows_count) % rows_count for k in (1, 2, -1))
        cell, onward = moved[row], moved[ahead]
        slope = onward - cell
        curve = jnp.where(
            rate_north >= 0.0, slope - (cell - moved[behind]), (moved[second] - onward) - slope
        )
        faces[row] = face_at(cell, onward, curve, rate_north)

    each(rows_count, face)

    def north(row):
        behind = (row - 1 + rows_count) % rows_count
        field[row] = (moved[row] - rate_north * (faces[row] - faces[behind])) * sea[row]

    each(rows_count, north)


def landing(row, into, order, lists):
    if into.shape[0] == order.shape[0]:
        return into[row]
    cols_count = order.shape[2]
    here = one_hot_across(down(lists[1:2]), row * cols_count, cols_count)
    return dot(here, order[row]).astype(bf16)


def prepare_kernel(
    spectra_in,
    tables_in,
    wet_in,
    send_in,
    recv_in,
    order,
    base,
    into,
    sea,
    taken,
    lists,
    spectra,
    tables,
    wet,
    arrived,
):
    copies = [
        pltpu.make_async_copy(source, target, arrived.at[which])
        for which, (source, target) in enumerate(
            (
                (tables_in, tables),
                (send_in, lists.at[0:1]),
                (recv_in, lists.at[1:2]),
                (wet_in, wet),
                (spectra_in, spectra),
            )
        )
    ]
    for copy in copies:
        copy.start()
    rows_count, bins, cols_count = base.shape
    listed = lists.shape[1]
    copies[0].wait()
    walk(tables, order)
    for copy in copies[1:]:
        copy.wait()
    recv_down = down(lists[1:2])

    def place(row):
        own = order[row]
        here = one_hot_across(recv_down, row * cols_count, cols_count)
        if into.shape[0] == rows_count:
            into[row] = dot(here, own).astype(bf16)
        got = dot(jnp.ones((SUBLANES, listed), bf16), here)[0:1]
        taken[row] = dot(eight(got).astype(bf16), own)[0:1]
        covered = wet[0:1, span(row, cols_count)].astype(f32)
        sea[row] = dot(eight(covered).astype(bf16), own)[0:1]
        values = spectra[:, span(row, cols_count)] * (covered * (1.0 - got))
        base[row] = joined(dot(split(values), own))

    each(rows_count, place)


def first_kernel(
    base,
    into,
    order,
    sea,
    lists,
    spectra_b,
    send_b,
    courant,
    steps,
    field,
    outgoing,
    rates,
    moved,
    faces,
):
    rows_count, bins, cols_count = base.shape
    listed = lists.shape[1]
    second = jnp.where(steps[...] > 1, 1.0, 0.0)
    for which in range(2):
        rate = column(courant[which : which + 1, :]) / steps[...].astype(f32)
        rates[which] = jnp.broadcast_to(rate, (bins, cols_count))
        rates[2 + which] = jnp.broadcast_to(rate * second, (bins, cols_count))
    rates[4] = jnp.broadcast_to(second, (bins, cols_count))

    def sent(row):
        own = one_hot(cols_count, send_b[...] - row * cols_count)
        return dot(split(spectra_b[:, span(row, cols_count)]), own)

    incoming = total_of(rows_count, (2 * bins, listed), sent).astype(bf16)

    def take(row):
        field[row] = base[row] + joined(dot(incoming, landing(row, into, order, lists)))

    each(rows_count, take)
    advance(field, moved, faces, sea, rates[0], rates[1])

    def sending(row):
        plain = dot_t(split(field[row]), order[row]).astype(bf16)
        return dot(plain, one_hot(cols_count, lists[0:1] - row * cols_count))

    outgoing[...] = joined(total_of(rows_count, (2 * bins, listed), sending))


def picked(row, ranks, picks, sea_count):
    if picks.shape[0] == ranks.shape[0]:
        return picks[row]
    return one_hot_across(down(ranks[row] - 1.0), 0, sea_count)


def places_kernel(order, sea, wind, ranks, picks, place, blown):
    rows_count, cols_count, _ = order.shape
    sea_count = blown.shape[1]
    at = lax.broadcasted_iota(jnp.int32, (cols_count, cols_count), 0)
    across = lax.broadcasted_iota(jnp.int32, (cols_count, cols_count), 1)
    upper = jnp.where(at <= across, 1.0, 0.0).astype(bf16)

    def number(row, before):
        here = sea[row]
        rank = dot(eight(here).astype(bf16), upper)[0:1] + before
        rank = jnp.where(here > 0.0, rank, 0.0)
        ranks[row] = rank
        if picks.shape[0] == rows_count:
            picks[row] = one_hot_across(down(rank - 1.0), 0, sea_count)
        high = jnp.floor(rank * (1.0 / cols_count))
        digits = jnp.concatenate([eight(high), eight(rank - high * cols_count)], axis=0)
        plain = dot_t(digits.astype(bf16), order[row])
        plain = plain[0:1] * cols_count + plain[SUBLANES : SUBLANES + 1]
        place[0:1, span(row, cols_count)] = plain.astype(jnp.int32)
        return before + jnp.sum(here, axis=1, keepdims=True)

    before = jnp.zeros((1, 1), f32)
    if rows_count <= 16:
        for row in range(rows_count):
            before = number(row, before)
    else:
        lax.fori_loop(0, rows_count, number, before)

    def there(row):
        terms = split(eight(wind[0:1, span(row, cols_count)]))
        by_grid = dot(terms, order[row]).astype(bf16)
        return dot(by_grid, picked(row, ranks, picks, sea_count))

    blown[...] = joined(total_of(rows_count, (2 * SUBLANES, sea_count), there))


def second_kernel(
    share,
    field_in,
    incoming,
    into,
    order,
    lists,
    taken,
    sea,
    rates,
    ranks,
    picks,
    pieces,
    field,
    moved,
    faces,
    columns,
):
    rows_count, bins, cols_count = field.shape
    tiles, _, _ = columns.shape
    sea_count = tiles * LANES
    terms = split(incoming[...])

    def take(row):
        got = joined(dot(terms, landing(row, into, order, lists)))
        field[row] = jnp.where(taken[row] * rates[4, 0:1] > 0.5, got, field_in[row])

    each(rows_count, take)
    advance(field, moved, faces, sea, rates[2], rates[3])

    def at_sea(row):
        return dot(split(field[row]), picked(row, ranks, picks, sea_count))

    total = joined(total_of(rows_count, (2 * bins, sea_count), at_sea))
    for tile in range(tiles):
        columns[tile] = total[:, tile * LANES : (tile + 1) * LANES]
    groups = LANES // share
    block = pieces.shape[0] // (tiles * groups)
    lane_group = lax.broadcasted_iota(jnp.int32, (block, LANES), 1) // share

    def fold(tile):
        parts = [columns[tile, pl.ds(q, block, stride=groups)] for q in range(groups)]
        for j in range(groups):
            piece = parts[j]
            for q in range(groups):
                if q != j:
                    part = pltpu.roll(parts[q], ((q - j) % groups) * share, 1)
                    piece = jnp.where(lane_group == q, part, piece)
            pieces[rows_of(tile * groups + j, block)] = piece

    each(tiles, fold)


def weights_kernel(
    devices,
    bins,
    share,
    coupling_in,
    growth,
    dissipation,
    blown,
    weights,
    rates,
    wind,
    coupling,
    rows,
    sorted_rows,
    turned,
    arrived,
):
    copy = pltpu.make_async_copy(coupling_in, coupling, arrived)
    copy.start()
    size = coupling.shape[0]
    lane_tiles = size // LANES
    groups = LANES // share
    block = sorted_rows.shape[0] // (devices * groups)
    mine = pltpu.roll(blown[...], blown.shape[1] - lax.axis_index("bin") * share, 1)
    wind[...] = jnp.broadcast_to(column(mine[0:1, 0:share]), wind.shape)
    rows[size:] = jnp.zeros((rows.shape[0] - size, LANES), f32)

    def sort():
        if groups * block == bins:
            every = devices * block
            taken = [rows[pl.ds(q, every, stride=groups)] for q in range(groups)]
            return jnp.concatenate(taken, axis=0)
        at = groups * lax.broadcasted_iota(jnp.int32, (block, LANES), 0)
        for q in range(groups):

            def move(device, q=q):
                taken = rows[pl.ds(device * bins + q, block, stride=groups)]
                taken = jnp.where(at + q < bins, taken, 0.0)
                sorted_rows[rows_of(q * devices + device, block)] = taken

            each(devices, move)
        return sorted_rows[...]

    at = lax.broadcasted_iota(jnp.int32, (LANES, LANES), 0)

    def lift(tile):
        here = span(tile, LANES)
        both = jnp.where(at == 0, growth[0:1, here], jnp.where(at == 1, dissipation[0:1, here], 0.0))
        rows[here] = jnp.transpose(both)

    each(lane_tiles, lift)
    rates[...] = jnp.transpose(sort())[0:SUBLANES]
    copy.wait()

    def turn(tile):
        rows[0:size] = coupling[:, span(tile, LANES)].astype(f32)
        turned[span(tile, LANES)] = jnp.transpose(sort())

    def lay(tile):
        rows[0:size] = turned[:, span(tile, LANES)]
        weights[:, span(tile, LANES)] = sort().astype(bf16)

    each(lane_tiles, turn)
    each(weights.shape[1] // LANES, lay)


def padded_transpose(array):
    rows_count, cols_count = array.shape
    full = up_to(rows_count, LANES)
    if full > rows_count:
        array = jnp.concatenate([array, jnp.zeros((full - rows_count, cols_count), f32)], axis=0)
    return jnp.transpose(array)


def integrate_kernel(share, total_bins, pieces, weights, rates, wind, out):
    width = pieces.shape[0]
    groups = LANES // share
    turned = padded_transpose(pieces[...])
    now = [turned[q * share : (q + 1) * share, 0:width] for q in range(groups)]
    now = jnp.concatenate(now, axis=1)
    push = 1.0 + source_dt * (rates[0:1] * wind[:, 0:1])
    drag = source_dt * rates[1:2]
    for repeat in range(SRC):
        linear = dot(now.astype(bf16), weights[...])
        mean = jnp.sum(now * now, axis=1, keepdims=True) * (1.0 / total_bins)
        spread = jnp.sqrt(mean + tiny_add)
        now = (now * push + source_dt * linear) / (1.0 + drag * spread)
    back = [now[:, q * width : (q + 1) * width] for q in range(groups)]
    back = jnp.concatenate(back, axis=0)
    full = up_to(width, LANES)
    if full > width:
        back = jnp.concatenate([back, jnp.zeros((LANES, full - width), f32)], axis=1)
    out[...] = jnp.transpose(back)[0:width]


def spread_kernel(share, pieces, place, out, columns):
    tiles, bins, _ = columns.shape
    groups = LANES // share
    block = pieces.shape[0] // (tiles * groups)
    sea_count = tiles * LANES
    points = place.shape[1]
    rows_count, cols_count = grid_shape(points)
    lane_group = lax.broadcasted_iota(jnp.int32, (block, LANES), 1) // share
    if groups * block < bins:
        columns[:, groups * block :] = jnp.zeros((tiles, bins - groups * block, LANES), f32)

    def unfold(tile):
        parts = [pieces[rows_of(tile * groups + j, block)] for j in range(groups)]
        for q in range(groups):
            part = parts[q]
            for j in range(groups):
                if j != q:
                    other = pltpu.roll(parts[j], ((j - q) % groups) * share, 1)
                    part = jnp.where(lane_group == j, other, part)
            columns[tile, pl.ds(q, block, stride=groups)] = part

    each(tiles, unfold)
    terms = jnp.concatenate([split(columns[tile]) for tile in range(tiles)], axis=1)

    def scatter(row):
        picks = one_hot(sea_count, place[0:1, span(row, cols_count)] - 1)
        out[:, span(row, cols_count)] = joined(dot(terms, picks))

    each(rows_count, scatter)


def call(kernel, outs, scratch, operands, flops, apart=()):
    held = sum(x.size * x.dtype.itemsize for x in operands)
    single = not isinstance(outs, list)
    shapes = [jax.ShapeDtypeStruct(*out) for out in ([outs] if single else outs)]
    held += sum(x.size * x.dtype.itemsize for x in shapes)
    own = sum(4 * math.prod(getattr(x, "shape", ())) for x in scratch)
    in_vmem = pl.BlockSpec(memory_space=pltpu.VMEM)
    places = [pl.BlockSpec(memory_space=pltpu.HBM) if x in apart else in_vmem for x in range(len(operands))]
    operands = [
        x if x.size == 1 else pltpu.with_memory_space_constraint(x, place.memory_space)
        for x, place in zip(operands, places)
    ]
    return pl.pallas_call(
        kernel,
        out_shape=shapes[0] if single else shapes,
        in_specs=places,
        out_specs=in_vmem if single else [in_vmem] * len(shapes),
        scratch_shapes=scratch,
        compiler_params=pltpu.CompilerParams(vmem_limit_bytes=min(60 << 20, (4 << 20) + held + own)),
        cost_estimate=pl.CostEstimate(flops=flops, bytes_accessed=held, transcendentals=0),
    )(*operands)


def local(
    spectra,
    courant,
    coupling,
    growth,
    dissipation,
    wind,
    neighbours,
    wet_mask,
    send_list,
    recv_list,
    substep_count,
):
    devices = lax.axis_size("bin")
    field = spectra[0]
    bins_here, points = field.shape
    rows_count, cols_count = grid_shape(points)
    sea_count = points // 2
    listed = send_list.shape[1]
    share = sea_count // devices
    groups = LANES // share
    block = -(-bins_here // groups)
    bins = up_to(groups * block, SUBLANES)
    size = devices * bins_here
    sorted_size = devices * groups * block
    extra = bins - bins_here
    if extra:
        field = jnp.pad(field, ((0, extra), (0, 0)))
        courant = jnp.pad(courant, ((0, 0), (0, extra)))
    def transpose_all(pieces):
        pieces = pieces.reshape(devices, 1, block * LANES)
        pieces = lax.all_to_all(pieces, "bin", split_axis=0, concat_axis=0)
        return pieces.reshape(devices * block, LANES)

    def swap(array):
        return lax.ppermute(array, "nest", [(0, 1), (1, 0)])

    spectra_b, send_b = swap(field), swap(send_list)
    grid = (rows_count, bins, cols_count)
    by_point = (rows_count, cols_count, cols_count)
    row_of = (rows_count, 1, cols_count)
    early = (
        field,
        neighbours[0],
        wet_mask,
        send_list,
        recv_list,
    )
    kept_into = rows_count if points * listed <= 1 << 22 else 1
    order, base, into, sea, taken, lists = call(
        prepare_kernel,
        [
            (by_point, bf16),
            (grid, f32),
            ((kept_into, listed, cols_count), bf16),
            (row_of, f32),
            (row_of, f32),
            ((2, listed), jnp.int32),
        ],
        [
            *(pltpu.VMEM(x.shape, x.dtype) for x in early[:3]),
            pltpu.SemaphoreType.DMA((5,)),
        ],
        early,
        10**9,
        range(5),
    )
    field, outgoing, rates = call(
        first_kernel,
        [(grid, f32), ((bins, listed), f32), ((5, bins, cols_count), f32)],
        [pltpu.VMEM(grid, f32)] * 2,
        (base, into, order, sea, lists, spectra_b, send_b, courant, substep_count.reshape(1, 1)),
        10**9,
    )
    incoming = swap(outgoing)
    kept = rows_count if points * sea_count <= 1 << 22 else 1
    ranks, picks, place, blown = call(
        places_kernel,
        [
            (row_of, f32),
            ((kept, cols_count, sea_count), bf16),
            ((1, points), jnp.int32),
            ((SUBLANES, sea_count), f32),
        ],
        [],
        (order, sea, wind),
        10**9,
    )
    tiles = sea_count // LANES
    pieces = call(
        functools.partial(second_kernel, share),
        ((devices * block, LANES), f32),
        [*[pltpu.VMEM(grid, f32)] * 3, pltpu.VMEM((tiles, bins, LANES), f32)],
        (field, incoming, into, order, lists, taken, sea, rates, ranks, picks),
        10**9,
    )
    pieces = transpose_all(pieces)
    weights, sorted_rates, wind_here = call(
        functools.partial(weights_kernel, devices, bins_here, share),
        [((sorted_size, sorted_size), bf16), ((SUBLANES, sorted_size), f32), ((share, LANES), f32)],
        [
            pltpu.VMEM((size, size), bf16),
            pltpu.VMEM((size + up_to(groups * block, SUBLANES), LANES), f32),
            pltpu.VMEM((sorted_size, LANES), f32),
            pltpu.VMEM((size, sorted_size), f32),
            pltpu.SemaphoreType.DMA,
        ],
        (coupling, growth.reshape(1, size), dissipation.reshape(1, size), blown),
        10**9,
        (0,),
    )
    pieces = call(
        functools.partial(integrate_kernel, share, size),
        ((devices * block, LANES), f32),
        [],
        (pieces, weights, sorted_rates, wind_here),
        10**9,
    )
    pieces = transpose_all(pieces)
    result = call(
        functools.partial(spread_kernel, share),
        ((bins, points), f32),
        [pltpu.VMEM((tiles, bins, LANES), f32)],
        (pieces, place),
        10**8,
    )
    return result[None, :bins_here]


def solution(mesh):
    in_specs = (
        P("nest", "bin", None),
        P(None, "bin"),
        P(),
        P(),
        P(),
        P("nest", None),
        P("nest", None, None),
        P("nest", None),
        P("nest", None),
        P("nest", None),
        P("nest"),
    )
    out_specs = P("nest", "bin", None)
    return jax.shard_map(local, mesh=mesh, in_specs=in_specs, out_specs=out_specs, check_vma=False)
```

```python
import functools
import math

import jax
import jax.numpy as jnp
from jax import lax
from jax.experimental import pallas as pl
from jax.experimental.pallas import tpu as pltpu
from jax.sharding import PartitionSpec as P

SUBSTEPS = 2
SRC = 5
LANES = 128
SUBLANES = 8

source_dt = 0.25
tiny_add = 1e-06
f32 = jnp.float32
bf16 = jnp.bfloat16


def up_to(value, unit):
    return -(-value // unit) * unit


def grid_shape(points):
    cols_count = min(256, points // 4)
    return points // cols_count, cols_count


def dot(left, right):
    return jnp.dot(left, right, preferred_element_type=f32)


def dot_t(left, right):
    return lax.dot_general(left, right, (((1,), (1,)), ((), ())), preferred_element_type=f32)


def split(values):
    rest = values - values.astype(bf16).astype(f32)
    return jnp.concatenate([values, rest], axis=0).astype(bf16)


def joined(terms):
    half = terms.shape[0] // 2
    return terms[:half] + terms[half:]


def one_hot(rows, index):
    at = lax.broadcasted_iota(jnp.int32, (rows, index.shape[1]), 0)
    return jnp.where(at == index, 1.0, 0.0).astype(bf16)


def column(row):
    size = row.shape[1]
    at = lax.broadcasted_iota(jnp.int32, (size, size), 0)
    across = lax.broadcasted_iota(jnp.int32, (size, size), 1)
    return jnp.sum(jnp.where(at == across, row, 0.0), axis=1, keepdims=True)


def each(count, body):
    if count <= 16:
        for step in range(count):
            body(step)
    else:
        pl.loop(0, count)(body)


def total_of(count, shape, term):
    total = jnp.zeros(shape, f32)
    if count <= 16:
        for step in range(count):
            total = total + term(step)
        return total
    return lax.fori_loop(0, count, lambda step, total: total + term(step), total)


def span(start, size):
    if isinstance(start, int):
        return pl.ds(start * size, size)
    return pl.ds(pl.multiple_of(start * size, size), size)


def rows_of(start, size):
    return pl.ds(start * size, size)


def rows_stacked(tiles):
    at = lax.broadcasted_iota(jnp.int32, (SUBLANES, LANES), 0)
    stacked = eight(tiles[0])
    for k in range(1, len(tiles)):
        stacked = jnp.where(at == k, eight(tiles[k]), stacked)
    return stacked


def tiles_of(row):
    return [row[:, k * LANES : (k + 1) * LANES] for k in range(row.shape[1] // LANES)]


def taken_from(tables, index):
    lane, tile = index & (LANES - 1), index >> (LANES - 1).bit_length()
    found = None
    for k, table in enumerate(tables):
        here = jnp.take_along_axis(eight(table), lane, axis=1, mode="promise_in_bounds")
        found = here if k == 0 else jnp.where(tile == k, here, found)
    return found


def look_up(table, index):
    count = index.shape[1] // LANES
    found = taken_from(tiles_of(table), rows_stacked(tiles_of(index)))
    return jnp.concatenate([found[k : k + 1] for k in range(count)], axis=1)


def walk(tables, order, rank):
    rows_count, _, cols_count = order.shape
    count = cols_count // LANES
    bits = (cols_count - 1).bit_length()
    at = lax.broadcasted_iota(jnp.int32, (SUBLANES, LANES), 0)
    place = (at % count) * LANES + lax.broadcasted_iota(jnp.int32, (SUBLANES, LANES), 1)

    first = tables[0:1, 0:cols_count]
    ahead = jnp.where(at < count, rows_stacked(tiles_of(first)), 0)
    behind = rows_stacked(tiles_of(tables[1:2, 0:cols_count]))
    behind = jnp.where(place == 0, 0, behind)
    steps = jnp.where(place == 0, 0, 1)
    for bit in range(bits):
        far = taken_from([ahead[k : k + 1] for k in range(count)], ahead)
        both = (steps << bits) + behind
        back = taken_from([both[k : k + 1] for k in range(count)], behind)
        ahead = jnp.where((at >= count) & ((place >> bit) & 1 == 0), ahead, far)
        steps = steps + (back >> bits)
        behind = back & ((1 << bits) - 1)
    order[0] = jnp.concatenate([ahead[count + k : count + k + 1] for k in range(count)], axis=1)
    rank[0] = jnp.concatenate([steps[k : k + 1] for k in range(count)], axis=1)

    def next_row(row):
        north = tables[2:3, span(row, cols_count)] - (row + 1) * cols_count
        south = tables[3:4, span(row + 1, cols_count)] - row * cols_count
        order[row + 1] = look_up(north, order[row])
        rank[row + 1] = look_up(rank[row], south)

    each(rows_count - 1, next_row)


def grid_places(listed, rank):
    rows_count, _, cols_count = rank.shape
    tiles = tiles_of(listed)
    found = []
    for tile in tiles:
        index = eight(tile)

        def column_in(row, best):
            first = row * cols_count
            within = jnp.clip(index - first, 0, cols_count - 1)
            here = taken_from(tiles_of(rank[row]), within)
            return jnp.where(index - first == within, here + first, best)

        best = jnp.zeros((SUBLANES, LANES), jnp.int32)
        if rows_count <= 16:
            for row in range(rows_count):
                best = column_in(row, best)
        else:
            best = lax.fori_loop(0, rows_count, column_in, best)
        found.append(best[0:1])
    return jnp.concatenate(found, axis=1)


def down(row):
    wide = jnp.broadcast_to(row.astype(f32), (LANES, row.shape[1]))
    return jnp.transpose(wide).astype(jnp.int32)


def one_hot_across(index, first, count):
    lane = lax.broadcasted_iota(jnp.int32, index.shape, 1)
    tiles = [
        jnp.where(lane + (first + tile * LANES) == index, 1.0, 0.0).astype(bf16)
        for tile in range(count // LANES)
    ]
    return jnp.concatenate(tiles, axis=1)


def eight(row):
    return jnp.broadcast_to(row, (SUBLANES, row.shape[1]))


def face_at(cell, onward, curve, rate):
    estimate = cell + (0.5 - 0.5 * rate) * (onward - cell) - (1.0 - rate * rate) / 6.0 * curve
    return jnp.clip(estimate, jnp.minimum(cell, onward), jnp.maximum(cell, onward))


def advance(field, moved, faces, sea, rate_east, rate_north):
    rows_count, _, cols_count = field.shape

    def east(row):
        cell = field[row]
        onward = pltpu.roll(cell, cols_count - 1, 1)
        slope = onward - cell
        bent = slope - pltpu.roll(slope, 1, 1)
        curve = jnp.where(rate_east >= 0.0, bent, pltpu.roll(bent, cols_count - 1, 1))
        face = face_at(cell, onward, curve, rate_east)
        moved[row] = cell - rate_east * (face - pltpu.roll(face, 1, 1))

    each(rows_count, east)

    def face(row):
        ahead, second, behind = ((row + k + rows_count) % rows_count for k in (1, 2, -1))
        cell, onward = moved[row], moved[ahead]
        slope = onward - cell
        curve = jnp.where(
            rate_north >= 0.0, slope - (cell - moved[behind]), (moved[second] - onward) - slope
        )
        faces[row] = face_at(cell, onward, curve, rate_north)

    each(rows_count, face)

    def north(row):
        behind = (row - 1 + rows_count) % rows_count
        field[row] = (moved[row] - rate_north * (faces[row] - faces[behind])) * sea[row]

    each(rows_count, north)


def landing(row, into, lists, cols_count):
    if into.shape[0] > 1:
        return into[row]
    return one_hot_across(down(lists[1:2]), row * cols_count, cols_count)


def prepare_kernel(
    spectra_in,
    tables_in,
    wet_in,
    send_in,
    recv_in,
    order,
    rank,
    base,
    into,
    sea,
    taken,
    lists,
    spectra,
    tables,
    wet,
    send,
    recv,
    arrived,
):
    copies = [
        pltpu.make_async_copy(source, target, arrived.at[which])
        for which, (source, target) in enumerate(
            (
                (tables_in, tables),
                (send_in, send),
                (recv_in, recv),
                (wet_in, wet),
                (spectra_in, spectra),
            )
        )
    ]
    for copy in copies:
        copy.start()
    rows_count, bins, cols_count = base.shape
    listed = send.shape[1]
    for copy in copies[:-1]:
        copy.wait()
    walk(tables, order, rank)
    lists[0:1] = grid_places(send[...], rank)
    lists[1:2] = grid_places(recv[...], rank)
    recv_down = down(lists[1:2])
    copies[-1].wait()

    def place(row):
        own = one_hot(cols_count, order[row])
        here = one_hot_across(recv_down, row * cols_count, cols_count)
        if into.shape[0] > 1:
            into[row] = here
        got = dot(jnp.ones((SUBLANES, listed), bf16), here)[0:1]
        taken[row] = got
        covered = look_up(wet[0:1, span(row, cols_count)], order[row]).astype(f32)
        sea[row] = covered
        values = joined(dot(split(spectra[:, span(row, cols_count)]), own))
        base[row] = values * (covered * (1.0 - got))

    each(rows_count, place)


def first_kernel(
    base,
    into,
    sea,
    lists,
    spectra_b,
    send_b,
    courant,
    steps,
    field,
    outgoing,
    rates,
    moved,
    faces,
):
    rows_count, bins, cols_count = base.shape
    listed = lists.shape[1]
    second = jnp.where(steps[...] > 1, 1.0, 0.0)
    for which in range(2):
        rate = column(courant[which : which + 1, :]) / steps[...].astype(f32)
        rates[which] = jnp.broadcast_to(rate, (bins, cols_count))
        rates[2 + which] = jnp.broadcast_to(rate * second, (bins, cols_count))
    rates[4] = jnp.broadcast_to(second, (bins, cols_count))

    def sent(row):
        own = one_hot(cols_count, send_b[...] - row * cols_count)
        return dot(split(spectra_b[:, span(row, cols_count)]), own)

    incoming = total_of(rows_count, (2 * bins, listed), sent).astype(bf16)

    def take(row):
        field[row] = base[row] + joined(dot(incoming, landing(row, into, lists, cols_count)))

    each(rows_count, take)
    advance(field, moved, faces, sea, rates[0], rates[1])

    def sending(row):
        return dot(split(field[row]), one_hot(cols_count, lists[0:1] - row * cols_count))

    outgoing[...] = joined(total_of(rows_count, (2 * bins, listed), sending))


def picked(row, ranks, picks, sea_count):
    if picks.shape[0] == ranks.shape[0]:
        return picks[row]
    return one_hot_across(down(ranks[row] - 1.0), 0, sea_count)


def places_kernel(order, rank, sea, wind, ranks, picks, place, blown):
    rows_count, _, cols_count = order.shape
    sea_count = blown.shape[1]
    at = lax.broadcasted_iota(jnp.int32, (cols_count, cols_count), 0)
    across = lax.broadcasted_iota(jnp.int32, (cols_count, cols_count), 1)
    upper = jnp.where(at <= across, 1.0, 0.0).astype(bf16)

    def number(row, before):
        here = sea[row]
        number_of = dot(eight(here).astype(bf16), upper)[0:1] + before
        number_of = jnp.where(here > 0.0, number_of, 0.0)
        ranks[row] = number_of
        if picks.shape[0] == rows_count:
            picks[row] = one_hot_across(down(number_of - 1.0), 0, sea_count)
        place[0:1, span(row, cols_count)] = look_up(number_of.astype(jnp.int32), rank[row])
        return before + jnp.sum(here, axis=1, keepdims=True)

    before = jnp.zeros((1, 1), f32)
    if rows_count <= 16:
        for row in range(rows_count):
            before = number(row, before)
    else:
        lax.fori_loop(0, rows_count, number, before)

    def there(row):
        by_grid = look_up(wind[0:1, span(row, cols_count)], order[row])
        return dot(split(eight(by_grid)), picked(row, ranks, picks, sea_count))

    blown[...] = joined(total_of(rows_count, (2 * SUBLANES, sea_count), there))


def second_kernel(
    share,
    field_in,
    incoming,
    into,
    lists,
    taken,
    sea,
    rates,
    ranks,
    picks,
    pieces,
    field,
    moved,
    faces,
    columns,
):
    rows_count, bins, cols_count = field.shape
    tiles, _, _ = columns.shape
    sea_count = tiles * LANES
    terms = split(incoming[...])

    def take(row):
        got = joined(dot(terms, landing(row, into, lists, cols_count)))
        field[row] = jnp.where(taken[row] * rates[4, 0:1] > 0.5, got, field_in[row])

    each(rows_count, take)
    advance(field, moved, faces, sea, rates[2], rates[3])

    def at_sea(row):
        return dot(split(field[row]), picked(row, ranks, picks, sea_count))

    total = joined(total_of(rows_count, (2 * bins, sea_count), at_sea))
    for tile in range(tiles):
        columns[tile] = total[:, tile * LANES : (tile + 1) * LANES]
    groups = LANES // share
    block = pieces.shape[0] // (tiles * groups)
    lane_group = lax.broadcasted_iota(jnp.int32, (block, LANES), 1) // share

    def fold(tile):
        parts = [columns[tile, pl.ds(q, block, stride=groups)] for q in range(groups)]
        for j in range(groups):
            piece = parts[j]
            for q in range(groups):
                if q != j:
                    part = pltpu.roll(parts[q], ((q - j) % groups) * share, 1)
                    piece = jnp.where(lane_group == q, part, piece)
            pieces[rows_of(tile * groups + j, block)] = piece

    each(tiles, fold)


def weights_kernel(
    devices,
    bins,
    share,
    coupling_in,
    growth,
    dissipation,
    blown,
    weights,
    rates,
    wind,
    coupling,
    rows,
    sorted_rows,
    turned,
    arrived,
):
    copy = pltpu.make_async_copy(coupling_in, coupling, arrived)
    copy.start()
    size = coupling.shape[0]
    lane_tiles = size // LANES
    groups = LANES // share
    block = sorted_rows.shape[0] // (devices * groups)
    mine = pltpu.roll(blown[...], blown.shape[1] - lax.axis_index("bin") * share, 1)
    wind[...] = jnp.broadcast_to(column(mine[0:1, 0:share]), wind.shape)
    rows[size:] = jnp.zeros((rows.shape[0] - size, LANES), f32)

    def sort():
        if groups * block == bins:
            every = devices * block
            taken = [rows[pl.ds(q, every, stride=groups)] for q in range(groups)]
            return jnp.concatenate(taken, axis=0)
        at = groups * lax.broadcasted_iota(jnp.int32, (block, LANES), 0)
        for q in range(groups):

            def move(device, q=q):
                taken = rows[pl.ds(device * bins + q, block, stride=groups)]
                taken = jnp.where(at + q < bins, taken, 0.0)
                sorted_rows[rows_of(q * devices + device, block)] = taken

            each(devices, move)
        return sorted_rows[...]

    at = lax.broadcasted_iota(jnp.int32, (LANES, LANES), 0)

    def lift(tile):
        here = span(tile, LANES)
        both = jnp.where(at == 0, growth[0:1, here], jnp.where(at == 1, dissipation[0:1, here], 0.0))
        rows[here] = jnp.transpose(both)

    each(lane_tiles, lift)
    rates[...] = jnp.transpose(sort())[0:SUBLANES]
    copy.wait()

    def turn(tile):
        rows[0:size] = coupling[:, span(tile, LANES)].astype(f32)
        turned[span(tile, LANES)] = jnp.transpose(sort())

    def lay(tile):
        rows[0:size] = turned[:, span(tile, LANES)]
        weights[:, span(tile, LANES)] = sort().astype(bf16)

    each(lane_tiles, turn)
    each(weights.shape[1] // LANES, lay)


def padded_transpose(array):
    rows_count, cols_count = array.shape
    full = up_to(rows_count, LANES)
    if full > rows_count:
        array = jnp.concatenate([array, jnp.zeros((full - rows_count, cols_count), f32)], axis=0)
    return jnp.transpose(array)


def integrate_kernel(share, total_bins, pieces, weights, rates, wind, out):
    width = pieces.shape[0]
    groups = LANES // share
    turned = padded_transpose(pieces[...])
    now = [turned[q * share : (q + 1) * share, 0:width] for q in range(groups)]
    now = jnp.concatenate(now, axis=1)
    push = 1.0 + source_dt * (rates[0:1] * wind[:, 0:1])
    drag = source_dt * rates[1:2]
    for repeat in range(SRC):
        linear = dot(now.astype(bf16), weights[...])
        mean = jnp.sum(now * now, axis=1, keepdims=True) * (1.0 / total_bins)
        spread = jnp.sqrt(mean + tiny_add)
        now = (now * push + source_dt * linear) / (1.0 + drag * spread)
    back = [now[:, q * width : (q + 1) * width] for q in range(groups)]
    back = jnp.concatenate(back, axis=0)
    full = up_to(width, LANES)
    if full > width:
        back = jnp.concatenate([back, jnp.zeros((LANES, full - width), f32)], axis=1)
    out[...] = jnp.transpose(back)[0:width]


def spread_kernel(share, pieces, place, out, columns):
    tiles, bins, _ = columns.shape
    groups = LANES // share
    block = pieces.shape[0] // (tiles * groups)
    sea_count = tiles * LANES
    points = place.shape[1]
    rows_count, cols_count = grid_shape(points)
    lane_group = lax.broadcasted_iota(jnp.int32, (block, LANES), 1) // share
    if groups * block < bins:
        columns[:, groups * block :] = jnp.zeros((tiles, bins - groups * block, LANES), f32)

    def unfold(tile):
        parts = [pieces[rows_of(tile * groups + j, block)] for j in range(groups)]
        for q in range(groups):
            part = parts[q]
            for j in range(groups):
                if j != q:
                    other = pltpu.roll(parts[j], ((j - q) % groups) * share, 1)
                    part = jnp.where(lane_group == j, other, part)
            columns[tile, pl.ds(q, block, stride=groups)] = part

    each(tiles, unfold)
    terms = jnp.concatenate([split(columns[tile]) for tile in range(tiles)], axis=1)

    def scatter(row):
        picks = one_hot(sea_count, place[0:1, span(row, cols_count)] - 1)
        out[:, span(row, cols_count)] = joined(dot(terms, picks))

    each(rows_count, scatter)


def call(kernel, outs, scratch, operands, flops, apart=()):
    held = sum(x.size * x.dtype.itemsize for x in operands)
    single = not isinstance(outs, list)
    shapes = [jax.ShapeDtypeStruct(*out) for out in ([outs] if single else outs)]
    held += sum(x.size * x.dtype.itemsize for x in shapes)
    own = sum(4 * math.prod(getattr(x, "shape", ())) for x in scratch)
    in_vmem = pl.BlockSpec(memory_space=pltpu.VMEM)
    places = [pl.BlockSpec(memory_space=pltpu.HBM) if x in apart else in_vmem for x in range(len(operands))]
    operands = [
        x if x.size == 1 else pltpu.with_memory_space_constraint(x, place.memory_space)
        for x, place in zip(operands, places)
    ]
    return pl.pallas_call(
        kernel,
        out_shape=shapes[0] if single else shapes,
        in_specs=places,
        out_specs=in_vmem if single else [in_vmem] * len(shapes),
        scratch_shapes=scratch,
        compiler_params=pltpu.CompilerParams(vmem_limit_bytes=min(60 << 20, (4 << 20) + held + own)),
        cost_estimate=pl.CostEstimate(flops=flops, bytes_accessed=held, transcendentals=0),
    )(*operands)


def local(
    spectra,
    courant,
    coupling,
    growth,
    dissipation,
    wind,
    neighbours,
    wet_mask,
    send_list,
    recv_list,
    substep_count,
):
    devices = lax.axis_size("bin")
    field = spectra[0]
    bins_here, points = field.shape
    rows_count, cols_count = grid_shape(points)
    sea_count = points // 2
    listed = send_list.shape[1]
    share = sea_count // devices
    groups = LANES // share
    block = -(-bins_here // groups)
    bins = up_to(groups * block, SUBLANES)
    size = devices * bins_here
    sorted_size = devices * groups * block
    extra = bins - bins_here
    if extra:
        field = jnp.pad(field, ((0, extra), (0, 0)))
        courant = jnp.pad(courant, ((0, 0), (0, extra)))
    def transpose_all(pieces):
        pieces = pieces.reshape(devices, 1, block * LANES)
        pieces = lax.all_to_all(pieces, "bin", split_axis=0, concat_axis=0)
        return pieces.reshape(devices * block, LANES)

    def swap(array):
        return lax.ppermute(array, "nest", [(0, 1), (1, 0)])

    spectra_b, send_b = swap(field), swap(send_list)
    grid = (rows_count, bins, cols_count)
    row_of = (rows_count, 1, cols_count)
    early = (
        field,
        neighbours[0],
        wet_mask,
        send_list,
        recv_list,
    )
    kept_into = rows_count if points * listed <= 1 << 22 else 1
    order, rank, base, into, sea, taken, lists = call(
        prepare_kernel,
        [
            (row_of, jnp.int32),
            (row_of, jnp.int32),
            (grid, f32),
            ((kept_into, listed, cols_count), bf16),
            (row_of, f32),
            (row_of, f32),
            ((2, listed), jnp.int32),
        ],
        [
            *(pltpu.VMEM(x.shape, x.dtype) for x in early),
            pltpu.SemaphoreType.DMA((5,)),
        ],
        early,
        10**9,
        range(5),
    )
    field, outgoing, rates = call(
        first_kernel,
        [(grid, f32), ((bins, listed), f32), ((5, bins, cols_count), f32)],
        [pltpu.VMEM(grid, f32)] * 2,
        (base, into, sea, lists, spectra_b, send_b, courant, substep_count.reshape(1, 1)),
        10**9,
    )
    incoming = swap(outgoing)
    kept = rows_count if points * sea_count <= 1 << 22 else 1
    ranks, picks, place, blown = call(
        places_kernel,
        [
            (row_of, f32),
            ((kept, cols_count, sea_count), bf16),
            ((1, points), jnp.int32),
            ((SUBLANES, sea_count), f32),
        ],
        [],
        (order, rank, sea, wind),
        10**9,
    )
    tiles = sea_count // LANES
    pieces = call(
        functools.partial(second_kernel, share),
        ((devices * block, LANES), f32),
        [*[pltpu.VMEM(grid, f32)] * 3, pltpu.VMEM((tiles, bins, LANES), f32)],
        (field, incoming, into, lists, taken, sea, rates, ranks, picks),
        10**9,
    )
    pieces = transpose_all(pieces)
    weights, sorted_rates, wind_here = call(
        functools.partial(weights_kernel, devices, bins_here, share),
        [((sorted_size, sorted_size), bf16), ((SUBLANES, sorted_size), f32), ((share, LANES), f32)],
        [
            pltpu.VMEM((size, size), bf16),
            pltpu.VMEM((size + up_to(groups * block, SUBLANES), LANES), f32),
            pltpu.VMEM((sorted_size, LANES), f32),
            pltpu.VMEM((size, sorted_size), f32),
            pltpu.SemaphoreType.DMA,
        ],
        (coupling, growth.reshape(1, size), dissipation.reshape(1, size), blown),
        10**9,
        (0,),
    )
    pieces = call(
        functools.partial(integrate_kernel, share, size),
        ((devices * block, LANES), f32),
        [],
        (pieces, weights, sorted_rates, wind_here),
        10**9,
    )
    pieces = transpose_all(pieces)
    result = call(
        functools.partial(spread_kernel, share),
        ((bins, points), f32),
        [pltpu.VMEM((tiles, bins, LANES), f32)],
        (pieces, place),
        10**8,
    )
    return result[None, :bins_here]


def solution(mesh):
    in_specs = (
        P("nest", "bin", None),
        P(None, "bin"),
        P(),
        P(),
        P(),
        P("nest", None),
        P("nest", None, None),
        P("nest", None),
        P("nest", None),
        P("nest", None),
        P("nest"),
    )
    out_specs = P("nest", "bin", None)
    return jax.shard_map(local, mesh=mesh, in_specs=in_specs, out_specs=out_specs, check_vma=False)
```

```python
import functools
import math

import jax
import jax.numpy as jnp
from jax import lax
from jax.experimental import pallas as pl
from jax.experimental.pallas import tpu as pltpu
from jax.sharding import PartitionSpec as P

SUBSTEPS = 2
SRC = 5
LANES = 128
SUBLANES = 8

source_dt = 0.25
tiny_add = 1e-06
f32 = jnp.float32
bf16 = jnp.bfloat16


def up_to(value, unit):
    return -(-value // unit) * unit


def grid_shape(points):
    cols_count = min(256, points // 4)
    return points // cols_count, cols_count


def dot(left, right):
    return jnp.dot(left, right, preferred_element_type=f32)


def dot_t(left, right):
    return lax.dot_general(left, right, (((1,), (1,)), ((), ())), preferred_element_type=f32)


def split(values):
    rest = values - values.astype(bf16).astype(f32)
    return jnp.concatenate([values, rest], axis=0).astype(bf16)


def joined(terms):
    half = terms.shape[0] // 2
    return terms[:half] + terms[half:]


def one_hot(rows, index):
    at = lax.broadcasted_iota(jnp.int32, (rows, index.shape[1]), 0)
    return jnp.where(at == index, 1.0, 0.0).astype(bf16)


def column(row):
    size = row.shape[1]
    at = lax.broadcasted_iota(jnp.int32, (size, size), 0)
    across = lax.broadcasted_iota(jnp.int32, (size, size), 1)
    return jnp.sum(jnp.where(at == across, row, 0.0), axis=1, keepdims=True)


def each(count, body):
    if count <= 16:
        for step in range(count):
            body(step)
    else:
        pl.loop(0, count)(body)


def total_of(count, shape, term):
    total = jnp.zeros(shape, f32)
    if count <= 16:
        for step in range(count):
            total = total + term(step)
        return total
    return lax.fori_loop(0, count, lambda step, total: total + term(step), total)


def span(start, size):
    if isinstance(start, int):
        return pl.ds(start * size, size)
    return pl.ds(pl.multiple_of(start * size, size), size)


def rows_of(start, size):
    return pl.ds(start * size, size)


def rows_stacked(tiles):
    at = lax.broadcasted_iota(jnp.int32, (SUBLANES, LANES), 0)
    stacked = eight(tiles[0])
    for k in range(1, len(tiles)):
        stacked = jnp.where(at == k, eight(tiles[k]), stacked)
    return stacked


def tiles_of(row):
    return [row[:, k * LANES : (k + 1) * LANES] for k in range(row.shape[1] // LANES)]


def taken_from(tables, index):
    lane, tile = index & (LANES - 1), index >> (LANES - 1).bit_length()
    found = None
    for k, table in enumerate(tables):
        here = jnp.take_along_axis(eight(table), lane, axis=1, mode="promise_in_bounds")
        found = here if k == 0 else jnp.where(tile == k, here, found)
    return found


def look_up(table, index):
    count = index.shape[1] // LANES
    found = taken_from(tiles_of(table), rows_stacked(tiles_of(index)))
    return jnp.concatenate([found[k : k + 1] for k in range(count)], axis=1)


def walk(tables, order, rank):
    rows_count, _, cols_count = order.shape
    count = cols_count // LANES
    bits = (cols_count - 1).bit_length()
    at = lax.broadcasted_iota(jnp.int32, (SUBLANES, LANES), 0)
    place = (at % count) * LANES + lax.broadcasted_iota(jnp.int32, (SUBLANES, LANES), 1)

    first = tables[0:1, 0:cols_count]
    ahead = jnp.where(at < count, rows_stacked(tiles_of(first)), 0)
    behind = rows_stacked(tiles_of(tables[1:2, 0:cols_count]))
    behind = jnp.where(place == 0, 0, behind)
    steps = jnp.where(place == 0, 0, 1)
    for bit in range(bits):
        far = taken_from([ahead[k : k + 1] for k in range(count)], ahead)
        both = (steps << bits) + behind
        back = taken_from([both[k : k + 1] for k in range(count)], behind)
        ahead = jnp.where((at >= count) & ((place >> bit) & 1 == 0), ahead, far)
        steps = steps + (back >> bits)
        behind = back & ((1 << bits) - 1)
    order[0] = jnp.concatenate([ahead[count + k : count + k + 1] for k in range(count)], axis=1)
    rank[0] = jnp.concatenate([steps[k : k + 1] for k in range(count)], axis=1)

    def next_row(row):
        north = tables[2:3, span(row, cols_count)] - (row + 1) * cols_count
        south = tables[3:4, span(row + 1, cols_count)] - row * cols_count
        order[row + 1] = look_up(north, order[row])
        rank[row + 1] = look_up(rank[row], south)

    each(rows_count - 1, next_row)


def grid_places(listed, rank):
    rows_count, _, cols_count = rank.shape
    tiles = tiles_of(listed)
    found = []
    for tile in tiles:
        index = eight(tile)

        def column_in(row, best):
            first = row * cols_count
            within = jnp.clip(index - first, 0, cols_count - 1)
            here = taken_from(tiles_of(rank[row]), within)
            return jnp.where(index - first == within, here + first, best)

        best = jnp.zeros((SUBLANES, LANES), jnp.int32)
        if rows_count <= 16:
            for row in range(rows_count):
                best = column_in(row, best)
        else:
            best = lax.fori_loop(0, rows_count, column_in, best)
        found.append(best[0:1])
    return jnp.concatenate(found, axis=1)


def down(row):
    wide = jnp.broadcast_to(row.astype(f32), (LANES, row.shape[1]))
    return jnp.transpose(wide).astype(jnp.int32)


def one_hot_across(index, first, count):
    lane = lax.broadcasted_iota(jnp.int32, index.shape, 1)
    tiles = [
        jnp.where(lane + (first + tile * LANES) == index, 1.0, 0.0).astype(bf16)
        for tile in range(count // LANES)
    ]
    return jnp.concatenate(tiles, axis=1)


def eight(row):
    return jnp.broadcast_to(row, (SUBLANES, row.shape[1]))


def face_at(cell, onward, curve, rate):
    estimate = cell + (0.5 - 0.5 * rate) * (onward - cell) - (1.0 - rate * rate) / 6.0 * curve
    return jnp.clip(estimate, jnp.minimum(cell, onward), jnp.maximum(cell, onward))


def advance(field, moved, faces, sea, rate_east, rate_north):
    rows_count, _, cols_count = field.shape

    def east(row):
        cell = field[row]
        onward = pltpu.roll(cell, cols_count - 1, 1)
        slope = onward - cell
        bent = slope - pltpu.roll(slope, 1, 1)
        curve = jnp.where(rate_east >= 0.0, bent, pltpu.roll(bent, cols_count - 1, 1))
        face = face_at(cell, onward, curve, rate_east)
        moved[row] = cell - rate_east * (face - pltpu.roll(face, 1, 1))

    each(rows_count, east)

    def face(row):
        ahead, second, behind = ((row + k + rows_count) % rows_count for k in (1, 2, -1))
        cell, onward = moved[row], moved[ahead]
        slope = onward - cell
        curve = jnp.where(
            rate_north >= 0.0, slope - (cell - moved[behind]), (moved[second] - onward) - slope
        )
        faces[row] = face_at(cell, onward, curve, rate_north)

    each(rows_count, face)

    def north(row):
        behind = (row - 1 + rows_count) % rows_count
        field[row] = (moved[row] - rate_north * (faces[row] - faces[behind])) * sea[row]

    each(rows_count, north)


def landing(row, into, lists, cols_count):
    if into.shape[0] > 1:
        return into[row]
    return one_hot_across(down(lists[1:2]), row * cols_count, cols_count)


def count_kernel(steps_in, steps):
    steps[...] = jnp.broadcast_to(steps_in[...].astype(f32), steps.shape)


def prepare_kernel(
    spectra,
    tables,
    wet,
    send,
    recv,
    order,
    rank,
    base,
    into,
    sea,
    taken,
    lists,
):
    rows_count, bins, cols_count = base.shape
    listed = send.shape[1]
    walk(tables, order, rank)
    lists[0:1] = grid_places(send[...], rank)
    lists[1:2] = grid_places(recv[...], rank)
    recv_down = down(lists[1:2])

    def place(row):
        own = one_hot(cols_count, order[row])
        here = one_hot_across(recv_down, row * cols_count, cols_count)
        if into.shape[0] > 1:
            into[row] = here
        got = dot(jnp.ones((SUBLANES, listed), bf16), here)[0:1]
        taken[row] = got
        covered = look_up(wet[0:1, span(row, cols_count)], order[row]).astype(f32)
        sea[row] = covered
        values = joined(dot(split(spectra[:, span(row, cols_count)]), own))
        base[row] = values * (covered * (1.0 - got))

    each(rows_count, place)


def first_kernel(
    base,
    into,
    sea,
    lists,
    spectra_b,
    send_b,
    courant,
    steps,
    field,
    outgoing,
    rates,
    moved,
    faces,
):
    rows_count, bins, cols_count = base.shape
    listed = lists.shape[1]
    second = jnp.where(steps[0:1] > 1.0, 1.0, 0.0)
    for which in range(2):
        rate = column(courant[which : which + 1, :]) / steps[0:1]
        rates[which] = jnp.broadcast_to(rate, (bins, cols_count))
        rates[2 + which] = jnp.broadcast_to(rate * second, (bins, cols_count))
    rates[4] = jnp.broadcast_to(second, (bins, cols_count))

    def sent(row):
        own = one_hot(cols_count, send_b[...] - row * cols_count)
        return dot(split(spectra_b[:, span(row, cols_count)]), own)

    incoming = total_of(rows_count, (2 * bins, listed), sent).astype(bf16)

    def take(row):
        field[row] = base[row] + joined(dot(incoming, landing(row, into, lists, cols_count)))

    each(rows_count, take)
    advance(field, moved, faces, sea, rates[0], rates[1])

    def sending(row):
        return dot(split(field[row]), one_hot(cols_count, lists[0:1] - row * cols_count))

    outgoing[...] = joined(total_of(rows_count, (2 * bins, listed), sending))


def picked(row, ranks, picks, sea_count):
    if picks.shape[0] == ranks.shape[0]:
        return picks[row]
    return one_hot_across(down(ranks[row] - 1.0), 0, sea_count)


def places_kernel(order, rank, sea, wind, ranks, picks, place, blown):
    rows_count, _, cols_count = order.shape
    sea_count = blown.shape[1]
    at = lax.broadcasted_iota(jnp.int32, (cols_count, cols_count), 0)
    across = lax.broadcasted_iota(jnp.int32, (cols_count, cols_count), 1)
    upper = jnp.where(at <= across, 1.0, 0.0).astype(bf16)

    def number(row, before):
        here = sea[row]
        number_of = dot(eight(here).astype(bf16), upper)[0:1] + before
        number_of = jnp.where(here > 0.0, number_of, 0.0)
        ranks[row] = number_of
        if picks.shape[0] == rows_count:
            picks[row] = one_hot_across(down(number_of - 1.0), 0, sea_count)
        place[0:1, span(row, cols_count)] = look_up(number_of.astype(jnp.int32), rank[row])
        return before + jnp.sum(here, axis=1, keepdims=True)

    before = jnp.zeros((1, 1), f32)
    if rows_count <= 16:
        for row in range(rows_count):
            before = number(row, before)
    else:
        lax.fori_loop(0, rows_count, number, before)

    def there(row):
        by_grid = look_up(wind[0:1, span(row, cols_count)], order[row])
        return dot(split(eight(by_grid)), picked(row, ranks, picks, sea_count))

    blown[...] = joined(total_of(rows_count, (2 * SUBLANES, sea_count), there))


def second_kernel(
    share,
    field_in,
    incoming,
    into,
    lists,
    taken,
    sea,
    rates,
    ranks,
    picks,
    pieces,
    field,
    moved,
    faces,
    columns,
):
    rows_count, bins, cols_count = field.shape
    tiles, _, _ = columns.shape
    sea_count = tiles * LANES
    terms = split(incoming[...])

    def take(row):
        got = joined(dot(terms, landing(row, into, lists, cols_count)))
        field[row] = jnp.where(taken[row] * rates[4, 0:1] > 0.5, got, field_in[row])

    each(rows_count, take)
    advance(field, moved, faces, sea, rates[2], rates[3])

    def at_sea(row):
        return dot(split(field[row]), picked(row, ranks, picks, sea_count))

    total = joined(total_of(rows_count, (2 * bins, sea_count), at_sea))
    for tile in range(tiles):
        columns[tile] = total[:, tile * LANES : (tile + 1) * LANES]
    groups = LANES // share
    block = pieces.shape[0] // (tiles * groups)
    lane_group = lax.broadcasted_iota(jnp.int32, (block, LANES), 1) // share

    def fold(tile):
        parts = [columns[tile, pl.ds(q, block, stride=groups)] for q in range(groups)]
        for j in range(groups):
            piece = parts[j]
            for q in range(groups):
                if q != j:
                    part = pltpu.roll(parts[q], ((q - j) % groups) * share, 1)
                    piece = jnp.where(lane_group == q, part, piece)
            pieces[rows_of(tile * groups + j, block)] = piece

    each(tiles, fold)


def weights_kernel(
    devices,
    bins,
    share,
    coupling_in,
    growth,
    dissipation,
    blown,
    weights,
    rates,
    wind,
    coupling,
    rows,
    sorted_rows,
    turned,
    arrived,
):
    copy = pltpu.make_async_copy(coupling_in, coupling, arrived)
    copy.start()
    size = coupling.shape[0]
    lane_tiles = size // LANES
    groups = LANES // share
    block = sorted_rows.shape[0] // (devices * groups)
    mine = pltpu.roll(blown[...], blown.shape[1] - lax.axis_index("bin") * share, 1)
    wind[...] = jnp.broadcast_to(column(mine[0:1, 0:share]), wind.shape)
    rows[size:] = jnp.zeros((rows.shape[0] - size, LANES), f32)

    def sort():
        if groups * block == bins:
            every = devices * block
            taken = [rows[pl.ds(q, every, stride=groups)] for q in range(groups)]
            return jnp.concatenate(taken, axis=0)
        at = groups * lax.broadcasted_iota(jnp.int32, (block, LANES), 0)
        for q in range(groups):

            def move(device, q=q):
                taken = rows[pl.ds(device * bins + q, block, stride=groups)]
                taken = jnp.where(at + q < bins, taken, 0.0)
                sorted_rows[rows_of(q * devices + device, block)] = taken

            each(devices, move)
        return sorted_rows[...]

    at = lax.broadcasted_iota(jnp.int32, (LANES, LANES), 0)

    def lift(tile):
        here = span(tile, LANES)
        both = jnp.where(at == 0, growth[0:1, here], jnp.where(at == 1, dissipation[0:1, here], 0.0))
        rows[here] = jnp.transpose(both)

    each(lane_tiles, lift)
    rates[...] = jnp.transpose(sort())[0:SUBLANES]
    copy.wait()

    def turn(tile):
        rows[0:size] = coupling[:, span(tile, LANES)].astype(f32)
        turned[span(tile, LANES)] = jnp.transpose(sort())

    def lay(tile):
        rows[0:size] = turned[:, span(tile, LANES)]
        weights[:, span(tile, LANES)] = sort().astype(bf16)

    each(lane_tiles, turn)
    each(weights.shape[1] // LANES, lay)


def padded_transpose(array):
    rows_count, cols_count = array.shape
    full = up_to(rows_count, LANES)
    if full > rows_count:
        array = jnp.concatenate([array, jnp.zeros((full - rows_count, cols_count), f32)], axis=0)
    return jnp.transpose(array)


def integrate_kernel(share, total_bins, pieces, weights, rates, wind, out):
    width = pieces.shape[0]
    groups = LANES // share
    turned = padded_transpose(pieces[...])
    now = [turned[q * share : (q + 1) * share, 0:width] for q in range(groups)]
    now = jnp.concatenate(now, axis=1)
    push = 1.0 + source_dt * (rates[0:1] * wind[:, 0:1])
    drag = source_dt * rates[1:2]
    for repeat in range(SRC):
        linear = dot(now.astype(bf16), weights[...])
        mean = jnp.sum(now * now, axis=1, keepdims=True) * (1.0 / total_bins)
        spread = jnp.sqrt(mean + tiny_add)
        now = (now * push + source_dt * linear) / (1.0 + drag * spread)
    back = [now[:, q * width : (q + 1) * width] for q in range(groups)]
    back = jnp.concatenate(back, axis=0)
    full = up_to(width, LANES)
    if full > width:
        back = jnp.concatenate([back, jnp.zeros((LANES, full - width), f32)], axis=1)
    out[...] = jnp.transpose(back)[0:width]


def spread_kernel(share, pieces, place, out, columns):
    tiles, bins, _ = columns.shape
    groups = LANES // share
    block = pieces.shape[0] // (tiles * groups)
    sea_count = tiles * LANES
    points = place.shape[1]
    rows_count, cols_count = grid_shape(points)
    lane_group = lax.broadcasted_iota(jnp.int32, (block, LANES), 1) // share
    if groups * block < bins:
        columns[:, groups * block :] = jnp.zeros((tiles, bins - groups * block, LANES), f32)

    def unfold(tile):
        parts = [pieces[rows_of(tile * groups + j, block)] for j in range(groups)]
        for q in range(groups):
            part = parts[q]
            for j in range(groups):
                if j != q:
                    other = pltpu.roll(parts[j], ((j - q) % groups) * share, 1)
                    part = jnp.where(lane_group == j, other, part)
            columns[tile, pl.ds(q, block, stride=groups)] = part

    each(tiles, unfold)
    terms = jnp.concatenate([split(columns[tile]) for tile in range(tiles)], axis=1)

    def scatter(row):
        picks = one_hot(sea_count, place[0:1, span(row, cols_count)] - 1)
        out[:, span(row, cols_count)] = joined(dot(terms, picks))

    each(rows_count, scatter)


def call(kernel, outs, scratch, operands, flops, apart=()):
    held = sum(x.size * x.dtype.itemsize for x in operands)
    single = not isinstance(outs, list)
    shapes = [jax.ShapeDtypeStruct(*out) for out in ([outs] if single else outs)]
    held += sum(x.size * x.dtype.itemsize for x in shapes)
    own = sum(4 * math.prod(getattr(x, "shape", ())) for x in scratch)
    in_vmem = pl.BlockSpec(memory_space=pltpu.VMEM)
    places = [pl.BlockSpec(memory_space=pltpu.HBM) if x in apart else in_vmem for x in range(len(operands))]
    operands = [
        x if x.size == 1 else pltpu.with_memory_space_constraint(x, place.memory_space)
        for x, place in zip(operands, places)
    ]
    return pl.pallas_call(
        kernel,
        out_shape=shapes[0] if single else shapes,
        in_specs=places,
        out_specs=in_vmem if single else [in_vmem] * len(shapes),
        scratch_shapes=scratch,
        compiler_params=pltpu.CompilerParams(vmem_limit_bytes=min(60 << 20, (4 << 20) + held + own)),
        cost_estimate=pl.CostEstimate(flops=flops, bytes_accessed=held, transcendentals=0),
    )(*operands)


def local(
    spectra,
    courant,
    coupling,
    growth,
    dissipation,
    wind,
    neighbours,
    wet_mask,
    send_list,
    recv_list,
    substep_count,
):
    devices = lax.axis_size("bin")
    field = spectra[0]
    bins_here, points = field.shape
    rows_count, cols_count = grid_shape(points)
    sea_count = points // 2
    listed = send_list.shape[1]
    share = sea_count // devices
    groups = LANES // share
    block = -(-bins_here // groups)
    bins = up_to(groups * block, SUBLANES)
    size = devices * bins_here
    sorted_size = devices * groups * block
    extra = bins - bins_here
    if extra:
        field = jnp.pad(field, ((0, extra), (0, 0)))
        courant = jnp.pad(courant, ((0, 0), (0, extra)))
    def transpose_all(pieces):
        pieces = pieces.reshape(devices, 1, block * LANES)
        pieces = lax.all_to_all(pieces, "bin", split_axis=0, concat_axis=0)
        return pieces.reshape(devices * block, LANES)

    def swap(array):
        return lax.ppermute(array, "nest", [(0, 1), (1, 0)])

    spectra_b, send_b = swap(field), swap(send_list)
    grid = (rows_count, bins, cols_count)
    row_of = (rows_count, 1, cols_count)
    steps = call(
        count_kernel, ((SUBLANES, cols_count), f32), [], (substep_count.reshape(1, 1),), 10**9
    )
    early = (
        field,
        neighbours[0],
        wet_mask,
        send_list,
        recv_list,
    )
    kept_into = rows_count if points * listed <= 1 << 22 else 1
    order, rank, base, into, sea, taken, lists = call(
        prepare_kernel,
        [
            (row_of, jnp.int32),
            (row_of, jnp.int32),
            (grid, f32),
            ((kept_into, listed, cols_count), bf16),
            (row_of, f32),
            (row_of, f32),
            ((2, listed), jnp.int32),
        ],
        [],
        early,
        10**9,
    )
    field, outgoing, rates = call(
        first_kernel,
        [(grid, f32), ((bins, listed), f32), ((5, bins, cols_count), f32)],
        [pltpu.VMEM(grid, f32)] * 2,
        (base, into, sea, lists, spectra_b, send_b, courant, steps),
        10**9,
    )
    incoming = swap(outgoing)
    kept = rows_count if points * sea_count <= 1 << 22 else 1
    ranks, picks, place, blown = call(
        places_kernel,
        [
            (row_of, f32),
            ((kept, cols_count, sea_count), bf16),
            ((1, points), jnp.int32),
            ((SUBLANES, sea_count), f32),
        ],
        [],
        (order, rank, sea, wind),
        10**9,
    )
    tiles = sea_count // LANES
    pieces = call(
        functools.partial(second_kernel, share),
        ((devices * block, LANES), f32),
        [*[pltpu.VMEM(grid, f32)] * 3, pltpu.VMEM((tiles, bins, LANES), f32)],
        (field, incoming, into, lists, taken, sea, rates, ranks, picks),
        10**9,
    )
    pieces = transpose_all(pieces)
    weights, sorted_rates, wind_here = call(
        functools.partial(weights_kernel, devices, bins_here, share),
        [((sorted_size, sorted_size), bf16), ((SUBLANES, sorted_size), f32), ((share, LANES), f32)],
        [
            pltpu.VMEM((size, size), bf16),
            pltpu.VMEM((size + up_to(groups * block, SUBLANES), LANES), f32),
            pltpu.VMEM((sorted_size, LANES), f32),
            pltpu.VMEM((size, sorted_size), f32),
            pltpu.SemaphoreType.DMA,
        ],
        (coupling, growth.reshape(1, size), dissipation.reshape(1, size), blown),
        10**9,
        (0,),
    )
    pieces = call(
        functools.partial(integrate_kernel, share, size),
        ((devices * block, LANES), f32),
        [],
        (pieces, weights, sorted_rates, wind_here),
        10**9,
    )
    pieces = transpose_all(pieces)
    result = call(
        functools.partial(spread_kernel, share),
        ((bins, points), f32),
        [pltpu.VMEM((tiles, bins, LANES), f32)],
        (pieces, place),
        10**8,
    )
    return result[None, :bins_here]


def solution(mesh):
    in_specs = (
        P("nest", "bin", None),
        P(None, "bin"),
        P(),
        P(),
        P(),
        P("nest", None),
        P("nest", None, None),
        P("nest", None),
        P("nest", None),
        P("nest", None),
        P("nest"),
    )
    out_specs = P("nest", "bin", None)
    return jax.shard_map(local, mesh=mesh, in_specs=in_specs, out_specs=out_specs, check_vma=False)
```

```python
import functools
import math

import jax
import jax.numpy as jnp
from jax import lax
from jax.experimental import pallas as pl
from jax.experimental.pallas import tpu as pltpu
from jax.sharding import PartitionSpec as P

SUBSTEPS = 2
SRC = 5
LANES = 128
SUBLANES = 8

source_dt = 0.25
tiny_add = 1e-06
f32 = jnp.float32
bf16 = jnp.bfloat16


def up_to(value, unit):
    return -(-value // unit) * unit


def grid_shape(points):
    cols_count = min(256, points // 4)
    return points // cols_count, cols_count


def dot(left, right):
    return jnp.dot(left, right, preferred_element_type=f32)


def dot_t(left, right):
    return lax.dot_general(left, right, (((1,), (1,)), ((), ())), preferred_element_type=f32)


def split(values):
    rest = values - values.astype(bf16).astype(f32)
    return jnp.concatenate([values, rest], axis=0).astype(bf16)


def joined(terms):
    half = terms.shape[0] // 2
    return terms[:half] + terms[half:]


def one_hot(rows, index):
    at = lax.broadcasted_iota(jnp.int32, (rows, index.shape[1]), 0)
    return jnp.where(at == index, 1.0, 0.0).astype(bf16)


def column(row):
    size = row.shape[1]
    at = lax.broadcasted_iota(jnp.int32, (size, size), 0)
    across = lax.broadcasted_iota(jnp.int32, (size, size), 1)
    return jnp.sum(jnp.where(at == across, row, 0.0), axis=1, keepdims=True)


def each(count, body):
    if count <= 16:
        for step in range(count):
            body(step)
    else:
        pl.loop(0, count)(body)


def total_of(count, shape, term):
    total = jnp.zeros(shape, f32)
    if count <= 16:
        for step in range(count):
            total = total + term(step)
        return total
    return lax.fori_loop(0, count, lambda step, total: total + term(step), total)


def span(start, size):
    if isinstance(start, int):
        return pl.ds(start * size, size)
    return pl.ds(pl.multiple_of(start * size, size), size)


def rows_of(start, size):
    return pl.ds(start * size, size)


def rows_stacked(tiles):
    at = lax.broadcasted_iota(jnp.int32, (SUBLANES, LANES), 0)
    stacked = eight(tiles[0])
    for k in range(1, len(tiles)):
        stacked = jnp.where(at == k, eight(tiles[k]), stacked)
    return stacked


def tiles_of(row):
    return [row[:, k * LANES : (k + 1) * LANES] for k in range(row.shape[1] // LANES)]


def taken_from(tables, index):
    lane, tile = index & (LANES - 1), index >> (LANES - 1).bit_length()
    found = None
    for k, table in enumerate(tables):
        here = jnp.take_along_axis(eight(table), lane, axis=1, mode="promise_in_bounds")
        found = here if k == 0 else jnp.where(tile == k, here, found)
    return found


def look_up(table, index):
    count = index.shape[1] // LANES
    found = taken_from(tiles_of(table), rows_stacked(tiles_of(index)))
    return jnp.concatenate([found[k : k + 1] for k in range(count)], axis=1)


def walk(tables, order, rank):
    rows_count, _, cols_count = order.shape
    count = cols_count // LANES
    bits = (cols_count - 1).bit_length()
    at = lax.broadcasted_iota(jnp.int32, (SUBLANES, LANES), 0)
    place = (at % count) * LANES + lax.broadcasted_iota(jnp.int32, (SUBLANES, LANES), 1)

    first = tables[0:1, 0:cols_count]
    ahead = jnp.where(at < count, rows_stacked(tiles_of(first)), 0)
    behind = rows_stacked(tiles_of(tables[1:2, 0:cols_count]))
    behind = jnp.where(place == 0, 0, behind)
    steps = jnp.where(place == 0, 0, 1)
    for bit in range(bits):
        far = taken_from([ahead[k : k + 1] for k in range(count)], ahead)
        both = (steps << bits) + behind
        back = taken_from([both[k : k + 1] for k in range(count)], behind)
        ahead = jnp.where((at >= count) & ((place >> bit) & 1 == 0), ahead, far)
        steps = steps + (back >> bits)
        behind = back & ((1 << bits) - 1)
    order[0] = jnp.concatenate([ahead[count + k : count + k + 1] for k in range(count)], axis=1)
    rank[0] = jnp.concatenate([steps[k : k + 1] for k in range(count)], axis=1)

    def north(row):
        return tables[2:3, span(row, cols_count)] - (row + 1) * cols_count

    def south(row):
        return tables[3:4, span(row, cols_count)] - (row - 1) * cols_count

    if rows_count <= 16:
        there, back = north(0), south(1)
        for row in range(1, rows_count):
            order[row] = look_up(there, order[0])
            rank[row] = look_up(rank[0], back)
            if row + 1 < rows_count:
                there, back = look_up(north(row), there), look_up(back, south(row + 1))
    else:

        def next_row(row):
            order[row + 1] = look_up(north(row), order[row])
            rank[row + 1] = look_up(rank[row], south(row + 1))

        each(rows_count - 1, next_row)


def grid_places(listed, rank):
    rows_count, _, cols_count = rank.shape
    tiles = tiles_of(listed)
    found = []
    for tile in tiles:
        index = eight(tile)

        def column_in(row, best):
            first = row * cols_count
            within = jnp.clip(index - first, 0, cols_count - 1)
            here = taken_from(tiles_of(rank[row]), within)
            return jnp.where(index - first == within, here + first, best)

        best = jnp.zeros((SUBLANES, LANES), jnp.int32)
        if rows_count <= 16:
            for row in range(rows_count):
                best = column_in(row, best)
        else:
            best = lax.fori_loop(0, rows_count, column_in, best)
        found.append(best[0:1])
    return jnp.concatenate(found, axis=1)


def down(row):
    wide = jnp.broadcast_to(row.astype(f32), (LANES, row.shape[1]))
    return jnp.transpose(wide).astype(jnp.int32)


def one_hot_across(index, first, count):
    lane = lax.broadcasted_iota(jnp.int32, index.shape, 1)
    tiles = [
        jnp.where(lane + (first + tile * LANES) == index, 1.0, 0.0).astype(bf16)
        for tile in range(count // LANES)
    ]
    return jnp.concatenate(tiles, axis=1)


def eight(row):
    return jnp.broadcast_to(row, (SUBLANES, row.shape[1]))


def face_at(cell, slope, onward, curve, coefs):
    _, lean, bend = coefs
    estimate = cell + lean * slope - bend * curve
    return jnp.clip(estimate, jnp.minimum(cell, onward), jnp.maximum(cell, onward))


def moved_east(cell, coefs):
    size = cell.shape[1]
    rate = coefs[0]
    onward = pltpu.roll(cell, size - 1, 1)
    slope = onward - cell
    bent = slope - pltpu.roll(slope, 1, 1)
    curve = jnp.where(rate >= 0.0, bent, pltpu.roll(bent, size - 1, 1))
    face = face_at(cell, slope, onward, curve, coefs)
    return cell - rate * (face - pltpu.roll(face, 1, 1))


def advance(field, moved, faces, sea, east, north):
    rows_count, bins, cols_count = field.shape
    if rows_count <= 16:
        for first in range(0, bins, SUBLANES):
            here = slice(first, first + SUBLANES)
            to_east, to_north = ([x[here] for x in coefs] for coefs in (east, north))
            cells = [moved_east(field[row, here], to_east) for row in range(rows_count)]
            onward = cells[1:] + cells[:1]
            slopes = [b - a for a, b in zip(cells, onward)]
            bents = [slopes[row] - slopes[row - 1] for row in range(rows_count)]
            forward = to_north[0] >= 0.0
            over = [
                face_at(
                    cells[row],
                    slopes[row],
                    onward[row],
                    jnp.where(forward, bents[row], bents[(row + 1) % rows_count]),
                    to_north,
                )
                for row in range(rows_count)
            ]
            for row in range(rows_count):
                change = to_north[0] * (over[row] - over[row - 1])
                field[row, here] = (cells[row] - change) * sea[row]
        return

    def to_east(row):
        moved[row] = moved_east(field[row], east)

    def over_row(row):
        ahead, second, behind = ((row + k + rows_count) % rows_count for k in (1, 2, -1))
        cell, onward = moved[row], moved[ahead]
        slope = onward - cell
        curve = jnp.where(
            north[0] >= 0.0, slope - (cell - moved[behind]), (moved[second] - onward) - slope
        )
        faces[row] = face_at(cell, slope, onward, curve, north)

    def to_north(row):
        behind = (row - 1 + rows_count) % rows_count
        field[row] = (moved[row] - north[0] * (faces[row] - faces[behind])) * sea[row]

    for step in (to_east, over_row, to_north):
        each(rows_count, step)


def coefs_of(rates, which):
    return [rates[3 * which + k] for k in range(3)]


def landing(row, into, lists, cols_count):
    if into.shape[0] > 1:
        return into[row]
    return one_hot_across(down(lists[1:2]), row * cols_count, cols_count)


def count_kernel(steps_in, steps):
    steps[...] = jnp.broadcast_to(steps_in[...].astype(f32), steps.shape)


def prepare_kernel(
    spectra,
    tables,
    wet,
    send,
    recv,
    order,
    rank,
    base,
    into,
    sea,
    taken,
    lists,
):
    rows_count, bins, cols_count = base.shape
    listed = send.shape[1]
    walk(tables, order, rank)
    lists[0:1] = grid_places(send[...], rank)
    lists[1:2] = grid_places(recv[...], rank)
    recv_down = down(lists[1:2])

    def place(row):
        own = one_hot(cols_count, order[row])
        here = one_hot_across(recv_down, row * cols_count, cols_count)
        if into.shape[0] > 1:
            into[row] = here
        got = dot(jnp.ones((SUBLANES, listed), bf16), here)[0:1]
        taken[row] = got
        covered = look_up(wet[0:1, span(row, cols_count)], order[row]).astype(f32)
        sea[row] = covered
        values = joined(dot(split(spectra[:, span(row, cols_count)]), own))
        base[row] = values * (covered * (1.0 - got))

    each(rows_count, place)


def first_kernel(
    base,
    into,
    sea,
    lists,
    spectra_b,
    send_b,
    courant,
    steps,
    field,
    outgoing,
    rates,
    moved,
    faces,
):
    rows_count, bins, cols_count = base.shape
    listed = lists.shape[1]
    second = jnp.where(steps[0:1] > 1.0, 1.0, 0.0)
    for which in range(2):
        rate = column(courant[which : which + 1, :]) / steps[0:1]
        for k, value in enumerate((rate, rate * second)):
            at = 3 * (2 * k + which)
            rates[at] = jnp.broadcast_to(value, (bins, cols_count))
            rates[at + 1] = 0.5 - 0.5 * rates[at]
            rates[at + 2] = (1.0 - rates[at] * rates[at]) * (1.0 / 6.0)
    rates[12] = jnp.broadcast_to(second, (bins, cols_count))

    def sent(row):
        own = one_hot(cols_count, send_b[...] - row * cols_count)
        return dot(split(spectra_b[:, span(row, cols_count)]), own)

    incoming = total_of(rows_count, (2 * bins, listed), sent).astype(bf16)

    def take(row):
        field[row] = base[row] + joined(dot(incoming, landing(row, into, lists, cols_count)))

    each(rows_count, take)
    advance(field, moved, faces, sea, coefs_of(rates, 0), coefs_of(rates, 1))

    def sending(row):
        return dot(split(field[row]), one_hot(cols_count, lists[0:1] - row * cols_count))

    outgoing[...] = joined(total_of(rows_count, (2 * bins, listed), sending))


def picked(row, ranks, picks, sea_count):
    if picks.shape[0] == ranks.shape[0]:
        return picks[row]
    return one_hot_across(down(ranks[row] - 1.0), 0, sea_count)


def places_kernel(rank, sea, coupling, growth, dissipation, ranks, picks, place, weights, rates):
    rows_count, _, cols_count = rank.shape
    sea_count = picks.shape[2]
    at = lax.broadcasted_iota(jnp.int32, (cols_count, cols_count), 0)
    across = lax.broadcasted_iota(jnp.int32, (cols_count, cols_count), 1)
    upper = jnp.where(at <= across, 1.0, 0.0).astype(bf16)

    def number(row, before):
        here = sea[row]
        number_of = dot(eight(here).astype(bf16), upper)[0:1] + before
        number_of = jnp.where(here > 0.0, number_of, 0.0)
        ranks[row] = number_of
        if picks.shape[0] == rows_count:
            picks[row] = one_hot_across(down(number_of - 1.0), 0, sea_count)
        place[0:1, span(row, cols_count)] = look_up(number_of.astype(jnp.int32), rank[row])
        return before + jnp.sum(here, axis=1, keepdims=True)

    before = jnp.zeros((1, 1), f32)
    if rows_count <= 16:
        for row in range(rows_count):
            before = number(row, before)
    else:
        lax.fori_loop(0, rows_count, number, before)
    weights[...] = jnp.transpose(coupling[...])
    rates[0:1] = growth[...]
    rates[1:2] = dissipation[...]


def second_kernel(
    share,
    field_in,
    incoming,
    into,
    lists,
    taken,
    sea,
    rates,
    ranks,
    picks,
    order,
    wind,
    pieces,
    blown,
    field,
    moved,
    faces,
    columns,
):
    rows_count, bins, cols_count = field.shape
    tiles, _, _ = columns.shape
    sea_count = tiles * LANES
    terms = split(incoming[...])

    def take(row):
        got = joined(dot(terms, landing(row, into, lists, cols_count)))
        field[row] = jnp.where(taken[row] * rates[12, 0:1] > 0.5, got, field_in[row])

    each(rows_count, take)
    advance(field, moved, faces, sea, coefs_of(rates, 2), coefs_of(rates, 3))

    def at_sea(row):
        by_grid = look_up(wind[0:1, span(row, cols_count)], order[row])
        terms = jnp.concatenate([split(field[row]), split(eight(by_grid))], axis=0)
        return dot(terms, picked(row, ranks, picks, sea_count))

    total = total_of(rows_count, (2 * bins + 2 * SUBLANES, sea_count), at_sea)
    blown[...] = joined(total[2 * bins :])
    total = joined(total[: 2 * bins])
    for tile in range(tiles):
        columns[tile] = total[:, tile * LANES : (tile + 1) * LANES]
    groups = LANES // share
    block = pieces.shape[0] // (tiles * groups)
    lane_group = lax.broadcasted_iota(jnp.int32, (block, LANES), 1) // share

    def fold(tile):
        parts = [columns[tile, pl.ds(q, block, stride=groups)] for q in range(groups)]
        for j in range(groups):
            piece = parts[j]
            for q in range(groups):
                if q != j:
                    part = pltpu.roll(parts[q], ((q - j) % groups) * share, 1)
                    piece = jnp.where(lane_group == q, part, piece)
            pieces[rows_of(tile * groups + j, block)] = piece

    each(tiles, fold)


def integrate_kernel(share, pieces, weights, rates, blown, out, values, rolled):
    size = weights.shape[0]
    devices = blown.shape[1] // share
    groups = LANES // share
    block = pieces.shape[0] // devices
    bins = size // devices
    even = bins == groups * block

    def bins_of(device, q):
        return pl.ds(device * bins + q, block, stride=groups)

    for q in range(groups):
        part = pieces[...]
        if q:
            part = pltpu.roll(part, LANES - q * share, 1)
        if even:
            values[pl.ds(q, devices * block, stride=groups)] = part
        else:
            rolled[q] = part
    if not even:

        def unfold(device):
            for q in range(groups):
                values[bins_of(device, q)] = rolled[q, rows_of(device, block)]

        pl.loop(0, devices)(unfold)
    now = jnp.transpose(values[0:size])[0:share]
    mine = pltpu.roll(blown[...], blown.shape[1] - lax.axis_index("bin") * share, 1)
    push = 1.0 + source_dt * (rates[0:1] * column(mine[0:1, 0:share]))
    drag = source_dt * rates[1:2]
    for repeat in range(SRC):
        linear = dot(now.astype(bf16), weights[...])
        mean = jnp.sum(now * now, axis=1, keepdims=True) * (1.0 / size)
        spread = jnp.sqrt(mean + tiny_add)
        now = (now * push + source_dt * linear) / (1.0 + drag * spread)
    values[0:size] = jnp.transpose(jnp.concatenate([now, jnp.zeros((LANES - share, size), f32)], axis=0))
    if not even:

        def fold(device):
            for q in range(groups):
                rolled[q, rows_of(device, block)] = values[bins_of(device, q)]

        pl.loop(0, devices)(fold)
    lane_group = lax.broadcasted_iota(jnp.int32, out.shape, 1) // share
    result = None
    for q in range(groups):
        part = values[pl.ds(q, devices * block, stride=groups)] if even else rolled[q]
        if q:
            part = pltpu.roll(part, q * share, 1)
        result = part if q == 0 else jnp.where(lane_group == q, part, result)
    out[...] = result


def spread_kernel(share, pieces, place, out, columns, done, left):
    tiles, bins, _ = columns.shape
    groups = LANES // share
    block = pieces.shape[0] // (tiles * groups)
    sea_count = tiles * LANES
    points = place.shape[1]
    rows_count, cols_count = grid_shape(points)
    lane_group = lax.broadcasted_iota(jnp.int32, (block, LANES), 1) // share
    if groups * block < bins:
        columns[:, groups * block :] = jnp.zeros((tiles, bins - groups * block, LANES), f32)

    def unfold(tile):
        parts = [pieces[rows_of(tile * groups + j, block)] for j in range(groups)]
        for q in range(groups):
            part = parts[q]
            for j in range(groups):
                if j != q:
                    other = pltpu.roll(parts[j], ((j - q) % groups) * share, 1)
                    part = jnp.where(lane_group == j, other, part)
            columns[tile, pl.ds(q, block, stride=groups)] = part

    each(tiles, unfold)
    terms = jnp.concatenate([split(columns[tile]) for tile in range(tiles)], axis=1)

    def scatter(row):
        here = span(row, cols_count)
        picks = one_hot(sea_count, place[0:1, here] - 1)
        done[:, here] = joined(dot(terms, picks))
        leave(row).start()

    def leave(row):
        here = span(row, cols_count)
        return pltpu.make_async_copy(done.at[:, here], out.at[:, here], left.at[row])

    each(rows_count, scatter)
    each(rows_count, lambda row: leave(row).wait())


def call(kernel, outs, scratch, operands, flops, apart=(), direct=False):
    held = sum(x.size * x.dtype.itemsize for x in operands)
    single = not isinstance(outs, list)
    shapes = [jax.ShapeDtypeStruct(*out) for out in ([outs] if single else outs)]
    held += sum(x.size * x.dtype.itemsize for x in shapes)
    own = sum(4 * math.prod(getattr(x, "shape", ())) for x in scratch)
    in_vmem = pl.BlockSpec(memory_space=pltpu.VMEM)
    places = [pl.BlockSpec(memory_space=pltpu.HBM) if x in apart else in_vmem for x in range(len(operands))]
    operands = [
        x if x.size == 1 else pltpu.with_memory_space_constraint(x, place.memory_space)
        for x, place in zip(operands, places)
    ]
    return pl.pallas_call(
        kernel,
        out_shape=shapes[0] if single else shapes,
        in_specs=places,
        out_specs=(pl.BlockSpec(memory_space=pltpu.HBM) if direct else in_vmem) if single else [in_vmem] * len(shapes),
        scratch_shapes=scratch,
        compiler_params=pltpu.CompilerParams(vmem_limit_bytes=min(60 << 20, (4 << 20) + held + own)),
        cost_estimate=pl.CostEstimate(flops=flops, bytes_accessed=held, transcendentals=0),
    )(*operands)


def local(
    spectra,
    courant,
    coupling,
    growth,
    dissipation,
    wind,
    neighbours,
    wet_mask,
    send_list,
    recv_list,
    substep_count,
):
    devices = lax.axis_size("bin")
    field = spectra[0]
    bins_here, points = field.shape
    rows_count, cols_count = grid_shape(points)
    sea_count = points // 2
    listed = send_list.shape[1]
    share = sea_count // devices
    groups = LANES // share
    block = -(-bins_here // groups)
    bins = up_to(groups * block, SUBLANES)
    size = devices * bins_here
    extra = bins - bins_here
    if extra:
        field = jnp.pad(field, ((0, extra), (0, 0)))
        courant = jnp.pad(courant, ((0, 0), (0, extra)))
    def transpose_all(pieces):
        pieces = pieces.reshape(devices, 1, block * LANES)
        pieces = lax.all_to_all(pieces, "bin", split_axis=0, concat_axis=0)
        return pieces.reshape(devices * block, LANES)

    def swap(array):
        return lax.ppermute(array, "nest", [(0, 1), (1, 0)])

    spectra_b, send_b = swap(field), swap(send_list)
    grid = (rows_count, bins, cols_count)
    row_of = (rows_count, 1, cols_count)
    steps = call(
        count_kernel, ((SUBLANES, cols_count), f32), [], (substep_count.reshape(1, 1),), 10**9
    )
    early = (
        field,
        neighbours[0],
        wet_mask,
        send_list,
        recv_list,
    )
    kept_into = rows_count if points * listed <= 1 << 22 else 1
    order, rank, base, into, sea, taken, lists = call(
        prepare_kernel,
        [
            (row_of, jnp.int32),
            (row_of, jnp.int32),
            (grid, f32),
            ((kept_into, listed, cols_count), bf16),
            (row_of, f32),
            (row_of, f32),
            ((2, listed), jnp.int32),
        ],
        [],
        early,
        10**9,
    )
    field, outgoing, rates = call(
        first_kernel,
        [(grid, f32), ((bins, listed), f32), ((13, bins, cols_count), f32)],
        [pltpu.VMEM(grid, f32)] * 2,
        (base, into, sea, lists, spectra_b, send_b, courant, steps),
        10**9,
    )
    incoming = swap(outgoing)
    kept = rows_count if points * sea_count <= 1 << 22 else 1
    ranks, picks, place, weights, source_rates = call(
        places_kernel,
        [
            (row_of, f32),
            ((kept, cols_count, sea_count), bf16),
            ((1, points), jnp.int32),
            ((size, size), bf16),
            ((2, size), f32),
        ],
        [],
        (rank, sea, coupling, growth.reshape(1, size), dissipation.reshape(1, size)),
        10**9,
    )
    tiles = sea_count // LANES
    pieces, blown = call(
        functools.partial(second_kernel, share),
        [((devices * block, LANES), f32), ((SUBLANES, sea_count), f32)],
        [*[pltpu.VMEM(grid, f32)] * 3, pltpu.VMEM((tiles, bins, LANES), f32)],
        (field, incoming, into, lists, taken, sea, rates, ranks, picks, order, wind),
        10**9,
    )
    pieces = transpose_all(pieces)
    pieces = call(
        functools.partial(integrate_kernel, share),
        ((devices * block, LANES), f32),
        [
            pltpu.VMEM((size + up_to(groups * block, SUBLANES), LANES), f32),
            pltpu.VMEM((groups, devices * block, LANES), f32),
        ],
        (pieces, weights, source_rates, blown),
        10**9,
    )
    pieces = transpose_all(pieces)
    result = call(
        functools.partial(spread_kernel, share),
        ((bins, points), f32),
        [
            pltpu.VMEM((tiles, bins, LANES), f32),
            pltpu.VMEM((bins, points), f32),
            pltpu.SemaphoreType.DMA((rows_count,)),
        ],
        (pieces, place),
        10**8,
        direct=True,
    )
    return result[None, :bins_here]


def solution(mesh):
    in_specs = (
        P("nest", "bin", None),
        P(None, "bin"),
        P(),
        P(),
        P(),
        P("nest", None),
        P("nest", None, None),
        P("nest", None),
        P("nest", None),
        P("nest", None),
        P("nest"),
    )
    out_specs = P("nest", "bin", None)
    return jax.shard_map(local, mesh=mesh, in_specs=in_specs, out_specs=out_specs, check_vma=False)
```

```python
import functools
import math

import jax
import jax.numpy as jnp
from jax import lax
from jax.experimental import pallas as pl
from jax.experimental.pallas import tpu as pltpu
from jax.sharding import PartitionSpec as P

SUBSTEPS = 2
SRC = 5
LANES = 128
SUBLANES = 8

source_dt = 0.25
tiny_add = 1e-06
f32 = jnp.float32
bf16 = jnp.bfloat16


def up_to(value, unit):
    return -(-value // unit) * unit


def grid_shape(points):
    cols_count = min(256, points // 4)
    return points // cols_count, cols_count


def dot(left, right):
    return jnp.dot(left, right, preferred_element_type=f32)


def dot_t(left, right):
    return lax.dot_general(left, right, (((1,), (1,)), ((), ())), preferred_element_type=f32)


def split(values):
    rest = values - values.astype(bf16).astype(f32)
    return jnp.concatenate([values, rest], axis=0).astype(bf16)


def joined(terms):
    half = terms.shape[0] // 2
    return terms[:half] + terms[half:]


def one_hot(rows, index):
    at = lax.broadcasted_iota(jnp.int32, (rows, index.shape[1]), 0)
    return jnp.where(at == index, 1.0, 0.0).astype(bf16)


def column(row):
    size = row.shape[1]
    at = lax.broadcasted_iota(jnp.int32, (size, size), 0)
    across = lax.broadcasted_iota(jnp.int32, (size, size), 1)
    return jnp.sum(jnp.where(at == across, row, 0.0), axis=1, keepdims=True)


def each(count, body):
    if count <= 16:
        for step in range(count):
            body(step)
    else:
        pl.loop(0, count)(body)


def total_of(count, shape, term):
    total = jnp.zeros(shape, f32)
    if count <= 16:
        for step in range(count):
            total = total + term(step)
        return total
    return lax.fori_loop(0, count, lambda step, total: total + term(step), total)


def span(start, size):
    if isinstance(start, int):
        return pl.ds(start * size, size)
    return pl.ds(pl.multiple_of(start * size, size), size)


def rows_of(start, size):
    return pl.ds(start * size, size)


def rows_stacked(tiles):
    at = lax.broadcasted_iota(jnp.int32, (SUBLANES, LANES), 0)
    stacked = eight(tiles[0])
    for k in range(1, len(tiles)):
        stacked = jnp.where(at == k, eight(tiles[k]), stacked)
    return stacked


def tiles_of(row):
    return [row[:, k * LANES : (k + 1) * LANES] for k in range(row.shape[1] // LANES)]


def taken_from(tables, index):
    lane, tile = index & (LANES - 1), index >> (LANES - 1).bit_length()
    found = None
    for k, table in enumerate(tables):
        here = jnp.take_along_axis(eight(table), lane, axis=1, mode="promise_in_bounds")
        found = here if k == 0 else jnp.where(tile == k, here, found)
    return found


def look_up(table, index):
    count = index.shape[1] // LANES
    found = taken_from(tiles_of(table), rows_stacked(tiles_of(index)))
    return jnp.concatenate([found[k : k + 1] for k in range(count)], axis=1)


def walk(tables, order, rank):
    rows_count, _, cols_count = order.shape
    count = cols_count // LANES
    bits = (cols_count - 1).bit_length()
    at = lax.broadcasted_iota(jnp.int32, (SUBLANES, LANES), 0)
    place = (at % count) * LANES + lax.broadcasted_iota(jnp.int32, (SUBLANES, LANES), 1)

    first = tables[0:1, 0:cols_count]
    ahead = jnp.where(at < count, rows_stacked(tiles_of(first)), 0)
    behind = rows_stacked(tiles_of(tables[1:2, 0:cols_count]))
    behind = jnp.where(place == 0, 0, behind)
    steps = jnp.where(place == 0, 0, 1)
    for bit in range(bits):
        far = taken_from([ahead[k : k + 1] for k in range(count)], ahead)
        both = (steps << bits) + behind
        back = taken_from([both[k : k + 1] for k in range(count)], behind)
        ahead = jnp.where((at >= count) & ((place >> bit) & 1 == 0), ahead, far)
        steps = steps + (back >> bits)
        behind = back & ((1 << bits) - 1)
    order[0] = jnp.concatenate([ahead[count + k : count + k + 1] for k in range(count)], axis=1)
    rank[0] = jnp.concatenate([steps[k : k + 1] for k in range(count)], axis=1)

    def north(row):
        return tables[2:3, span(row, cols_count)] - (row + 1) * cols_count

    def south(row):
        return tables[3:4, span(row, cols_count)] - (row - 1) * cols_count

    if rows_count <= 16:
        there, back = north(0), south(1)
        for row in range(1, rows_count):
            order[row] = look_up(there, order[0])
            rank[row] = look_up(rank[0], back)
            if row + 1 < rows_count:
                there, back = look_up(north(row), there), look_up(back, south(row + 1))
    else:

        def next_row(row):
            order[row + 1] = look_up(north(row), order[row])
            rank[row + 1] = look_up(rank[row], south(row + 1))

        each(rows_count - 1, next_row)


def grid_places(listed, rank):
    rows_count, _, cols_count = rank.shape
    tiles = tiles_of(listed)
    found = []
    for tile in tiles:
        index = eight(tile)

        def column_in(row, best):
            first = row * cols_count
            within = jnp.clip(index - first, 0, cols_count - 1)
            here = taken_from(tiles_of(rank[row]), within)
            return jnp.where(index - first == within, here + first, best)

        best = jnp.zeros((SUBLANES, LANES), jnp.int32)
        if rows_count <= 16:
            for row in range(rows_count):
                best = column_in(row, best)
        else:
            best = lax.fori_loop(0, rows_count, column_in, best)
        found.append(best[0:1])
    return jnp.concatenate(found, axis=1)


def down(row):
    wide = jnp.broadcast_to(row.astype(f32), (LANES, row.shape[1]))
    return jnp.transpose(wide).astype(jnp.int32)


def one_hot_across(index, first, count):
    lane = lax.broadcasted_iota(jnp.int32, index.shape, 1)
    tiles = [
        jnp.where(lane + (first + tile * LANES) == index, 1.0, 0.0).astype(bf16)
        for tile in range(count // LANES)
    ]
    return jnp.concatenate(tiles, axis=1)


def eight(row):
    return jnp.broadcast_to(row, (SUBLANES, row.shape[1]))


def face_at(cell, slope, onward, curve, coefs):
    _, lean, bend = coefs
    estimate = cell + lean * slope - bend * curve
    return jnp.clip(estimate, jnp.minimum(cell, onward), jnp.maximum(cell, onward))


def moved_east(cell, coefs):
    size = cell.shape[1]
    rate = coefs[0]
    onward = pltpu.roll(cell, size - 1, 1)
    slope = onward - cell
    bent = slope - pltpu.roll(slope, 1, 1)
    curve = jnp.where(rate >= 0.0, bent, pltpu.roll(bent, size - 1, 1))
    face = face_at(cell, slope, onward, curve, coefs)
    return cell - rate * (face - pltpu.roll(face, 1, 1))


def advance(field, moved, faces, sea, east, north):
    rows_count, bins, cols_count = field.shape
    if rows_count <= 16:
        for first in range(0, bins, SUBLANES):
            here = slice(first, first + SUBLANES)
            to_east, to_north = ([x[here] for x in coefs] for coefs in (east, north))
            cells = [moved_east(field[row, here], to_east) for row in range(rows_count)]
            onward = cells[1:] + cells[:1]
            slopes = [b - a for a, b in zip(cells, onward)]
            bents = [slopes[row] - slopes[row - 1] for row in range(rows_count)]
            forward = to_north[0] >= 0.0
            over = [
                face_at(
                    cells[row],
                    slopes[row],
                    onward[row],
                    jnp.where(forward, bents[row], bents[(row + 1) % rows_count]),
                    to_north,
                )
                for row in range(rows_count)
            ]
            for row in range(rows_count):
                change = to_north[0] * (over[row] - over[row - 1])
                field[row, here] = (cells[row] - change) * sea[row]
        return

    def to_east(row):
        moved[row] = moved_east(field[row], east)

    def over_row(row):
        ahead, second, behind = ((row + k + rows_count) % rows_count for k in (1, 2, -1))
        cell, onward = moved[row], moved[ahead]
        slope = onward - cell
        curve = jnp.where(
            north[0] >= 0.0, slope - (cell - moved[behind]), (moved[second] - onward) - slope
        )
        faces[row] = face_at(cell, slope, onward, curve, north)

    def to_north(row):
        behind = (row - 1 + rows_count) % rows_count
        field[row] = (moved[row] - north[0] * (faces[row] - faces[behind])) * sea[row]

    for step in (to_east, over_row, to_north):
        each(rows_count, step)


def coefs_of(rates, which):
    return [rates[3 * which + k] for k in range(3)]


def landing(row, into, lists, cols_count):
    if into.shape[0] > 1:
        return into[row]
    return one_hot_across(down(lists[1:2]), row * cols_count, cols_count)


def count_kernel(steps_in, steps):
    steps[...] = jnp.broadcast_to(steps_in[...].astype(f32), steps.shape)


def prepare_kernel(
    spectra,
    tables,
    wet,
    send,
    recv,
    order,
    rank,
    base,
    into,
    sea,
    taken,
    lists,
):
    rows_count, bins, cols_count = base.shape
    listed = send.shape[1]
    walk(tables, order, rank)
    lists[0:1] = grid_places(send[...], rank)
    lists[1:2] = grid_places(recv[...], rank)
    recv_down = down(lists[1:2])

    def place(row):
        own = one_hot(cols_count, order[row])
        here = one_hot_across(recv_down, row * cols_count, cols_count)
        if into.shape[0] > 1:
            into[row] = here
        got = dot(jnp.ones((SUBLANES, listed), bf16), here)[0:1]
        taken[row] = got
        covered = look_up(wet[0:1, span(row, cols_count)], order[row]).astype(f32)
        sea[row] = covered
        values = joined(dot(split(spectra[:, span(row, cols_count)]), own))
        base[row] = values * (covered * (1.0 - got))

    each(rows_count, place)


def first_kernel(
    base,
    into,
    sea,
    lists,
    spectra_b,
    send_b,
    courant,
    steps,
    field,
    outgoing,
    rates,
    moved,
    faces,
):
    rows_count, bins, cols_count = base.shape
    listed = lists.shape[1]
    second = jnp.where(steps[0:1] > 1.0, 1.0, 0.0)
    for which in range(2):
        rate = column(courant[which : which + 1, :]) / steps[0:1]
        for k, value in enumerate((rate, rate * second)):
            at = 3 * (2 * k + which)
            rates[at] = jnp.broadcast_to(value, (bins, cols_count))
            rates[at + 1] = 0.5 - 0.5 * rates[at]
            rates[at + 2] = (1.0 - rates[at] * rates[at]) * (1.0 / 6.0)
    rates[12] = jnp.broadcast_to(second, (bins, cols_count))

    def sent(row):
        own = one_hot(cols_count, send_b[...] - row * cols_count)
        return dot(split(spectra_b[:, span(row, cols_count)]), own)

    incoming = total_of(rows_count, (2 * bins, listed), sent).astype(bf16)

    def take(row):
        field[row] = base[row] + joined(dot(incoming, landing(row, into, lists, cols_count)))

    each(rows_count, take)
    advance(field, moved, faces, sea, coefs_of(rates, 0), coefs_of(rates, 1))

    def sending(row):
        return dot(split(field[row]), one_hot(cols_count, lists[0:1] - row * cols_count))

    outgoing[...] = joined(total_of(rows_count, (2 * bins, listed), sending))


def picked(row, ranks, picks, sea_count):
    if picks.shape[0] == ranks.shape[0]:
        return picks[row]
    return one_hot_across(down(ranks[row] - 1.0), 0, sea_count)


def places_kernel(rank, sea, coupling, growth, dissipation, ranks, picks, place, weights, rates):
    rows_count, _, cols_count = rank.shape
    sea_count = picks.shape[2]
    at = lax.broadcasted_iota(jnp.int32, (cols_count, cols_count), 0)
    across = lax.broadcasted_iota(jnp.int32, (cols_count, cols_count), 1)
    upper = jnp.where(at <= across, 1.0, 0.0).astype(bf16)

    def number(row, before):
        here = sea[row]
        number_of = dot(eight(here).astype(bf16), upper)[0:1] + before
        number_of = jnp.where(here > 0.0, number_of, 0.0)
        ranks[row] = number_of
        if picks.shape[0] == rows_count:
            picks[row] = one_hot_across(down(number_of - 1.0), 0, sea_count)
        place[0:1, span(row, cols_count)] = look_up(number_of.astype(jnp.int32), rank[row])
        return before + jnp.sum(here, axis=1, keepdims=True)

    before = jnp.zeros((1, 1), f32)
    if rows_count <= 16:
        for row in range(rows_count):
            before = number(row, before)
    else:
        lax.fori_loop(0, rows_count, number, before)
    weights[...] = jnp.transpose(coupling[...])
    rates[0:1] = growth[...]
    rates[1:2] = dissipation[...]


def second_kernel(
    share,
    field_in,
    incoming,
    into,
    lists,
    taken,
    sea,
    rates,
    ranks,
    picks,
    order,
    wind,
    pieces,
    blown,
    field,
    moved,
    faces,
    columns,
):
    rows_count, bins, cols_count = field.shape
    tiles, _, _ = columns.shape
    sea_count = tiles * LANES
    terms = split(incoming[...])

    def take(row):
        got = joined(dot(terms, landing(row, into, lists, cols_count)))
        field[row] = jnp.where(taken[row] * rates[12, 0:1] > 0.5, got, field_in[row])

    each(rows_count, take)
    advance(field, moved, faces, sea, coefs_of(rates, 2), coefs_of(rates, 3))

    def at_sea(row):
        by_grid = look_up(wind[0:1, span(row, cols_count)], order[row])
        terms = jnp.concatenate([split(field[row]), split(eight(by_grid))], axis=0)
        return dot(terms, picked(row, ranks, picks, sea_count))

    total = total_of(rows_count, (2 * bins + 2 * SUBLANES, sea_count), at_sea)
    blown[...] = joined(total[2 * bins :])
    total = joined(total[: 2 * bins])
    for tile in range(tiles):
        columns[tile] = total[:, tile * LANES : (tile + 1) * LANES]
    groups = LANES // share
    block = pieces.shape[0] // (tiles * groups)
    lane_group = lax.broadcasted_iota(jnp.int32, (block, LANES), 1) // share

    def fold(tile):
        parts = [columns[tile, pl.ds(q, block, stride=groups)] for q in range(groups)]
        for j in range(groups):
            piece = parts[j]
            for q in range(groups):
                if q != j:
                    part = pltpu.roll(parts[q], ((q - j) % groups) * share, 1)
                    piece = jnp.where(lane_group == q, part, piece)
            pieces[rows_of(tile * groups + j, block)] = piece

    each(tiles, fold)


def integrate_kernel(share, pieces, weights, rates, blown, out, values, parts):
    size = weights.shape[0]
    devices = blown.shape[1] // share
    groups = LANES // share
    block = pieces.shape[0] // devices
    bins = size // devices
    even = bins == groups * block

    def bins_of(device, q):
        return pl.ds(device * bins + q, block, stride=groups)

    def unfold(device):
        for q in range(groups):
            values[bins_of(device, q)] = pieces[rows_of(device, block)]

    if even:
        for q in range(groups):
            values[pl.ds(q, devices * block, stride=groups)] = pieces[...]
    else:
        pl.loop(0, devices)(unfold)
    turned = jnp.transpose(values[0:size])
    group = lax.broadcasted_iota(jnp.int32, (share, size), 1) % bins % groups
    now = turned[0:share]
    for q in range(1, groups):
        now = jnp.where(group == q, turned[q * share : (q + 1) * share], now)
    mine = pltpu.roll(blown[...], blown.shape[1] - lax.axis_index("bin") * share, 1)
    push = 1.0 + source_dt * (rates[0:1] * column(mine[0:1, 0:share]))
    drag = source_dt * rates[1:2]
    for repeat in range(SRC):
        linear = dot(now.astype(bf16), weights[...])
        mean = jnp.sum(now * now, axis=1, keepdims=True) * (1.0 / size)
        spread = jnp.sqrt(mean + tiny_add)
        now = (now * push + source_dt * linear) / (1.0 + drag * spread)
    values[0:size] = jnp.transpose(jnp.concatenate([now] * groups, axis=0))

    def fold(device):
        for q in range(groups):
            parts[q, rows_of(device, block)] = values[bins_of(device, q)]

    if not even:
        pl.loop(0, devices)(fold)
    lane_group = lax.broadcasted_iota(jnp.int32, out.shape, 1) // share
    result = None
    for q in range(groups):
        part = values[pl.ds(q, devices * block, stride=groups)] if even else parts[q]
        result = part if q == 0 else jnp.where(lane_group == q, part, result)
    out[...] = result


def spread_kernel(share, pieces, place, out, columns, done, left):
    tiles, bins, _ = columns.shape
    groups = LANES // share
    block = pieces.shape[0] // (tiles * groups)
    sea_count = tiles * LANES
    points = place.shape[1]
    rows_count, cols_count = grid_shape(points)
    lane_group = lax.broadcasted_iota(jnp.int32, (block, LANES), 1) // share
    if groups * block < bins:
        columns[:, groups * block :] = jnp.zeros((tiles, bins - groups * block, LANES), f32)

    def unfold(tile):
        parts = [pieces[rows_of(tile * groups + j, block)] for j in range(groups)]
        for q in range(groups):
            part = parts[q]
            for j in range(groups):
                if j != q:
                    other = pltpu.roll(parts[j], ((j - q) % groups) * share, 1)
                    part = jnp.where(lane_group == j, other, part)
            columns[tile, pl.ds(q, block, stride=groups)] = part

    each(tiles, unfold)
    terms = jnp.concatenate([split(columns[tile]) for tile in range(tiles)], axis=1)

    def scatter(row):
        here = span(row, cols_count)
        picks = one_hot(sea_count, place[0:1, here] - 1)
        done[:, here] = joined(dot(terms, picks))
        leave(row).start()

    def leave(row):
        here = span(row, cols_count)
        return pltpu.make_async_copy(done.at[:, here], out.at[:, here], left.at[row])

    each(rows_count, scatter)
    each(rows_count, lambda row: leave(row).wait())


def call(kernel, outs, scratch, operands, flops, apart=(), direct=False):
    held = sum(x.size * x.dtype.itemsize for x in operands)
    single = not isinstance(outs, list)
    shapes = [jax.ShapeDtypeStruct(*out) for out in ([outs] if single else outs)]
    held += sum(x.size * x.dtype.itemsize for x in shapes)
    own = sum(4 * math.prod(getattr(x, "shape", ())) for x in scratch)
    in_vmem = pl.BlockSpec(memory_space=pltpu.VMEM)
    places = [pl.BlockSpec(memory_space=pltpu.HBM) if x in apart else in_vmem for x in range(len(operands))]
    operands = [
        x if x.size == 1 else pltpu.with_memory_space_constraint(x, place.memory_space)
        for x, place in zip(operands, places)
    ]
    return pl.pallas_call(
        kernel,
        out_shape=shapes[0] if single else shapes,
        in_specs=places,
        out_specs=(pl.BlockSpec(memory_space=pltpu.HBM) if direct else in_vmem) if single else [in_vmem] * len(shapes),
        scratch_shapes=scratch,
        compiler_params=pltpu.CompilerParams(vmem_limit_bytes=min(60 << 20, (4 << 20) + held + own)),
        cost_estimate=pl.CostEstimate(flops=flops, bytes_accessed=held, transcendentals=0),
    )(*operands)


def local(
    spectra,
    courant,
    coupling,
    growth,
    dissipation,
    wind,
    neighbours,
    wet_mask,
    send_list,
    recv_list,
    substep_count,
):
    devices = lax.axis_size("bin")
    field = spectra[0]
    bins_here, points = field.shape
    rows_count, cols_count = grid_shape(points)
    sea_count = points // 2
    listed = send_list.shape[1]
    share = sea_count // devices
    groups = LANES // share
    block = -(-bins_here // groups)
    bins = up_to(groups * block, SUBLANES)
    size = devices * bins_here
    extra = bins - bins_here
    if extra:
        field = jnp.pad(field, ((0, extra), (0, 0)))
        courant = jnp.pad(courant, ((0, 0), (0, extra)))
    def transpose_all(pieces):
        pieces = pieces.reshape(devices, 1, block * LANES)
        pieces = lax.all_to_all(pieces, "bin", split_axis=0, concat_axis=0)
        return pieces.reshape(devices * block, LANES)

    def swap(array):
        return lax.ppermute(array, "nest", [(0, 1), (1, 0)])

    spectra_b, send_b = swap(field), swap(send_list)
    grid = (rows_count, bins, cols_count)
    row_of = (rows_count, 1, cols_count)
    steps = call(
        count_kernel, ((SUBLANES, cols_count), f32), [], (substep_count.reshape(1, 1),), 10**9
    )
    early = (
        field,
        neighbours[0],
        wet_mask,
        send_list,
        recv_list,
    )
    kept_into = rows_count if points * listed <= 1 << 22 else 1
    order, rank, base, into, sea, taken, lists = call(
        prepare_kernel,
        [
            (row_of, jnp.int32),
            (row_of, jnp.int32),
            (grid, f32),
            ((kept_into, listed, cols_count), bf16),
            (row_of, f32),
            (row_of, f32),
            ((2, listed), jnp.int32),
        ],
        [],
        early,
        10**9,
    )
    field, outgoing, rates = call(
        first_kernel,
        [(grid, f32), ((bins, listed), f32), ((13, bins, cols_count), f32)],
        [pltpu.VMEM(grid, f32)] * 2,
        (base, into, sea, lists, spectra_b, send_b, courant, steps),
        10**9,
    )
    incoming = swap(outgoing)
    kept = rows_count if points * sea_count <= 1 << 22 else 1
    ranks, picks, place, weights, source_rates = call(
        places_kernel,
        [
            (row_of, f32),
            ((kept, cols_count, sea_count), bf16),
            ((1, points), jnp.int32),
            ((size, size), bf16),
            ((2, size), f32),
        ],
        [],
        (rank, sea, coupling, growth.reshape(1, size), dissipation.reshape(1, size)),
        10**9,
    )
    tiles = sea_count // LANES
    pieces, blown = call(
        functools.partial(second_kernel, share),
        [((devices * block, LANES), f32), ((SUBLANES, sea_count), f32)],
        [*[pltpu.VMEM(grid, f32)] * 3, pltpu.VMEM((tiles, bins, LANES), f32)],
        (field, incoming, into, lists, taken, sea, rates, ranks, picks, order, wind),
        10**9,
    )
    pieces = transpose_all(pieces)
    pieces = call(
        functools.partial(integrate_kernel, share),
        ((devices * block, LANES), f32),
        [
            pltpu.VMEM((size + up_to(groups * block, SUBLANES), LANES), f32),
            pltpu.VMEM((groups, devices * block, LANES), f32),
        ],
        (pieces, weights, source_rates, blown),
        10**9,
    )
    pieces = transpose_all(pieces)
    result = call(
        functools.partial(spread_kernel, share),
        ((bins, points), f32),
        [
            pltpu.VMEM((tiles, bins, LANES), f32),
            pltpu.VMEM((bins, points), f32),
            pltpu.SemaphoreType.DMA((rows_count,)),
        ],
        (pieces, place),
        10**8,
        direct=True,
    )
    return result[None, :bins_here]


def solution(mesh):
    in_specs = (
        P("nest", "bin", None),
        P(None, "bin"),
        P(),
        P(),
        P(),
        P("nest", None),
        P("nest", None, None),
        P("nest", None),
        P("nest", None),
        P("nest", None),
        P("nest"),
    )
    out_specs = P("nest", "bin", None)
    return jax.shard_map(local, mesh=mesh, in_specs=in_specs, out_specs=out_specs, check_vma=False)
```

```python
import functools
import math

import jax
import jax.numpy as jnp
from jax import lax
from jax.experimental import pallas as pl
from jax.experimental.pallas import tpu as pltpu
from jax.sharding import PartitionSpec as P

SUBSTEPS = 2
SRC = 5
LANES = 128
SUBLANES = 8

source_dt = 0.25
tiny_add = 1e-06
f32 = jnp.float32
bf16 = jnp.bfloat16


def up_to(value, unit):
    return -(-value // unit) * unit


def grid_shape(points):
    cols_count = min(256, points // 4)
    return points // cols_count, cols_count


def dot(left, right):
    return jnp.dot(left, right, preferred_element_type=f32)


def dot_t(left, right):
    return lax.dot_general(left, right, (((1,), (1,)), ((), ())), preferred_element_type=f32)


def split(values):
    rest = values - values.astype(bf16).astype(f32)
    return jnp.concatenate([values, rest], axis=0).astype(bf16)


def joined(terms):
    half = terms.shape[0] // 2
    return terms[:half] + terms[half:]


def one_hot(rows, index):
    at = lax.broadcasted_iota(jnp.int32, (rows, index.shape[1]), 0)
    return jnp.where(at == index, 1.0, 0.0).astype(bf16)


def column(row):
    size = row.shape[1]
    at = lax.broadcasted_iota(jnp.int32, (size, size), 0)
    across = lax.broadcasted_iota(jnp.int32, (size, size), 1)
    return jnp.sum(jnp.where(at == across, row, 0.0), axis=1, keepdims=True)


def each(count, body):
    if count <= 16:
        for step in range(count):
            body(step)
    else:
        pl.loop(0, count)(body)


def total_of(count, shape, term):
    total = jnp.zeros(shape, f32)
    if count <= 16:
        for step in range(count):
            total = total + term(step)
        return total
    return lax.fori_loop(0, count, lambda step, total: total + term(step), total)


def span(start, size):
    if isinstance(start, int):
        return pl.ds(start * size, size)
    return pl.ds(pl.multiple_of(start * size, size), size)


def rows_of(start, size):
    return pl.ds(start * size, size)


def rows_stacked(tiles):
    at = lax.broadcasted_iota(jnp.int32, (SUBLANES, LANES), 0)
    stacked = eight(tiles[0])
    for k in range(1, len(tiles)):
        stacked = jnp.where(at == k, eight(tiles[k]), stacked)
    return stacked


def tiles_of(row):
    return [row[:, k * LANES : (k + 1) * LANES] for k in range(row.shape[1] // LANES)]


def taken_from(tables, index):
    lane, tile = index & (LANES - 1), index >> (LANES - 1).bit_length()
    found = None
    for k, table in enumerate(tables):
        here = jnp.take_along_axis(eight(table), lane, axis=1, mode="promise_in_bounds")
        found = here if k == 0 else jnp.where(tile == k, here, found)
    return found


def look_up(table, index):
    count = index.shape[1] // LANES
    found = taken_from(tiles_of(table), rows_stacked(tiles_of(index)))
    return jnp.concatenate([found[k : k + 1] for k in range(count)], axis=1)


def walk(tables, order, rank):
    rows_count, _, cols_count = order.shape
    count = cols_count // LANES
    bits = (cols_count - 1).bit_length()
    at = lax.broadcasted_iota(jnp.int32, (SUBLANES, LANES), 0)
    place = (at % count) * LANES + lax.broadcasted_iota(jnp.int32, (SUBLANES, LANES), 1)

    first = tables[0:1, 0:cols_count]
    ahead = jnp.where(at < count, rows_stacked(tiles_of(first)), 0)
    behind = rows_stacked(tiles_of(tables[1:2, 0:cols_count]))
    behind = jnp.where(place == 0, 0, behind)
    steps = jnp.where(place == 0, 0, 1)
    for bit in range(bits):
        far = taken_from([ahead[k : k + 1] for k in range(count)], ahead)
        both = (steps << bits) + behind
        back = taken_from([both[k : k + 1] for k in range(count)], behind)
        ahead = jnp.where((at >= count) & ((place >> bit) & 1 == 0), ahead, far)
        steps = steps + (back >> bits)
        behind = back & ((1 << bits) - 1)
    order[0] = jnp.concatenate([ahead[count + k : count + k + 1] for k in range(count)], axis=1)
    rank[0] = jnp.concatenate([steps[k : k + 1] for k in range(count)], axis=1)

    def north(row):
        return tables[2:3, span(row, cols_count)] - (row + 1) * cols_count

    def south(row):
        return tables[3:4, span(row, cols_count)] - (row - 1) * cols_count

    if rows_count <= 16:
        there, back = north(0), south(1)
        for row in range(1, rows_count):
            order[row] = look_up(there, order[0])
            rank[row] = look_up(rank[0], back)
            if row + 1 < rows_count:
                there, back = look_up(north(row), there), look_up(back, south(row + 1))
    else:

        def next_row(row):
            order[row + 1] = look_up(north(row), order[row])
            rank[row + 1] = look_up(rank[row], south(row + 1))

        each(rows_count - 1, next_row)


def grid_places(listed, rank):
    rows_count, _, cols_count = rank.shape
    tiles = tiles_of(listed)
    found = []
    for tile in tiles:
        index = eight(tile)

        def column_in(row, best):
            first = row * cols_count
            within = jnp.clip(index - first, 0, cols_count - 1)
            here = taken_from(tiles_of(rank[row]), within)
            return jnp.where(index - first == within, here + first, best)

        best = jnp.zeros((SUBLANES, LANES), jnp.int32)
        if rows_count <= 16:
            for row in range(rows_count):
                best = column_in(row, best)
        else:
            best = lax.fori_loop(0, rows_count, column_in, best)
        found.append(best[0:1])
    return jnp.concatenate(found, axis=1)


def down(row):
    wide = jnp.broadcast_to(row.astype(f32), (LANES, row.shape[1]))
    return jnp.transpose(wide).astype(jnp.int32)


def one_hot_across(index, first, count):
    lane = lax.broadcasted_iota(jnp.int32, index.shape, 1)
    tiles = [
        jnp.where(lane + (first + tile * LANES) == index, 1.0, 0.0).astype(bf16)
        for tile in range(count // LANES)
    ]
    return jnp.concatenate(tiles, axis=1)


def eight(row):
    return jnp.broadcast_to(row, (SUBLANES, row.shape[1]))


def face_at(cell, slope, onward, curve, coefs):
    _, lean, bend = coefs
    estimate = cell + lean * slope - bend * curve
    return jnp.clip(estimate, jnp.minimum(cell, onward), jnp.maximum(cell, onward))


def moved_east(cell, coefs):
    size = cell.shape[1]
    rate = coefs[0]
    onward = pltpu.roll(cell, size - 1, 1)
    slope = onward - cell
    bent = slope - pltpu.roll(slope, 1, 1)
    curve = jnp.where(rate >= 0.0, bent, pltpu.roll(bent, size - 1, 1))
    face = face_at(cell, slope, onward, curve, coefs)
    return cell - rate * (face - pltpu.roll(face, 1, 1))


def advance(field, moved, faces, sea, east, north):
    rows_count, bins, cols_count = field.shape
    if rows_count <= 16:
        for first in range(0, bins, SUBLANES):
            here = slice(first, first + SUBLANES)
            to_east, to_north = ([x[here] for x in coefs] for coefs in (east, north))
            cells = [moved_east(field[row, here], to_east) for row in range(rows_count)]
            onward = cells[1:] + cells[:1]
            slopes = [b - a for a, b in zip(cells, onward)]
            bents = [slopes[row] - slopes[row - 1] for row in range(rows_count)]
            forward = to_north[0] >= 0.0
            over = [
                face_at(
                    cells[row],
                    slopes[row],
                    onward[row],
                    jnp.where(forward, bents[row], bents[(row + 1) % rows_count]),
                    to_north,
                )
                for row in range(rows_count)
            ]
            for row in range(rows_count):
                change = to_north[0] * (over[row] - over[row - 1])
                field[row, here] = (cells[row] - change) * sea[row]
        return

    def to_east(row):
        moved[row] = moved_east(field[row], east)

    def over_row(row):
        ahead, second, behind = ((row + k + rows_count) % rows_count for k in (1, 2, -1))
        cell, onward = moved[row], moved[ahead]
        slope = onward - cell
        curve = jnp.where(
            north[0] >= 0.0, slope - (cell - moved[behind]), (moved[second] - onward) - slope
        )
        faces[row] = face_at(cell, slope, onward, curve, north)

    def to_north(row):
        behind = (row - 1 + rows_count) % rows_count
        field[row] = (moved[row] - north[0] * (faces[row] - faces[behind])) * sea[row]

    for step in (to_east, over_row, to_north):
        each(rows_count, step)


def coefs_of(rates, which):
    return [rates[3 * which + k] for k in range(3)]


def landing(row, into, lists, cols_count):
    if into.shape[0] > 1:
        return into[row]
    return one_hot_across(down(lists[1:2]), row * cols_count, cols_count)


def count_kernel(steps_in, steps):
    steps[...] = jnp.broadcast_to(steps_in[...].astype(f32), steps.shape)


def prepare_kernel(
    spectra,
    tables,
    wet,
    send,
    recv,
    order,
    rank,
    base,
    into,
    sea,
    taken,
    lists,
):
    rows_count, bins, cols_count = base.shape
    listed = send.shape[1]
    walk(tables, order, rank)
    lists[0:1] = grid_places(send[...], rank)
    lists[1:2] = grid_places(recv[...], rank)
    recv_down = down(lists[1:2])

    def place(row):
        own = one_hot(cols_count, order[row])
        here = one_hot_across(recv_down, row * cols_count, cols_count)
        if into.shape[0] > 1:
            into[row] = here
        got = dot(jnp.ones((SUBLANES, listed), bf16), here)[0:1]
        taken[row] = got
        covered = look_up(wet[0:1, span(row, cols_count)], order[row]).astype(f32)
        sea[row] = covered
        values = joined(dot(split(spectra[:, span(row, cols_count)]), own))
        base[row] = values * (covered * (1.0 - got))

    each(rows_count, place)


def first_kernel(
    base,
    into,
    sea,
    lists,
    spectra_b,
    send_b,
    courant,
    steps,
    field,
    outgoing,
    rates,
    moved,
    faces,
):
    rows_count, bins, cols_count = base.shape
    listed = lists.shape[1]
    second = jnp.where(steps[0:1] > 1.0, 1.0, 0.0)
    for which in range(2):
        rate = column(courant[which : which + 1, :]) / steps[0:1]
        for k, value in enumerate((rate, rate * second)):
            at = 3 * (2 * k + which)
            rates[at] = jnp.broadcast_to(value, (bins, cols_count))
            rates[at + 1] = 0.5 - 0.5 * rates[at]
            rates[at + 2] = (1.0 - rates[at] * rates[at]) * (1.0 / 6.0)
    rates[12] = jnp.broadcast_to(second, (bins, cols_count))

    def sent(row):
        own = one_hot(cols_count, send_b[...] - row * cols_count)
        return dot(split(spectra_b[:, span(row, cols_count)]), own)

    incoming = total_of(rows_count, (2 * bins, listed), sent).astype(bf16)

    def take(row):
        field[row] = base[row] + joined(dot(incoming, landing(row, into, lists, cols_count)))

    each(rows_count, take)
    advance(field, moved, faces, sea, coefs_of(rates, 0), coefs_of(rates, 1))

    def sending(row):
        return dot(split(field[row]), one_hot(cols_count, lists[0:1] - row * cols_count))

    outgoing[...] = joined(total_of(rows_count, (2 * bins, listed), sending))


def picked(row, ranks, picks, sea_count):
    if picks.shape[0] == ranks.shape[0]:
        return picks[row]
    return one_hot_across(down(ranks[row] - 1.0), 0, sea_count)


def places_kernel(rank, sea, coupling, growth, dissipation, ranks, picks, place, weights, rates):
    rows_count, _, cols_count = rank.shape
    sea_count = picks.shape[2]
    at = lax.broadcasted_iota(jnp.int32, (cols_count, cols_count), 0)
    across = lax.broadcasted_iota(jnp.int32, (cols_count, cols_count), 1)
    upper = jnp.where(at <= across, 1.0, 0.0).astype(bf16)

    def number(row, before):
        here = sea[row]
        number_of = dot(eight(here).astype(bf16), upper)[0:1] + before
        number_of = jnp.where(here > 0.0, number_of, 0.0)
        ranks[row] = number_of
        if picks.shape[0] == rows_count:
            picks[row] = one_hot_across(down(number_of - 1.0), 0, sea_count)
        place[0:1, span(row, cols_count)] = look_up(number_of.astype(jnp.int32), rank[row])
        return before + jnp.sum(here, axis=1, keepdims=True)

    before = jnp.zeros((1, 1), f32)
    if rows_count <= 16:
        for row in range(rows_count):
            before = number(row, before)
    else:
        lax.fori_loop(0, rows_count, number, before)
    turned = min(2 * cols_count, weights.shape[0])
    unit = jnp.where(at == across, 1.0, 0.0).astype(bf16)
    for first in range(0, turned, cols_count):
        here = slice(first, first + cols_count)
        weights[here] = dot_t(unit, coupling[:, here]).astype(bf16)
    weights[turned:] = jnp.transpose(coupling[:, turned:])
    rates[0:1] = growth[...]
    rates[1:2] = dissipation[...]


def second_kernel(
    share,
    field_in,
    incoming,
    into,
    lists,
    taken,
    sea,
    rates,
    ranks,
    picks,
    order,
    wind,
    pieces,
    blown,
    field,
    moved,
    faces,
    columns,
):
    rows_count, bins, cols_count = field.shape
    tiles, _, _ = columns.shape
    sea_count = tiles * LANES
    terms = split(incoming[...])

    def take(row):
        got = joined(dot(terms, landing(row, into, lists, cols_count)))
        field[row] = jnp.where(taken[row] * rates[12, 0:1] > 0.5, got, field_in[row])

    each(rows_count, take)
    advance(field, moved, faces, sea, coefs_of(rates, 2), coefs_of(rates, 3))

    def at_sea(row):
        by_grid = look_up(wind[0:1, span(row, cols_count)], order[row])
        terms = jnp.concatenate([split(field[row]), split(eight(by_grid))], axis=0)
        return dot(terms, picked(row, ranks, picks, sea_count))

    total = total_of(rows_count, (2 * bins + 2 * SUBLANES, sea_count), at_sea)
    blown[...] = joined(total[2 * bins :])
    total = joined(total[: 2 * bins])
    for tile in range(tiles):
        columns[tile] = total[:, tile * LANES : (tile + 1) * LANES]
    groups = LANES // share
    block = pieces.shape[0] // (tiles * groups)
    lane_group = lax.broadcasted_iota(jnp.int32, (block, LANES), 1) // share

    def fold(tile):
        parts = [columns[tile, pl.ds(q, block, stride=groups)] for q in range(groups)]
        for j in range(groups):
            piece = parts[j]
            for q in range(groups):
                if q != j:
                    part = pltpu.roll(parts[q], ((q - j) % groups) * share, 1)
                    piece = jnp.where(lane_group == q, part, piece)
            pieces[rows_of(tile * groups + j, block)] = piece

    each(tiles, fold)


def integrate_kernel(share, pieces, weights, rates, blown, out, values, parts):
    size = weights.shape[0]
    devices = blown.shape[1] // share
    groups = LANES // share
    block = pieces.shape[0] // devices
    bins = size // devices
    even = bins == groups * block

    def bins_of(device, q):
        return pl.ds(device * bins + q, block, stride=groups)

    def unfold(device):
        for q in range(groups):
            values[bins_of(device, q)] = pieces[rows_of(device, block)]

    if even:
        for q in range(groups):
            values[pl.ds(q, devices * block, stride=groups)] = pieces[...]
    else:
        pl.loop(0, devices)(unfold)
    turned = jnp.transpose(values[0:size])
    group = lax.broadcasted_iota(jnp.int32, (share, size), 1) % bins % groups
    now = turned[0:share]
    for q in range(1, groups):
        now = jnp.where(group == q, turned[q * share : (q + 1) * share], now)
    mine = pltpu.roll(blown[...], blown.shape[1] - lax.axis_index("bin") * share, 1)
    push = 1.0 + source_dt * (rates[0:1] * column(mine[0:1, 0:share]))
    drag = source_dt * rates[1:2]
    for repeat in range(SRC):
        linear = dot(now.astype(bf16), weights[...])
        mean = jnp.sum(now * now, axis=1, keepdims=True) * (1.0 / size)
        spread = jnp.sqrt(mean + tiny_add)
        now = (now * push + source_dt * linear) / (1.0 + drag * spread)
    values[0:size] = jnp.transpose(jnp.concatenate([now] * groups, axis=0))

    def fold(device):
        for q in range(groups):
            parts[q, rows_of(device, block)] = values[bins_of(device, q)]

    if not even:
        pl.loop(0, devices)(fold)
    lane_group = lax.broadcasted_iota(jnp.int32, out.shape, 1) // share
    result = None
    for q in range(groups):
        part = values[pl.ds(q, devices * block, stride=groups)] if even else parts[q]
        result = part if q == 0 else jnp.where(lane_group == q, part, result)
    out[...] = result


def spread_kernel(share, pieces, place, out, columns, done, left):
    tiles, bins, _ = columns.shape
    groups = LANES // share
    block = pieces.shape[0] // (tiles * groups)
    sea_count = tiles * LANES
    points = place.shape[1]
    rows_count, cols_count = grid_shape(points)
    lane_group = lax.broadcasted_iota(jnp.int32, (block, LANES), 1) // share
    if groups * block < bins:
        columns[:, groups * block :] = jnp.zeros((tiles, bins - groups * block, LANES), f32)

    def unfold(tile):
        parts = [pieces[rows_of(tile * groups + j, block)] for j in range(groups)]
        for q in range(groups):
            part = parts[q]
            for j in range(groups):
                if j != q:
                    other = pltpu.roll(parts[j], ((j - q) % groups) * share, 1)
                    part = jnp.where(lane_group == j, other, part)
            columns[tile, pl.ds(q, block, stride=groups)] = part

    each(tiles, unfold)
    terms = jnp.concatenate([split(columns[tile]) for tile in range(tiles)], axis=1)

    def scatter(row):
        here = span(row, cols_count)
        picks = one_hot(sea_count, place[0:1, here] - 1)
        done[:, here] = joined(dot(terms, picks))
        leave(row).start()

    def leave(row):
        here = span(row, cols_count)
        return pltpu.make_async_copy(done.at[:, here], out.at[:, here], left.at[row])

    each(rows_count, scatter)
    each(rows_count, lambda row: leave(row).wait())


def call(kernel, outs, scratch, operands, flops, apart=(), direct=False):
    held = sum(x.size * x.dtype.itemsize for x in operands)
    single = not isinstance(outs, list)
    shapes = [jax.ShapeDtypeStruct(*out) for out in ([outs] if single else outs)]
    held += sum(x.size * x.dtype.itemsize for x in shapes)
    own = sum(4 * math.prod(getattr(x, "shape", ())) for x in scratch)
    in_vmem = pl.BlockSpec(memory_space=pltpu.VMEM)
    places = [pl.BlockSpec(memory_space=pltpu.HBM) if x in apart else in_vmem for x in range(len(operands))]
    operands = [
        x if x.size == 1 else pltpu.with_memory_space_constraint(x, place.memory_space)
        for x, place in zip(operands, places)
    ]
    return pl.pallas_call(
        kernel,
        out_shape=shapes[0] if single else shapes,
        in_specs=places,
        out_specs=(pl.BlockSpec(memory_space=pltpu.HBM) if direct else in_vmem) if single else [in_vmem] * len(shapes),
        scratch_shapes=scratch,
        compiler_params=pltpu.CompilerParams(vmem_limit_bytes=min(60 << 20, (4 << 20) + held + own)),
        cost_estimate=pl.CostEstimate(flops=flops, bytes_accessed=held, transcendentals=0),
    )(*operands)


def local(
    spectra,
    courant,
    coupling,
    growth,
    dissipation,
    wind,
    neighbours,
    wet_mask,
    send_list,
    recv_list,
    substep_count,
):
    devices = lax.axis_size("bin")
    field = spectra[0]
    bins_here, points = field.shape
    rows_count, cols_count = grid_shape(points)
    sea_count = points // 2
    listed = send_list.shape[1]
    share = sea_count // devices
    groups = LANES // share
    block = -(-bins_here // groups)
    bins = up_to(groups * block, SUBLANES)
    size = devices * bins_here
    extra = bins - bins_here
    if extra:
        field = jnp.pad(field, ((0, extra), (0, 0)))
        courant = jnp.pad(courant, ((0, 0), (0, extra)))
    def transpose_all(pieces):
        pieces = pieces.reshape(devices, 1, block * LANES)
        pieces = lax.all_to_all(pieces, "bin", split_axis=0, concat_axis=0)
        return pieces.reshape(devices * block, LANES)

    def swap(array):
        return lax.ppermute(array, "nest", [(0, 1), (1, 0)])

    spectra_b, send_b = swap(field), swap(send_list)
    grid = (rows_count, bins, cols_count)
    row_of = (rows_count, 1, cols_count)
    steps = call(
        count_kernel, ((SUBLANES, cols_count), f32), [], (substep_count.reshape(1, 1),), 10**9
    )
    early = (
        field,
        neighbours[0],
        wet_mask,
        send_list,
        recv_list,
    )
    kept_into = rows_count if points * listed <= 1 << 22 else 1
    order, rank, base, into, sea, taken, lists = call(
        prepare_kernel,
        [
            (row_of, jnp.int32),
            (row_of, jnp.int32),
            (grid, f32),
            ((kept_into, listed, cols_count), bf16),
            (row_of, f32),
            (row_of, f32),
            ((2, listed), jnp.int32),
        ],
        [],
        early,
        10**9,
    )
    field, outgoing, rates = call(
        first_kernel,
        [(grid, f32), ((bins, listed), f32), ((13, bins, cols_count), f32)],
        [pltpu.VMEM(grid, f32)] * 2,
        (base, into, sea, lists, spectra_b, send_b, courant, steps),
        10**9,
    )
    incoming = swap(outgoing)
    kept = rows_count if points * sea_count <= 1 << 22 else 1
    ranks, picks, place, weights, source_rates = call(
        places_kernel,
        [
            (row_of, f32),
            ((kept, cols_count, sea_count), bf16),
            ((1, points), jnp.int32),
            ((size, size), bf16),
            ((2, size), f32),
        ],
        [],
        (rank, sea, coupling, growth.reshape(1, size), dissipation.reshape(1, size)),
        10**9,
    )
    tiles = sea_count // LANES
    pieces, blown = call(
        functools.partial(second_kernel, share),
        [((devices * block, LANES), f32), ((SUBLANES, sea_count), f32)],
        [*[pltpu.VMEM(grid, f32)] * 3, pltpu.VMEM((tiles, bins, LANES), f32)],
        (field, incoming, into, lists, taken, sea, rates, ranks, picks, order, wind),
        10**9,
    )
    pieces = transpose_all(pieces)
    pieces = call(
        functools.partial(integrate_kernel, share),
        ((devices * block, LANES), f32),
        [
            pltpu.VMEM((size + up_to(groups * block, SUBLANES), LANES), f32),
            pltpu.VMEM((groups, devices * block, LANES), f32),
        ],
        (pieces, weights, source_rates, blown),
        10**9,
    )
    pieces = transpose_all(pieces)
    result = call(
        functools.partial(spread_kernel, share),
        ((bins, points), f32),
        [
            pltpu.VMEM((tiles, bins, LANES), f32),
            pltpu.VMEM((bins, points), f32),
            pltpu.SemaphoreType.DMA((rows_count,)),
        ],
        (pieces, place),
        10**8,
        direct=True,
    )
    return result[None, :bins_here]


def solution(mesh):
    in_specs = (
        P("nest", "bin", None),
        P(None, "bin"),
        P(),
        P(),
        P(),
        P("nest", None),
        P("nest", None, None),
        P("nest", None),
        P("nest", None),
        P("nest", None),
        P("nest"),
    )
    out_specs = P("nest", "bin", None)
    return jax.shard_map(local, mesh=mesh, in_specs=in_specs, out_specs=out_specs, check_vma=False)
```

```python
import functools
import math

import jax
import jax.numpy as jnp
from jax import lax
from jax.experimental import pallas as pl
from jax.experimental.pallas import tpu as pltpu
from jax.sharding import PartitionSpec as P

SUBSTEPS = 2
SRC = 5
LANES = 128
SUBLANES = 8
CHUNK = 640

source_dt = 0.25
tiny_add = 1e-06
f32 = jnp.float32
bf16 = jnp.bfloat16


def up_to(value, unit):
    return -(-value // unit) * unit


def grid_shape(points):
    cols_count = min(256, points // 4)
    return points // cols_count, cols_count


def dot(left, right):
    return jnp.dot(left, right, preferred_element_type=f32)


def dot_t(left, right):
    return lax.dot_general(left, right, (((1,), (1,)), ((), ())), preferred_element_type=f32)


def split(values):
    rest = values - values.astype(bf16).astype(f32)
    return jnp.concatenate([values, rest], axis=0).astype(bf16)


def joined(terms):
    half = terms.shape[0] // 2
    return terms[:half] + terms[half:]


def one_hot(rows, index):
    at = lax.broadcasted_iota(jnp.int32, (rows, index.shape[1]), 0)
    return jnp.where(at == index, 1.0, 0.0).astype(bf16)


def column(row):
    size = row.shape[1]
    at = lax.broadcasted_iota(jnp.int32, (size, size), 0)
    across = lax.broadcasted_iota(jnp.int32, (size, size), 1)
    return jnp.sum(jnp.where(at == across, row, 0.0), axis=1, keepdims=True)


def each(count, body):
    if count <= 16:
        for step in range(count):
            body(step)
    else:
        pl.loop(0, count)(body)


def total_of(count, shape, term):
    total = jnp.zeros(shape, f32)
    if count <= 16:
        for step in range(count):
            total = total + term(step)
        return total
    return lax.fori_loop(0, count, lambda step, total: total + term(step), total)


def span(start, size):
    if isinstance(start, int):
        return pl.ds(start * size, size)
    return pl.ds(pl.multiple_of(start * size, size), size)


def rows_of(start, size):
    return pl.ds(start * size, size)


def rows_stacked(tiles):
    at = lax.broadcasted_iota(jnp.int32, (SUBLANES, LANES), 0)
    stacked = eight(tiles[0])
    for k in range(1, len(tiles)):
        stacked = jnp.where(at == k, eight(tiles[k]), stacked)
    return stacked


def tiles_of(row):
    return [row[:, k * LANES : (k + 1) * LANES] for k in range(row.shape[1] // LANES)]


def taken_from(tables, index):
    lane, tile = index & (LANES - 1), index >> (LANES - 1).bit_length()
    found = None
    for k, table in enumerate(tables):
        here = jnp.take_along_axis(eight(table), lane, axis=1, mode="promise_in_bounds")
        found = here if k == 0 else jnp.where(tile == k, here, found)
    return found


def look_up(table, index):
    count = index.shape[1] // LANES
    found = taken_from(tiles_of(table), rows_stacked(tiles_of(index)))
    return jnp.concatenate([found[k : k + 1] for k in range(count)], axis=1)


def walk(tables, order, rank):
    rows_count, _, cols_count = order.shape
    count = cols_count // LANES
    bits = (cols_count - 1).bit_length()
    at = lax.broadcasted_iota(jnp.int32, (SUBLANES, LANES), 0)
    lane = lax.broadcasted_iota(jnp.int32, (SUBLANES, LANES), 1)
    point = (at % count) * LANES + lane
    column_at = lane * count + at % count

    first = tables[0:1, 0:cols_count]
    ahead = jnp.where(at < count, rows_stacked(tiles_of(first)), 0)
    behind = rows_stacked(tiles_of(tables[1:2, 0:cols_count]))
    behind = jnp.where(point == 0, 0, behind)
    steps = jnp.where(point == 0, 0, 1)
    for bit in range(bits):
        far = taken_from([ahead[k : k + 1] for k in range(count)], ahead)
        both = (steps << bits) + behind
        back = taken_from([both[k : k + 1] for k in range(count)], behind)
        ahead = jnp.where((at >= count) & ((column_at >> bit) & 1 == 0), ahead, far)
        steps = steps + (back >> bits)
        behind = back & ((1 << bits) - 1)
    order[0] = jnp.concatenate([ahead[count + k : count + k + 1] for k in range(count)], axis=1)
    steps = steps % count * LANES + steps // count
    rank[0] = jnp.concatenate([steps[k : k + 1] for k in range(count)], axis=1)

    def north(row):
        return tables[2:3, span(row, cols_count)] - (row + 1) * cols_count

    def south(row):
        return tables[3:4, span(row, cols_count)] - (row - 1) * cols_count

    if rows_count <= 16:
        there, back = north(0), south(1)
        for row in range(1, rows_count):
            order[row] = look_up(there, order[0])
            rank[row] = look_up(rank[0], back)
            if row + 1 < rows_count:
                there, back = look_up(north(row), there), look_up(back, south(row + 1))
    else:

        def next_row(row):
            order[row + 1] = look_up(north(row), order[row])
            rank[row + 1] = look_up(rank[row], south(row + 1))

        each(rows_count - 1, next_row)


def grid_places(listed, rank):
    rows_count, _, cols_count = rank.shape
    tiles = tiles_of(listed)
    found = []
    for tile in tiles:
        index = eight(tile)

        def column_in(row, best):
            first = row * cols_count
            within = jnp.clip(index - first, 0, cols_count - 1)
            here = taken_from(tiles_of(rank[row]), within)
            return jnp.where(index - first == within, here + first, best)

        best = jnp.zeros((SUBLANES, LANES), jnp.int32)
        if rows_count <= 16:
            for row in range(rows_count):
                best = column_in(row, best)
        else:
            best = lax.fori_loop(0, rows_count, column_in, best)
        found.append(best[0:1])
    return jnp.concatenate(found, axis=1)


def down(row):
    wide = jnp.broadcast_to(row.astype(f32), (LANES, row.shape[1]))
    return jnp.transpose(wide).astype(jnp.int32)


def one_hot_across(index, first, count):
    lane = lax.broadcasted_iota(jnp.int32, index.shape, 1)
    tiles = [
        jnp.where(lane + (first + tile * LANES) == index, 1.0, 0.0).astype(bf16)
        for tile in range(count // LANES)
    ]
    return jnp.concatenate(tiles, axis=1)


def eight(row):
    return jnp.broadcast_to(row, (SUBLANES, row.shape[1]))


def face_at(cell, onward, slope, other, coefs):
    _, near, far = coefs
    estimate = cell + near * slope + far * other
    return jnp.clip(estimate, jnp.minimum(cell, onward), jnp.maximum(cell, onward))


def ahead(tiles):
    return tiles[1:] + [pltpu.roll(tiles[0], LANES - 1, 1)]


def behind(tiles):
    return [pltpu.roll(tiles[-1], 1, 1)] + tiles[:-1]


def moved_east(cells, coefs):
    rate = coefs[0]
    onward = ahead(cells)
    slopes = [b - a for a, b in zip(cells, onward)]
    others = [jnp.where(rate >= 0.0, a, b) for a, b in zip(behind(slopes), ahead(slopes))]
    faces = [face_at(*values, coefs) for values in zip(cells, onward, slopes, others)]
    return [a - rate * (b - c) for a, b, c in zip(cells, faces, behind(faces))]


def advance(field, moved, faces, sea, east, north):
    rows_count, bins, cols_count = field.shape
    if rows_count <= 16:
        for first in range(0, bins, SUBLANES):
            here = slice(first, first + SUBLANES)
            to_east, to_north = ([x[here, :LANES] for x in coefs] for coefs in (east, north))
            forward = to_north[0] >= 0.0
            rows = [moved_east(tiles_of(field[row, here]), to_east) for row in range(rows_count)]
            for k in range(cols_count // LANES):
                cells = [tiles[k] for tiles in rows]
                onward = cells[1:] + cells[:1]
                slopes = [b - a for a, b in zip(cells, onward)]
                over = [
                    face_at(
                        cells[row],
                        onward[row],
                        slopes[row],
                        jnp.where(forward, slopes[row - 1], slopes[(row + 1) % rows_count]),
                        to_north,
                    )
                    for row in range(rows_count)
                ]
                there = slice(k * LANES, (k + 1) * LANES)
                for row in range(rows_count):
                    change = to_north[0] * (over[row] - over[row - 1])
                    field[row, here, there] = (cells[row] - change) * sea[row, :, there]
        return

    def to_east(row):
        tiles = moved_east(tiles_of(field[row]), [x[:, :LANES] for x in east])
        moved[row] = jnp.concatenate(tiles, axis=1)

    def over_row(row):
        first, second, last = (moved[(row + k + rows_count) % rows_count] for k in (1, 2, -1))
        cell = moved[row]
        other = jnp.where(north[0] >= 0.0, cell - last, second - first)
        faces[row] = face_at(cell, first, first - cell, other, north)

    def to_north(row):
        last = (row - 1 + rows_count) % rows_count
        field[row] = (moved[row] - north[0] * (faces[row] - faces[last])) * sea[row]

    for step in (to_east, over_row, to_north):
        each(rows_count, step)


def coefs_of(rates, which):
    return [rates[3 * which + k] for k in range(3)]


def landing(row, into, lists, cols_count):
    if into.shape[0] > 1:
        return into[row]
    return one_hot_across(down(lists[1:2]), row * cols_count, cols_count)


def count_kernel(steps_in, steps):
    steps[...] = jnp.broadcast_to(steps_in[...].astype(f32), steps.shape)


def prepare_kernel(
    spectra,
    tables,
    wet,
    send,
    recv,
    order,
    rank,
    base,
    into,
    sea,
    taken,
    lists,
):
    rows_count, bins, cols_count = base.shape
    listed = send.shape[1]
    walk(tables, order, rank)
    lists[0:1] = grid_places(send[...], rank)
    lists[1:2] = grid_places(recv[...], rank)
    recv_down = down(lists[1:2])

    def place(row):
        own = one_hot(cols_count, order[row])
        here = one_hot_across(recv_down, row * cols_count, cols_count)
        if into.shape[0] > 1:
            into[row] = here
        got = dot(jnp.ones((SUBLANES, listed), bf16), here)[0:1]
        taken[row] = got
        covered = look_up(wet[0:1, span(row, cols_count)], order[row]).astype(f32)
        sea[row] = covered
        values = joined(dot(split(spectra[:, span(row, cols_count)]), own))
        base[row] = values * (covered * (1.0 - got))

    each(rows_count, place)


def first_kernel(
    base,
    into,
    sea,
    lists,
    spectra_b,
    send_b,
    courant,
    steps,
    field,
    outgoing,
    rates,
    moved,
    faces,
):
    rows_count, bins, cols_count = base.shape
    listed = lists.shape[1]
    second = jnp.where(steps[0:1] > 1.0, 1.0, 0.0)
    for which in range(2):
        rate = column(courant[which : which + 1, :]) / steps[0:1]
        for k, value in enumerate((rate, rate * second)):
            at = 3 * (2 * k + which)
            rates[at] = jnp.broadcast_to(value, (bins, cols_count))
            bend = (1.0 - rates[at] * rates[at]) * (1.0 / 6.0)
            bend = jnp.where(rates[at] >= 0.0, bend, -bend)
            rates[at + 1] = 0.5 - 0.5 * rates[at] - bend
            rates[at + 2] = bend
    rates[12] = jnp.broadcast_to(second, (bins, cols_count))

    def sent(row):
        own = one_hot(cols_count, send_b[...] - row * cols_count)
        return dot(split(spectra_b[:, span(row, cols_count)]), own)

    incoming = total_of(rows_count, (2 * bins, listed), sent).astype(bf16)

    def take(row):
        field[row] = base[row] + joined(dot(incoming, landing(row, into, lists, cols_count)))

    each(rows_count, take)
    advance(field, moved, faces, sea, coefs_of(rates, 0), coefs_of(rates, 1))

    def sending(row):
        return dot(split(field[row]), one_hot(cols_count, lists[0:1] - row * cols_count))

    outgoing[...] = joined(total_of(rows_count, (2 * bins, listed), sending))


def picked(row, ranks, picks, sea_count):
    if picks.shape[0] == ranks.shape[0]:
        return picks[row]
    return one_hot_across(down(ranks[row] - 1.0), 0, sea_count)


def places_kernel(rank, sea, coupling, growth, dissipation, ranks, picks, place, weights, rates):
    rows_count, _, cols_count = rank.shape
    sea_count = picks.shape[2]
    at = lax.broadcasted_iota(jnp.int32, (cols_count, cols_count), 0)
    across = lax.broadcasted_iota(jnp.int32, (cols_count, cols_count), 1)
    upper = jnp.where(at <= across, 1.0, 0.0).astype(bf16)

    def number(row, before):
        here = sea[row]
        number_of = dot(eight(here).astype(bf16), upper)[0:1] + before
        number_of = jnp.where(here > 0.0, number_of, 0.0)
        ranks[row] = number_of
        if picks.shape[0] == rows_count:
            picks[row] = one_hot_across(down(number_of - 1.0), 0, sea_count)
        place[0:1, span(row, cols_count)] = look_up(number_of.astype(jnp.int32), rank[row])
        return before + jnp.sum(here, axis=1, keepdims=True)

    before = jnp.zeros((1, 1), f32)
    if rows_count <= 16:
        for row in range(rows_count):
            before = number(row, before)
    else:
        lax.fori_loop(0, rows_count, number, before)
    turned = min(2, weights.shape[0] // cols_count) * cols_count
    unit = jnp.where(at == across, 1.0, 0.0).astype(bf16)
    for first in range(0, turned, cols_count):
        here = slice(first, first + cols_count)
        weights[here] = dot_t(unit, coupling[:, here]).astype(bf16)
    weights[turned:] = jnp.transpose(coupling[:, turned:])
    rates[0:1] = growth[...]
    rates[1:2] = dissipation[...]


def second_kernel(
    share,
    field_in,
    incoming,
    into,
    lists,
    taken,
    sea,
    rates,
    ranks,
    picks,
    order,
    wind,
    pieces,
    blown,
    field,
    moved,
    faces,
    columns,
):
    rows_count, bins, cols_count = field.shape
    tiles, _, _ = columns.shape
    sea_count = tiles * LANES
    terms = split(incoming[...])

    def take(row):
        got = joined(dot(terms, landing(row, into, lists, cols_count)))
        field[row] = jnp.where(taken[row] * rates[12, 0:1] > 0.5, got, field_in[row])

    each(rows_count, take)
    advance(field, moved, faces, sea, coefs_of(rates, 2), coefs_of(rates, 3))

    def at_sea(row):
        by_grid = look_up(wind[0:1, span(row, cols_count)], order[row])
        terms = jnp.concatenate([split(field[row]), split(eight(by_grid))], axis=0)
        return dot(terms, picked(row, ranks, picks, sea_count))

    total = total_of(rows_count, (2 * bins + 2 * SUBLANES, sea_count), at_sea)
    blown[...] = joined(total[2 * bins :])
    total = joined(total[: 2 * bins])
    for tile in range(tiles):
        columns[tile] = total[:, tile * LANES : (tile + 1) * LANES]
    groups = LANES // share
    block = pieces.shape[0] // (tiles * groups)
    lane_group = lax.broadcasted_iota(jnp.int32, (block, LANES), 1) // share

    def fold(tile):
        parts = [columns[tile, pl.ds(q, block, stride=groups)] for q in range(groups)]
        for j in range(groups):
            piece = parts[j]
            for q in range(groups):
                if q != j:
                    part = pltpu.roll(parts[q], ((q - j) % groups) * share, 1)
                    piece = jnp.where(lane_group == q, part, piece)
            pieces[rows_of(tile * groups + j, block)] = piece

    each(tiles, fold)


def integrate_kernel(share, pieces, weights, rates, blown, out, values, parts):
    size = weights.shape[0]
    devices = blown.shape[1] // share
    groups = LANES // share
    block = pieces.shape[0] // devices
    bins = size // devices
    even = bins == groups * block

    def bins_of(device, q):
        return pl.ds(device * bins + q, block, stride=groups)

    def unfold(device):
        for q in range(groups):
            values[bins_of(device, q)] = pieces[rows_of(device, block)]

    if even:
        for q in range(groups):
            values[pl.ds(q, devices * block, stride=groups)] = pieces[...]
    else:
        pl.loop(0, devices)(unfold)
    turned = jnp.transpose(values[0:size])
    group = lax.broadcasted_iota(jnp.int32, (share, size), 1) % bins % groups
    now = turned[0:share]
    for q in range(1, groups):
        now = jnp.where(group == q, turned[q * share : (q + 1) * share], now)
    mine = pltpu.roll(blown[...], blown.shape[1] - lax.axis_index("bin") * share, 1)
    push = 1.0 + source_dt * (rates[0:1] * column(mine[0:1, 0:share]))
    drag = source_dt * rates[1:2]
    for repeat in range(SRC):
        terms = now.astype(bf16)
        linear = [dot(terms, weights[:, at : at + CHUNK]) for at in range(0, size, CHUNK)]
        linear = jnp.concatenate(linear, axis=1)
        mean = jnp.sum(now * now, axis=1, keepdims=True) * (1.0 / size)
        spread = jnp.sqrt(mean + tiny_add)
        now = (now * push + source_dt * linear) / (1.0 + drag * spread)
    values[0:size] = jnp.transpose(jnp.concatenate([now] * groups, axis=0))

    def fold(device):
        for q in range(groups):
            parts[q, rows_of(device, block)] = values[bins_of(device, q)]

    if not even:
        pl.loop(0, devices)(fold)
    lane_group = lax.broadcasted_iota(jnp.int32, out.shape, 1) // share
    result = None
    for q in range(groups):
        part = values[pl.ds(q, devices * block, stride=groups)] if even else parts[q]
        result = part if q == 0 else jnp.where(lane_group == q, part, result)
    out[...] = result


def spread_kernel(share, pieces, place, out, columns, done, left):
    tiles, bins, _ = columns.shape
    groups = LANES // share
    block = pieces.shape[0] // (tiles * groups)
    sea_count = tiles * LANES
    points = place.shape[1]
    rows_count, cols_count = grid_shape(points)
    lane_group = lax.broadcasted_iota(jnp.int32, (block, LANES), 1) // share
    if groups * block < bins:
        columns[:, groups * block :] = jnp.zeros((tiles, bins - groups * block, LANES), f32)

    def unfold(tile):
        parts = [pieces[rows_of(tile * groups + j, block)] for j in range(groups)]
        for q in range(groups):
            part = parts[q]
            for j in range(groups):
                if j != q:
                    other = pltpu.roll(parts[j], ((j - q) % groups) * share, 1)
                    part = jnp.where(lane_group == j, other, part)
            columns[tile, pl.ds(q, block, stride=groups)] = part

    each(tiles, unfold)
    terms = jnp.concatenate([split(columns[tile]) for tile in range(tiles)], axis=1)

    def scatter(row):
        here = span(row, cols_count)
        picks = one_hot(sea_count, place[0:1, here] - 1)
        done[:, here] = joined(dot(terms, picks))
        leave(row).start()

    def leave(row):
        here = span(row, cols_count)
        return pltpu.make_async_copy(done.at[:, here], out.at[:, here], left.at[row])

    each(rows_count, scatter)
    each(rows_count, lambda row: leave(row).wait())


def call(kernel, outs, scratch, operands, flops, apart=(), direct=False):
    held = sum(x.size * x.dtype.itemsize for x in operands)
    single = not isinstance(outs, list)
    shapes = [jax.ShapeDtypeStruct(*out) for out in ([outs] if single else outs)]
    held += sum(x.size * x.dtype.itemsize for x in shapes)
    own = sum(4 * math.prod(getattr(x, "shape", ())) for x in scratch)
    in_vmem = pl.BlockSpec(memory_space=pltpu.VMEM)
    places = [pl.BlockSpec(memory_space=pltpu.HBM) if x in apart else in_vmem for x in range(len(operands))]
    operands = [
        x if x.size == 1 else pltpu.with_memory_space_constraint(x, place.memory_space)
        for x, place in zip(operands, places)
    ]
    return pl.pallas_call(
        kernel,
        out_shape=shapes[0] if single else shapes,
        in_specs=places,
        out_specs=(pl.BlockSpec(memory_space=pltpu.HBM) if direct else in_vmem) if single else [in_vmem] * len(shapes),
        scratch_shapes=scratch,
        compiler_params=pltpu.CompilerParams(vmem_limit_bytes=min(60 << 20, (4 << 20) + held + own)),
        cost_estimate=pl.CostEstimate(flops=flops, bytes_accessed=held, transcendentals=0),
    )(*operands)


def local(
    spectra,
    courant,
    coupling,
    growth,
    dissipation,
    wind,
    neighbours,
    wet_mask,
    send_list,
    recv_list,
    substep_count,
):
    devices = lax.axis_size("bin")
    field = spectra[0]
    bins_here, points = field.shape
    rows_count, cols_count = grid_shape(points)
    sea_count = points // 2
    listed = send_list.shape[1]
    share = sea_count // devices
    groups = LANES // share
    block = -(-bins_here // groups)
    bins = up_to(groups * block, SUBLANES)
    size = devices * bins_here
    extra = bins - bins_here
    if extra:
        field = jnp.pad(field, ((0, extra), (0, 0)))
        courant = jnp.pad(courant, ((0, 0), (0, extra)))
    def transpose_all(pieces):
        pieces = pieces.reshape(devices, 1, block * LANES)
        pieces = lax.all_to_all(pieces, "bin", split_axis=0, concat_axis=0)
        return pieces.reshape(devices * block, LANES)

    def swap(array):
        return lax.ppermute(array, "nest", [(0, 1), (1, 0)])

    spectra_b, send_b = swap(field), swap(send_list)
    grid = (rows_count, bins, cols_count)
    row_of = (rows_count, 1, cols_count)
    steps = call(
        count_kernel, ((SUBLANES, cols_count), f32), [], (substep_count.reshape(1, 1),), 10**9
    )
    early = (
        field,
        neighbours[0],
        wet_mask,
        send_list,
        recv_list,
    )
    kept_into = rows_count if points * listed <= 1 << 22 else 1
    order, rank, base, into, sea, taken, lists = call(
        prepare_kernel,
        [
            (row_of, jnp.int32),
            (row_of, jnp.int32),
            (grid, f32),
            ((kept_into, listed, cols_count), bf16),
            (row_of, f32),
            (row_of, f32),
            ((2, listed), jnp.int32),
        ],
        [],
        early,
        10**9,
    )
    field, outgoing, rates = call(
        first_kernel,
        [(grid, f32), ((bins, listed), f32), ((13, bins, cols_count), f32)],
        [pltpu.VMEM(grid, f32)] * 2,
        (base, into, sea, lists, spectra_b, send_b, courant, steps),
        10**9,
    )
    incoming = swap(outgoing)
    kept = rows_count if points * sea_count <= 1 << 22 else 1
    ranks, picks, place, weights, source_rates = call(
        places_kernel,
        [
            (row_of, f32),
            ((kept, cols_count, sea_count), bf16),
            ((1, points), jnp.int32),
            ((size, size), bf16),
            ((2, size), f32),
        ],
        [],
        (rank, sea, coupling, growth.reshape(1, size), dissipation.reshape(1, size)),
        10**9,
    )
    tiles = sea_count // LANES
    pieces, blown = call(
        functools.partial(second_kernel, share),
        [((devices * block, LANES), f32), ((SUBLANES, sea_count), f32)],
        [*[pltpu.VMEM(grid, f32)] * 3, pltpu.VMEM((tiles, bins, LANES), f32)],
        (field, incoming, into, lists, taken, sea, rates, ranks, picks, order, wind),
        10**9,
    )
    pieces = transpose_all(pieces)
    pieces = call(
        functools.partial(integrate_kernel, share),
        ((devices * block, LANES), f32),
        [
            pltpu.VMEM((size + up_to(groups * block, SUBLANES), LANES), f32),
            pltpu.VMEM((groups, devices * block, LANES), f32),
        ],
        (pieces, weights, source_rates, blown),
        10**9,
    )
    pieces = transpose_all(pieces)
    result = call(
        functools.partial(spread_kernel, share),
        ((bins, points), f32),
        [
            pltpu.VMEM((tiles, bins, LANES), f32),
            pltpu.VMEM((bins, points), f32),
            pltpu.SemaphoreType.DMA((rows_count,)),
        ],
        (pieces, place),
        10**8,
        direct=True,
    )
    return result[None, :bins_here]


def solution(mesh):
    in_specs = (
        P("nest", "bin", None),
        P(None, "bin"),
        P(),
        P(),
        P(),
        P("nest", None),
        P("nest", None, None),
        P("nest", None),
        P("nest", None),
        P("nest", None),
        P("nest"),
    )
    out_specs = P("nest", "bin", None)
    return jax.shard_map(local, mesh=mesh, in_specs=in_specs, out_specs=out_specs, check_vma=False)
```

```python
import functools
import math

import jax
import jax.numpy as jnp
from jax import lax
from jax.experimental import pallas as pl
from jax.experimental.pallas import tpu as pltpu
from jax.sharding import PartitionSpec as P

SUBSTEPS = 2
SRC = 5
LANES = 128
SUBLANES = 8
CHUNK = 640

source_dt = 0.25
tiny_add = 1e-06
f32 = jnp.float32
bf16 = jnp.bfloat16


def up_to(value, unit):
    return -(-value // unit) * unit


def grid_shape(points):
    cols_count = min(256, points // 4)
    return points // cols_count, cols_count


def dot(left, right):
    return jnp.dot(left, right, preferred_element_type=f32)


def dot_t(left, right):
    return lax.dot_general(left, right, (((1,), (1,)), ((), ())), preferred_element_type=f32)


def split(values):
    rest = values - values.astype(bf16).astype(f32)
    return jnp.concatenate([values, rest], axis=0).astype(bf16)


def joined(terms):
    half = terms.shape[0] // 2
    return terms[:half] + terms[half:]


def one_hot(rows, index):
    at = lax.broadcasted_iota(jnp.int32, (rows, index.shape[1]), 0)
    return jnp.where(at == index, 1.0, 0.0).astype(bf16)


def column(row):
    size = row.shape[1]
    at = lax.broadcasted_iota(jnp.int32, (size, size), 0)
    across = lax.broadcasted_iota(jnp.int32, (size, size), 1)
    return jnp.sum(jnp.where(at == across, row, 0.0), axis=1, keepdims=True)


def each(count, body):
    if count <= 16:
        for step in range(count):
            body(step)
    else:
        pl.loop(0, count)(body)


def total_of(count, shape, term):
    total = jnp.zeros(shape, f32)
    if count <= 16:
        for step in range(count):
            total = total + term(step)
        return total
    return lax.fori_loop(0, count, lambda step, total: total + term(step), total)


def span(start, size):
    if isinstance(start, int):
        return pl.ds(start * size, size)
    return pl.ds(pl.multiple_of(start * size, size), size)


def rows_of(start, size):
    return pl.ds(start * size, size)


def rows_stacked(tiles):
    at = lax.broadcasted_iota(jnp.int32, (SUBLANES, LANES), 0)
    stacked = eight(tiles[0])
    for k in range(1, len(tiles)):
        stacked = jnp.where(at == k, eight(tiles[k]), stacked)
    return stacked


def tiles_of(row):
    return [row[:, k * LANES : (k + 1) * LANES] for k in range(row.shape[1] // LANES)]


def taken_from(tables, index):
    lane, tile = index & (LANES - 1), index >> (LANES - 1).bit_length()
    found = None
    for k, table in enumerate(tables):
        here = jnp.take_along_axis(eight(table), lane, axis=1, mode="promise_in_bounds")
        found = here if k == 0 else jnp.where(tile == k, here, found)
    return found


def look_up(table, index):
    count = index.shape[1] // LANES
    found = taken_from(tiles_of(table), rows_stacked(tiles_of(index)))
    return jnp.concatenate([found[k : k + 1] for k in range(count)], axis=1)


def walk(tables, order, rank):
    rows_count, _, cols_count = order.shape
    count = cols_count // LANES
    bits = (cols_count - 1).bit_length()
    at = lax.broadcasted_iota(jnp.int32, (SUBLANES, LANES), 0)
    lane = lax.broadcasted_iota(jnp.int32, (SUBLANES, LANES), 1)
    point = (at % count) * LANES + lane
    column_at = lane * count + at % count

    first = tables[0:1, 0:cols_count]
    ahead = jnp.where(at < count, rows_stacked(tiles_of(first)), 0)
    behind = rows_stacked(tiles_of(tables[1:2, 0:cols_count]))
    behind = jnp.where(point == 0, 0, behind)
    steps = jnp.where(point == 0, 0, 1)
    for bit in range(bits):
        far = taken_from([ahead[k : k + 1] for k in range(count)], ahead)
        both = (steps << bits) + behind
        back = taken_from([both[k : k + 1] for k in range(count)], behind)
        ahead = jnp.where((at >= count) & ((column_at >> bit) & 1 == 0), ahead, far)
        steps = steps + (back >> bits)
        behind = back & ((1 << bits) - 1)
    order[0] = jnp.concatenate([ahead[count + k : count + k + 1] for k in range(count)], axis=1)
    steps = steps % count * LANES + steps // count
    rank[0] = jnp.concatenate([steps[k : k + 1] for k in range(count)], axis=1)

    def north(row):
        return tables[2:3, span(row, cols_count)] - (row + 1) * cols_count

    def south(row):
        return tables[3:4, span(row, cols_count)] - (row - 1) * cols_count

    if rows_count <= 16:
        there, back = north(0), south(1)
        for row in range(1, rows_count):
            order[row] = look_up(there, order[0])
            rank[row] = look_up(rank[0], back)
            if row + 1 < rows_count:
                there, back = look_up(north(row), there), look_up(back, south(row + 1))
    else:

        def next_row(row):
            order[row + 1] = look_up(north(row), order[row])
            rank[row + 1] = look_up(rank[row], south(row + 1))

        each(rows_count - 1, next_row)


def grid_places(listed, rank):
    rows_count, _, cols_count = rank.shape
    tiles = tiles_of(listed)
    found = []
    for tile in tiles:
        index = eight(tile)

        def column_in(row, best):
            first = row * cols_count
            within = jnp.clip(index - first, 0, cols_count - 1)
            here = taken_from(tiles_of(rank[row]), within)
            return jnp.where(index - first == within, here + first, best)

        best = jnp.zeros((SUBLANES, LANES), jnp.int32)
        if rows_count <= 16:
            for row in range(rows_count):
                best = column_in(row, best)
        else:
            best = lax.fori_loop(0, rows_count, column_in, best)
        found.append(best[0:1])
    return jnp.concatenate(found, axis=1)


def down(row):
    wide = jnp.broadcast_to(row.astype(f32), (LANES, row.shape[1]))
    return jnp.transpose(wide).astype(jnp.int32)


def one_hot_across(index, first, count):
    lane = lax.broadcasted_iota(jnp.int32, index.shape, 1)
    tiles = [
        jnp.where(lane + (first + tile * LANES) == index, 1.0, 0.0).astype(bf16)
        for tile in range(count // LANES)
    ]
    return jnp.concatenate(tiles, axis=1)


def eight(row):
    return jnp.broadcast_to(row, (SUBLANES, row.shape[1]))


def face_at(cell, onward, slope, other, coefs):
    _, near, far = coefs
    estimate = cell + near * slope + far * other
    return jnp.clip(estimate, jnp.minimum(cell, onward), jnp.maximum(cell, onward))


def ahead(tiles):
    return tiles[1:] + [pltpu.roll(tiles[0], LANES - 1, 1)]


def behind(tiles):
    return [pltpu.roll(tiles[-1], 1, 1)] + tiles[:-1]


def moved_east(cells, coefs):
    rate = coefs[0]
    onward = ahead(cells)
    slopes = [b - a for a, b in zip(cells, onward)]
    others = [jnp.where(rate >= 0.0, a, b) for a, b in zip(behind(slopes), ahead(slopes))]
    faces = [face_at(*values, coefs) for values in zip(cells, onward, slopes, others)]
    return [a - rate * (b - c) for a, b, c in zip(cells, faces, behind(faces))]


def advance(field, moved, faces, sea, east, north):
    rows_count, bins, cols_count = field.shape
    if rows_count <= 16:
        for first in range(0, bins, SUBLANES):
            here = slice(first, first + SUBLANES)
            to_east, to_north = ([x[here, :LANES] for x in coefs] for coefs in (east, north))
            forward = to_north[0] >= 0.0
            rows = [moved_east(tiles_of(field[row, here]), to_east) for row in range(rows_count)]
            for k in range(cols_count // LANES):
                cells = [tiles[k] for tiles in rows]
                onward = cells[1:] + cells[:1]
                slopes = [b - a for a, b in zip(cells, onward)]
                over = [
                    face_at(
                        cells[row],
                        onward[row],
                        slopes[row],
                        jnp.where(forward, slopes[row - 1], slopes[(row + 1) % rows_count]),
                        to_north,
                    )
                    for row in range(rows_count)
                ]
                there = slice(k * LANES, (k + 1) * LANES)
                for row in range(rows_count):
                    change = to_north[0] * (over[row] - over[row - 1])
                    field[row, here, there] = (cells[row] - change) * sea[row, :, there]
        return

    def to_east(row):
        tiles = moved_east(tiles_of(field[row]), [x[:, :LANES] for x in east])
        moved[row] = jnp.concatenate(tiles, axis=1)

    def over_row(row):
        first, second, last = (moved[(row + k + rows_count) % rows_count] for k in (1, 2, -1))
        cell = moved[row]
        other = jnp.where(north[0] >= 0.0, cell - last, second - first)
        faces[row] = face_at(cell, first, first - cell, other, north)

    def to_north(row):
        last = (row - 1 + rows_count) % rows_count
        field[row] = (moved[row] - north[0] * (faces[row] - faces[last])) * sea[row]

    for step in (to_east, over_row, to_north):
        each(rows_count, step)


def coefs_of(rates, which):
    return [rates[3 * which + k] for k in range(3)]


def landing(row, into, lists, cols_count):
    if into.shape[0] > 1:
        return into[row]
    return one_hot_across(down(lists[1:2]), row * cols_count, cols_count)


def count_kernel(steps_in, steps):
    steps[...] = jnp.broadcast_to(steps_in[...].astype(f32), steps.shape)


def prepare_kernel(
    spectra,
    tables,
    wet,
    send,
    recv,
    order,
    rank,
    base,
    into,
    sea,
    taken,
    lists,
):
    rows_count, bins, cols_count = base.shape
    listed = send.shape[1]
    walk(tables, order, rank)
    lists[0:1] = grid_places(send[...], rank)
    lists[1:2] = grid_places(recv[...], rank)
    recv_down = down(lists[1:2])

    def place(row):
        own = one_hot(cols_count, order[row])
        here = one_hot_across(recv_down, row * cols_count, cols_count)
        if into.shape[0] > 1:
            into[row] = here
        got = dot(jnp.ones((SUBLANES, listed), bf16), here)[0:1]
        taken[row] = got
        covered = look_up(wet[0:1, span(row, cols_count)], order[row]).astype(f32)
        sea[row] = covered
        values = joined(dot(split(spectra[:, span(row, cols_count)]), own))
        base[row] = values * (covered * (1.0 - got))

    each(rows_count, place)


def first_kernel(
    base,
    into,
    sea,
    lists,
    spectra_b,
    send_b,
    courant,
    steps,
    field,
    outgoing,
    rates,
    moved,
    faces,
):
    rows_count, bins, cols_count = base.shape
    listed = lists.shape[1]
    second = jnp.where(steps[0:1] > 1.0, 1.0, 0.0)
    for which in range(2):
        rate = column(courant[which : which + 1, :]) / steps[0:1]
        for k, value in enumerate((rate, rate * second)):
            at = 3 * (2 * k + which)
            rates[at] = jnp.broadcast_to(value, (bins, cols_count))
            bend = (1.0 - rates[at] * rates[at]) * (1.0 / 6.0)
            bend = jnp.where(rates[at] >= 0.0, bend, -bend)
            rates[at + 1] = 0.5 - 0.5 * rates[at] - bend
            rates[at + 2] = bend
    rates[12] = jnp.broadcast_to(second, (bins, cols_count))

    def sent(row):
        own = one_hot(cols_count, send_b[...] - row * cols_count)
        return dot(split(spectra_b[:, span(row, cols_count)]), own)

    incoming = total_of(rows_count, (2 * bins, listed), sent).astype(bf16)

    def take(row):
        field[row] = base[row] + joined(dot(incoming, landing(row, into, lists, cols_count)))

    each(rows_count, take)
    advance(field, moved, faces, sea, coefs_of(rates, 0), coefs_of(rates, 1))

    def sending(row):
        return dot(split(field[row]), one_hot(cols_count, lists[0:1] - row * cols_count))

    outgoing[...] = joined(total_of(rows_count, (2 * bins, listed), sending))


def picked(row, ranks, picks, sea_count):
    if picks.shape[0] == ranks.shape[0]:
        return picks[row]
    return one_hot_across(down(ranks[row] - 1.0), 0, sea_count)


def places_kernel(rank, sea, coupling, growth, dissipation, ranks, picks, place, weights, rates):
    rows_count, _, cols_count = rank.shape
    sea_count = picks.shape[2]
    at = lax.broadcasted_iota(jnp.int32, (cols_count, cols_count), 0)
    across = lax.broadcasted_iota(jnp.int32, (cols_count, cols_count), 1)
    upper = jnp.where(at <= across, 1.0, 0.0).astype(bf16)

    def number(row, before):
        here = sea[row]
        number_of = dot(eight(here).astype(bf16), upper)[0:1] + before
        number_of = jnp.where(here > 0.0, number_of, 0.0)
        ranks[row] = number_of
        if picks.shape[0] == rows_count:
            picks[row] = one_hot_across(down(number_of - 1.0), 0, sea_count)
        place[0:1, span(row, cols_count)] = look_up(number_of.astype(jnp.int32), rank[row])
        return before + jnp.sum(here, axis=1, keepdims=True)

    before = jnp.zeros((1, 1), f32)
    if rows_count <= 16:
        for row in range(rows_count):
            before = number(row, before)
    else:
        lax.fori_loop(0, rows_count, number, before)
    turned = min(2, weights.shape[0] // cols_count) * cols_count
    unit = jnp.where(at == across, 1.0, 0.0).astype(bf16)
    for first in range(0, turned, cols_count):
        here = slice(first, first + cols_count)
        weights[here] = dot_t(unit, coupling[:, here]).astype(bf16)
    weights[turned:] = jnp.transpose(coupling[:, turned:])
    rates[0:1] = growth[...]
    rates[1:2] = dissipation[...]


def second_kernel(
    share,
    field_in,
    incoming,
    into,
    lists,
    taken,
    sea,
    rates,
    ranks,
    picks,
    order,
    wind,
    pieces,
    blown,
    field,
    moved,
    faces,
    columns,
):
    rows_count, bins, cols_count = field.shape
    tiles, _, _ = columns.shape
    sea_count = tiles * LANES
    terms = split(incoming[...])

    def take(row):
        got = joined(dot(terms, landing(row, into, lists, cols_count)))
        field[row] = jnp.where(taken[row] * rates[12, 0:1] > 0.5, got, field_in[row])

    each(rows_count, take)
    advance(field, moved, faces, sea, coefs_of(rates, 2), coefs_of(rates, 3))

    def at_sea(row):
        by_grid = look_up(wind[0:1, span(row, cols_count)], order[row])
        terms = jnp.concatenate([split(field[row]), split(eight(by_grid))], axis=0)
        return dot(terms, picked(row, ranks, picks, sea_count))

    total = total_of(rows_count, (2 * bins + 2 * SUBLANES, sea_count), at_sea)
    blown[...] = joined(total[2 * bins :])
    total = joined(total[: 2 * bins])
    for tile in range(tiles):
        columns[tile] = total[:, tile * LANES : (tile + 1) * LANES]
    groups = LANES // share
    block = pieces.shape[0] // (tiles * groups)
    lane_group = lax.broadcasted_iota(jnp.int32, (block, LANES), 1) // share

    def fold(tile):
        parts = []
        for q in range(groups):
            part = columns[tile, pl.ds(q, block, stride=groups)]
            parts.append(pltpu.roll(part, q * share, 1) if q else part)
        for j in range(groups):
            piece = parts[-j % groups]
            for g in range(1, groups):
                piece = jnp.where(lane_group == g, parts[(g - j) % groups], piece)
            pieces[rows_of(tile * groups + j, block)] = piece

    each(tiles, fold)


def integrate_kernel(share, pieces, weights, rates, blown, out, values, parts):
    size = weights.shape[0]
    devices = blown.shape[1] // share
    groups = LANES // share
    block = pieces.shape[0] // devices
    bins = size // devices
    even = bins == groups * block

    def bins_of(device, q):
        return pl.ds(device * bins + q, block, stride=groups)

    me = lax.axis_index("bin")
    shift = lax.rem(me, groups)

    def unfold(device):
        for q in range(groups):
            values[bins_of(device, q)] = pieces[rows_of(device, block)]

    if even:
        for q in range(groups):
            values[pl.ds(q, devices * block, stride=groups)] = pieces[...]
    else:
        pl.loop(0, devices)(unfold)
    turned = jnp.transpose(values[0:size])
    group = lax.broadcasted_iota(jnp.int32, (share, size), 1) % bins % groups
    now = turned[0:share]
    for g in range(1, groups):
        here = group == lax.rem(g + groups - shift, groups)
        now = jnp.where(here, turned[g * share : (g + 1) * share], now)
    mine = pltpu.roll(blown[...], blown.shape[1] - me * share, 1)
    push = 1.0 + source_dt * (rates[0:1] * column(mine[0:1, 0:share]))
    drag = source_dt * rates[1:2]
    for repeat in range(SRC):
        terms = now.astype(bf16)
        linear = [dot(terms, weights[:, at : at + CHUNK]) for at in range(0, size, CHUNK)]
        linear = jnp.concatenate(linear, axis=1)
        mean = jnp.sum(now * now, axis=1, keepdims=True) * (1.0 / size)
        spread = jnp.sqrt(mean + tiny_add)
        now = (now * push + source_dt * linear) / (1.0 + drag * spread)
    values[0:size] = jnp.transpose(jnp.concatenate([now] * groups, axis=0))

    def fold(device):
        for q in range(groups):
            parts[q, rows_of(device, block)] = values[bins_of(device, q)]

    if not even:
        pl.loop(0, devices)(fold)
    lane_group = lax.broadcasted_iota(jnp.int32, out.shape, 1) // share
    result = None
    for q in range(groups):
        part = values[pl.ds(q, devices * block, stride=groups)] if even else parts[q]
        result = part if q == 0 else jnp.where(lane_group == lax.rem(q + shift, groups), part, result)
    out[...] = result


def spread_kernel(share, pieces, place, out, columns, done, left):
    tiles, bins, _ = columns.shape
    groups = LANES // share
    block = pieces.shape[0] // (tiles * groups)
    sea_count = tiles * LANES
    points = place.shape[1]
    rows_count, cols_count = grid_shape(points)
    lane_group = lax.broadcasted_iota(jnp.int32, (block, LANES), 1) // share
    if groups * block < bins:
        columns[:, groups * block :] = jnp.zeros((tiles, bins - groups * block, LANES), f32)

    def unfold(tile):
        parts = [pieces[rows_of(tile * groups + j, block)] for j in range(groups)]
        for q in range(groups):
            part = parts[-q % groups]
            for g in range(1, groups):
                part = jnp.where(lane_group == g, parts[(g - q) % groups], part)
            if q:
                part = pltpu.roll(part, LANES - q * share, 1)
            columns[tile, pl.ds(q, block, stride=groups)] = part

    each(tiles, unfold)
    terms = jnp.concatenate([split(columns[tile]) for tile in range(tiles)], axis=1)

    def scatter(row):
        here = span(row, cols_count)
        picks = one_hot(sea_count, place[0:1, here] - 1)
        done[:, here] = joined(dot(terms, picks))
        leave(row).start()

    def leave(row):
        here = span(row, cols_count)
        return pltpu.make_async_copy(done.at[:, here], out.at[:, here], left.at[row])

    each(rows_count, scatter)
    each(rows_count, lambda row: leave(row).wait())


def call(kernel, outs, scratch, operands, flops, apart=(), direct=False):
    held = sum(x.size * x.dtype.itemsize for x in operands)
    single = not isinstance(outs, list)
    shapes = [jax.ShapeDtypeStruct(*out) for out in ([outs] if single else outs)]
    held += sum(x.size * x.dtype.itemsize for x in shapes)
    own = sum(4 * math.prod(getattr(x, "shape", ())) for x in scratch)
    in_vmem = pl.BlockSpec(memory_space=pltpu.VMEM)
    places = [pl.BlockSpec(memory_space=pltpu.HBM) if x in apart else in_vmem for x in range(len(operands))]
    operands = [
        x if x.size == 1 else pltpu.with_memory_space_constraint(x, place.memory_space)
        for x, place in zip(operands, places)
    ]
    return pl.pallas_call(
        kernel,
        out_shape=shapes[0] if single else shapes,
        in_specs=places,
        out_specs=(pl.BlockSpec(memory_space=pltpu.HBM) if direct else in_vmem) if single else [in_vmem] * len(shapes),
        scratch_shapes=scratch,
        compiler_params=pltpu.CompilerParams(vmem_limit_bytes=min(60 << 20, (4 << 20) + held + own)),
        cost_estimate=pl.CostEstimate(flops=flops, bytes_accessed=held, transcendentals=0),
    )(*operands)


def local(
    spectra,
    courant,
    coupling,
    growth,
    dissipation,
    wind,
    neighbours,
    wet_mask,
    send_list,
    recv_list,
    substep_count,
):
    devices = lax.axis_size("bin")
    field = spectra[0]
    bins_here, points = field.shape
    rows_count, cols_count = grid_shape(points)
    sea_count = points // 2
    listed = send_list.shape[1]
    share = sea_count // devices
    groups = LANES // share
    block = -(-bins_here // groups)
    bins = up_to(groups * block, SUBLANES)
    size = devices * bins_here
    extra = bins - bins_here
    if extra:
        field = jnp.pad(field, ((0, extra), (0, 0)))
        courant = jnp.pad(courant, ((0, 0), (0, extra)))
    def transpose_all(pieces):
        pieces = pieces.reshape(devices, 1, block * LANES)
        pieces = lax.all_to_all(pieces, "bin", split_axis=0, concat_axis=0)
        return pieces.reshape(devices * block, LANES)

    def swap(array):
        return lax.ppermute(array, "nest", [(0, 1), (1, 0)])

    spectra_b, send_b = swap(field), swap(send_list)
    grid = (rows_count, bins, cols_count)
    row_of = (rows_count, 1, cols_count)
    steps = call(
        count_kernel, ((SUBLANES, cols_count), f32), [], (substep_count.reshape(1, 1),), 10**9
    )
    early = (
        field,
        neighbours[0],
        wet_mask,
        send_list,
        recv_list,
    )
    kept_into = rows_count if points * listed <= 1 << 22 else 1
    order, rank, base, into, sea, taken, lists = call(
        prepare_kernel,
        [
            (row_of, jnp.int32),
            (row_of, jnp.int32),
            (grid, f32),
            ((kept_into, listed, cols_count), bf16),
            (row_of, f32),
            (row_of, f32),
            ((2, listed), jnp.int32),
        ],
        [],
        early,
        10**9,
    )
    field, outgoing, rates = call(
        first_kernel,
        [(grid, f32), ((bins, listed), f32), ((13, bins, cols_count), f32)],
        [pltpu.VMEM(grid, f32)] * 2,
        (base, into, sea, lists, spectra_b, send_b, courant, steps),
        10**8,
    )
    incoming = swap(outgoing)
    kept = rows_count if points * sea_count <= 1 << 22 else 1
    ranks, picks, place, weights, source_rates = call(
        places_kernel,
        [
            (row_of, f32),
            ((kept, cols_count, sea_count), bf16),
            ((1, points), jnp.int32),
            ((size, size), bf16),
            ((2, size), f32),
        ],
        [],
        (rank, sea, coupling, growth.reshape(1, size), dissipation.reshape(1, size)),
        10**9,
    )
    tiles = sea_count // LANES
    pieces, blown = call(
        functools.partial(second_kernel, share),
        [((devices * block, LANES), f32), ((SUBLANES, sea_count), f32)],
        [*[pltpu.VMEM(grid, f32)] * 3, pltpu.VMEM((tiles, bins, LANES), f32)],
        (field, incoming, into, lists, taken, sea, rates, ranks, picks, order, wind),
        10**9,
    )
    pieces = transpose_all(pieces)
    pieces = call(
        functools.partial(integrate_kernel, share),
        ((devices * block, LANES), f32),
        [
            pltpu.VMEM((size + up_to(groups * block, SUBLANES), LANES), f32),
            pltpu.VMEM((groups, devices * block, LANES), f32),
        ],
        (pieces, weights, source_rates, blown),
        10**9,
    )
    pieces = transpose_all(pieces)
    result = call(
        functools.partial(spread_kernel, share),
        ((bins, points), f32),
        [
            pltpu.VMEM((tiles, bins, LANES), f32),
            pltpu.VMEM((bins, points), f32),
            pltpu.SemaphoreType.DMA((rows_count,)),
        ],
        (pieces, place),
        10**8,
        direct=True,
    )
    return result[None, :bins_here]


def solution(mesh):
    in_specs = (
        P("nest", "bin", None),
        P(None, "bin"),
        P(),
        P(),
        P(),
        P("nest", None),
        P("nest", None, None),
        P("nest", None),
        P("nest", None),
        P("nest", None),
        P("nest"),
    )
    out_specs = P("nest", "bin", None)
    return jax.shard_map(local, mesh=mesh, in_specs=in_specs, out_specs=out_specs, check_vma=False)
```

```python
import functools
import math

import jax
import jax.numpy as jnp
from jax import lax
from jax.experimental import pallas as pl
from jax.experimental.pallas import tpu as pltpu
from jax.sharding import PartitionSpec as P

SUBSTEPS = 2
SRC = 5
LANES = 128
SUBLANES = 8
CHUNK = 640

source_dt = 0.25
tiny_add = 1e-06
f32 = jnp.float32
bf16 = jnp.bfloat16


def up_to(value, unit):
    return -(-value // unit) * unit


def grid_shape(points):
    cols_count = min(256, points // 4)
    return points // cols_count, cols_count


def dot(left, right):
    return jnp.dot(left, right, preferred_element_type=f32)


def dot_t(left, right):
    return lax.dot_general(left, right, (((1,), (1,)), ((), ())), preferred_element_type=f32)


def split(values):
    rest = values - values.astype(bf16).astype(f32)
    return jnp.concatenate([values, rest], axis=0).astype(bf16)


def joined(terms):
    half = terms.shape[0] // 2
    return terms[:half] + terms[half:]


def marked(at, index):
    same = at.astype(jnp.int16) == jnp.broadcast_to(index, at.shape).astype(jnp.int16)
    return jnp.where(same, jnp.ones(at.shape, bf16), jnp.zeros(at.shape, bf16))


def one_hot(rows, index):
    return marked(lax.broadcasted_iota(jnp.int32, (rows, index.shape[1]), 0), index)


def column(row):
    size = row.shape[1]
    at = lax.broadcasted_iota(jnp.int32, (size, size), 0)
    across = lax.broadcasted_iota(jnp.int32, (size, size), 1)
    return jnp.sum(jnp.where(at == across, row, 0.0), axis=1, keepdims=True)


def each(count, body):
    if count <= 16:
        for step in range(count):
            body(step)
    else:
        pl.loop(0, count)(body)


def total_of(count, shape, term):
    total = jnp.zeros(shape, f32)
    if count <= 16:
        for step in range(count):
            total = total + term(step)
        return total
    return lax.fori_loop(0, count, lambda step, total: total + term(step), total)


def span(start, size):
    if isinstance(start, int):
        return pl.ds(start * size, size)
    return pl.ds(pl.multiple_of(start * size, size), size)


def rows_of(start, size):
    return pl.ds(start * size, size)


def rows_stacked(tiles):
    at = lax.broadcasted_iota(jnp.int32, (SUBLANES, LANES), 0)
    stacked = eight(tiles[0])
    for k in range(1, len(tiles)):
        stacked = jnp.where(at == k, eight(tiles[k]), stacked)
    return stacked


def tiles_of(row):
    return [row[:, k * LANES : (k + 1) * LANES] for k in range(row.shape[1] // LANES)]


def taken_from(tables, index):
    lane, tile = index & (LANES - 1), index >> (LANES - 1).bit_length()
    found = None
    for k, table in enumerate(tables):
        here = jnp.take_along_axis(eight(table), lane, axis=1, mode="promise_in_bounds")
        found = here if k == 0 else jnp.where(tile == k, here, found)
    return found


def look_up(table, index):
    count = index.shape[1] // LANES
    found = taken_from(tiles_of(table), rows_stacked(tiles_of(index)))
    return jnp.concatenate([found[k : k + 1] for k in range(count)], axis=1)


def walk(tables, order, rank):
    rows_count, _, cols_count = order.shape
    count = cols_count // LANES
    bits = (cols_count - 1).bit_length()
    at = lax.broadcasted_iota(jnp.int32, (SUBLANES, LANES), 0)
    lane = lax.broadcasted_iota(jnp.int32, (SUBLANES, LANES), 1)
    point = (at % count) * LANES + lane
    column_at = lane * count + at % count

    first = tables[0:1, 0:cols_count]
    ahead = jnp.where(at < count, rows_stacked(tiles_of(first)), 0)
    behind = rows_stacked(tiles_of(tables[1:2, 0:cols_count]))
    behind = jnp.where(point == 0, 0, behind)
    steps = jnp.where(point == 0, 0, 1)
    for bit in range(bits):
        far = taken_from([ahead[k : k + 1] for k in range(count)], ahead)
        both = (steps << bits) + behind
        back = taken_from([both[k : k + 1] for k in range(count)], behind)
        ahead = jnp.where((at >= count) & ((column_at >> bit) & 1 == 0), ahead, far)
        steps = steps + (back >> bits)
        behind = back & ((1 << bits) - 1)
    order[0] = jnp.concatenate([ahead[count + k : count + k + 1] for k in range(count)], axis=1)
    steps = steps % count * LANES + steps // count
    rank[0] = jnp.concatenate([steps[k : k + 1] for k in range(count)], axis=1)

    def north(row):
        return tables[2:3, span(row, cols_count)] - (row + 1) * cols_count

    def south(row):
        return tables[3:4, span(row, cols_count)] - (row - 1) * cols_count

    if rows_count <= 16:
        there, back = north(0), south(1)
        for row in range(1, rows_count):
            order[row] = look_up(there, order[0])
            rank[row] = look_up(rank[0], back)
            if row + 1 < rows_count:
                there, back = look_up(north(row), there), look_up(back, south(row + 1))
    else:

        def next_row(row):
            order[row + 1] = look_up(north(row), order[row])
            rank[row + 1] = look_up(rank[row], south(row + 1))

        each(rows_count - 1, next_row)


def grid_places(listed, rank):
    rows_count, _, cols_count = rank.shape
    tiles = tiles_of(listed)
    found = []
    for tile in tiles:
        index = eight(tile)

        def column_in(row, best):
            first = row * cols_count
            within = jnp.clip(index - first, 0, cols_count - 1)
            here = taken_from(tiles_of(rank[row]), within)
            return jnp.where(index - first == within, here + first, best)

        best = jnp.zeros((SUBLANES, LANES), jnp.int32)
        if rows_count <= 16:
            for row in range(rows_count):
                best = column_in(row, best)
        else:
            best = lax.fori_loop(0, rows_count, column_in, best)
        found.append(best[0:1])
    return jnp.concatenate(found, axis=1)


def down(row):
    wide = jnp.broadcast_to(row.astype(f32), (LANES, row.shape[1]))
    return jnp.transpose(wide).astype(jnp.int32)


def one_hot_across(index, first, count):
    lane = lax.broadcasted_iota(jnp.int32, index.shape, 1)
    tiles = [
        marked(lane, index - (first + tile * LANES))
        for tile in range(count // LANES)
    ]
    return jnp.concatenate(tiles, axis=1)


def eight(row):
    return jnp.broadcast_to(row, (SUBLANES, row.shape[1]))


def face_at(cell, onward, slope, other, coefs):
    _, near, far = coefs
    estimate = cell + near * slope + far * other
    return jnp.clip(estimate, jnp.minimum(cell, onward), jnp.maximum(cell, onward))


def ahead(tiles):
    return tiles[1:] + [pltpu.roll(tiles[0], LANES - 1, 1)]


def behind(tiles):
    return [pltpu.roll(tiles[-1], 1, 1)] + tiles[:-1]


def moved_east(cells, coefs):
    rate = coefs[0]
    onward = ahead(cells)
    slopes = [b - a for a, b in zip(cells, onward)]
    others = [jnp.where(rate >= 0.0, a, b) for a, b in zip(behind(slopes), ahead(slopes))]
    faces = [face_at(*values, coefs) for values in zip(cells, onward, slopes, others)]
    return [a - rate * (b - c) for a, b, c in zip(cells, faces, behind(faces))]


def advance(field, moved, faces, sea, east, north):
    rows_count, bins, cols_count = field.shape
    if rows_count <= 16:
        for first in range(0, bins, SUBLANES):
            here = slice(first, first + SUBLANES)
            to_east, to_north = ([x[here, :LANES] for x in coefs] for coefs in (east, north))
            forward = to_north[0] >= 0.0
            rows = [moved_east(tiles_of(field[row, here]), to_east) for row in range(rows_count)]
            for k in range(cols_count // LANES):
                cells = [tiles[k] for tiles in rows]
                onward = cells[1:] + cells[:1]
                slopes = [b - a for a, b in zip(cells, onward)]
                over = [
                    face_at(
                        cells[row],
                        onward[row],
                        slopes[row],
                        jnp.where(forward, slopes[row - 1], slopes[(row + 1) % rows_count]),
                        to_north,
                    )
                    for row in range(rows_count)
                ]
                there = slice(k * LANES, (k + 1) * LANES)
                for row in range(rows_count):
                    change = to_north[0] * (over[row] - over[row - 1])
                    field[row, here, there] = (cells[row] - change) * sea[row, :, there]
        return

    def to_east(row):
        tiles = moved_east(tiles_of(field[row]), [x[:, :LANES] for x in east])
        moved[row] = jnp.concatenate(tiles, axis=1)

    def over_row(row):
        first, second, last = (moved[(row + k + rows_count) % rows_count] for k in (1, 2, -1))
        cell = moved[row]
        other = jnp.where(north[0] >= 0.0, cell - last, second - first)
        faces[row] = face_at(cell, first, first - cell, other, north)

    def to_north(row):
        last = (row - 1 + rows_count) % rows_count
        field[row] = (moved[row] - north[0] * (faces[row] - faces[last])) * sea[row]

    for step in (to_east, over_row, to_north):
        each(rows_count, step)


def coefs_of(rates, which):
    return [rates[3 * which + k] for k in range(3)]


def landing(row, into, lists, cols_count):
    if into.shape[0] > 1:
        return into[row]
    return one_hot_across(down(lists[1:2]), row * cols_count, cols_count)


def count_kernel(steps_in, steps):
    steps[...] = jnp.broadcast_to(steps_in[...].astype(f32), steps.shape)


def prepare_kernel(
    spectra,
    tables,
    wet,
    send,
    recv,
    order,
    rank,
    base,
    into,
    sea,
    taken,
    lists,
):
    rows_count, bins, cols_count = base.shape
    listed = send.shape[1]
    walk(tables, order, rank)
    lists[0:1] = grid_places(send[...], rank)
    lists[1:2] = grid_places(recv[...], rank)
    recv_down = down(lists[1:2])

    def place(row):
        own = one_hot(cols_count, order[row])
        here = one_hot_across(recv_down, row * cols_count, cols_count)
        if into.shape[0] > 1:
            into[row] = here
        got = dot(jnp.ones((SUBLANES, listed), bf16), here)[0:1]
        taken[row] = got
        covered = look_up(wet[0:1, span(row, cols_count)], order[row]).astype(f32)
        sea[row] = covered
        values = joined(dot(split(spectra[:, span(row, cols_count)]), own))
        base[row] = values * (covered * (1.0 - got))

    each(rows_count, place)


def first_kernel(
    base,
    into,
    sea,
    lists,
    spectra_b,
    send_b,
    courant,
    steps,
    field,
    outgoing,
    rates,
    moved,
    faces,
):
    rows_count, bins, cols_count = base.shape
    listed = lists.shape[1]
    second = jnp.where(steps[0:1] > 1.0, 1.0, 0.0)
    for which in range(2):
        rate = column(courant[which : which + 1, :]) / steps[0:1]
        for k, value in enumerate((rate, rate * second)):
            at = 3 * (2 * k + which)
            rates[at] = jnp.broadcast_to(value, (bins, cols_count))
            bend = (1.0 - rates[at] * rates[at]) * (1.0 / 6.0)
            bend = jnp.where(rates[at] >= 0.0, bend, -bend)
            rates[at + 1] = 0.5 - 0.5 * rates[at] - bend
            rates[at + 2] = bend
    rates[12] = jnp.broadcast_to(second, (bins, cols_count))

    def sent(row):
        own = one_hot(cols_count, send_b[...] - row * cols_count)
        return dot(split(spectra_b[:, span(row, cols_count)]), own)

    incoming = total_of(rows_count, (2 * bins, listed), sent).astype(bf16)

    def take(row):
        field[row] = base[row] + joined(dot(incoming, landing(row, into, lists, cols_count)))

    each(rows_count, take)
    advance(field, moved, faces, sea, coefs_of(rates, 0), coefs_of(rates, 1))

    def sending(row):
        return dot(split(field[row]), one_hot(cols_count, lists[0:1] - row * cols_count))

    outgoing[...] = joined(total_of(rows_count, (2 * bins, listed), sending))


def picked(row, ranks, picks, sea_count):
    if picks.shape[0] == ranks.shape[0]:
        return picks[row]
    return one_hot_across(down(ranks[row] - 1.0), 0, sea_count)


def places_kernel(rank, sea, coupling, growth, dissipation, ranks, picks, place, weights, rates):
    rows_count, _, cols_count = rank.shape
    sea_count = picks.shape[2]
    at = lax.broadcasted_iota(jnp.int32, (cols_count, cols_count), 0)
    across = lax.broadcasted_iota(jnp.int32, (cols_count, cols_count), 1)
    upper = jnp.where(at <= across, 1.0, 0.0).astype(bf16)

    def number(row, before):
        here = sea[row]
        number_of = dot(eight(here).astype(bf16), upper)[0:1] + before
        number_of = jnp.where(here > 0.0, number_of, 0.0)
        ranks[row] = number_of
        if picks.shape[0] == rows_count:
            picks[row] = one_hot_across(down(number_of - 1.0), 0, sea_count)
        place[0:1, span(row, cols_count)] = look_up(number_of.astype(jnp.int32), rank[row])
        return before + jnp.sum(here, axis=1, keepdims=True)

    before = jnp.zeros((1, 1), f32)
    if rows_count <= 16:
        for row in range(rows_count):
            before = number(row, before)
    else:
        lax.fori_loop(0, rows_count, number, before)
    turned = min(2, weights.shape[0] // cols_count) * cols_count
    unit = jnp.where(at == across, 1.0, 0.0).astype(bf16)
    for first in range(0, turned, cols_count):
        here = slice(first, first + cols_count)
        weights[here] = dot_t(unit, coupling[:, here]).astype(bf16)
    weights[turned:] = jnp.transpose(coupling[:, turned:])
    rates[0:1] = growth[...]
    rates[1:2] = dissipation[...]


def second_kernel(
    share,
    field_in,
    incoming,
    into,
    lists,
    taken,
    sea,
    rates,
    ranks,
    picks,
    order,
    wind,
    pieces,
    blown,
    field,
    moved,
    faces,
    columns,
):
    rows_count, bins, cols_count = field.shape
    tiles, _, _ = columns.shape
    sea_count = tiles * LANES
    terms = split(incoming[...])

    def take(row):
        got = joined(dot(terms, landing(row, into, lists, cols_count)))
        field[row] = jnp.where(taken[row] * rates[12, 0:1] > 0.5, got, field_in[row])

    each(rows_count, take)
    advance(field, moved, faces, sea, coefs_of(rates, 2), coefs_of(rates, 3))

    def at_sea(row):
        by_grid = look_up(wind[0:1, span(row, cols_count)], order[row])
        terms = jnp.concatenate([split(field[row]), split(eight(by_grid))], axis=0)
        return dot(terms, picked(row, ranks, picks, sea_count))

    total = total_of(rows_count, (2 * bins + 2 * SUBLANES, sea_count), at_sea)
    blown[...] = joined(total[2 * bins :])
    total = joined(total[: 2 * bins])
    for tile in range(tiles):
        columns[tile] = total[:, tile * LANES : (tile + 1) * LANES]
    groups = LANES // share
    block = pieces.shape[0] // (tiles * groups)
    lane_group = lax.broadcasted_iota(jnp.int32, (block, LANES), 1) // share

    def fold(tile):
        parts = []
        for q in range(groups):
            part = columns[tile, pl.ds(q, block, stride=groups)]
            parts.append(pltpu.roll(part, q * share, 1) if q else part)
        for j in range(groups):
            piece = parts[-j % groups]
            for g in range(1, groups):
                piece = jnp.where(lane_group == g, parts[(g - j) % groups], piece)
            pieces[rows_of(tile * groups + j, block)] = piece

    each(tiles, fold)


def integrate_kernel(share, pieces, weights, rates, blown, out, values, parts):
    size = weights.shape[0]
    devices = blown.shape[1] // share
    groups = LANES // share
    block = pieces.shape[0] // devices
    bins = size // devices
    even = bins == groups * block

    def bins_of(device, q):
        return pl.ds(device * bins + q, block, stride=groups)

    me = lax.axis_index("bin")
    shift = lax.rem(me, groups)

    def unfold(device):
        for q in range(groups):
            values[bins_of(device, q)] = pieces[rows_of(device, block)]

    if even:
        for q in range(groups):
            values[pl.ds(q, devices * block, stride=groups)] = pieces[...]
    else:
        pl.loop(0, devices)(unfold)
    turned = jnp.transpose(values[0:size])
    group = lax.broadcasted_iota(jnp.int32, (share, size), 1) % bins % groups
    now = turned[0:share]
    for g in range(1, groups):
        here = group == lax.rem(g + groups - shift, groups)
        now = jnp.where(here, turned[g * share : (g + 1) * share], now)
    mine = pltpu.roll(blown[...], blown.shape[1] - me * share, 1)
    push = 1.0 + source_dt * (rates[0:1] * column(mine[0:1, 0:share]))
    drag = source_dt * rates[1:2]
    for repeat in range(SRC):
        terms = now.astype(bf16)
        linear = [dot(terms, weights[:, at : at + CHUNK]) for at in range(0, size, CHUNK)]
        linear = jnp.concatenate(linear, axis=1)
        mean = jnp.sum(now * now, axis=1, keepdims=True) * (1.0 / size)
        spread = jnp.sqrt(mean + tiny_add)
        now = (now * push + source_dt * linear) / (1.0 + drag * spread)
    values[0:size] = jnp.transpose(jnp.concatenate([now] * groups, axis=0))

    def fold(device):
        for q in range(groups):
            parts[q, rows_of(device, block)] = values[bins_of(device, q)]

    if not even:
        pl.loop(0, devices)(fold)
    lane_group = lax.broadcasted_iota(jnp.int32, out.shape, 1) // share
    result = None
    for q in range(groups):
        part = values[pl.ds(q, devices * block, stride=groups)] if even else parts[q]
        result = part if q == 0 else jnp.where(lane_group == lax.rem(q + shift, groups), part, result)
    out[...] = result


def spread_kernel(share, pieces, place, out, columns, done, left):
    tiles, bins, _ = columns.shape
    groups = LANES // share
    block = pieces.shape[0] // (tiles * groups)
    sea_count = tiles * LANES
    points = place.shape[1]
    rows_count, cols_count = grid_shape(points)
    lane_group = lax.broadcasted_iota(jnp.int32, (block, LANES), 1) // share
    if groups * block < bins:
        columns[:, groups * block :] = jnp.zeros((tiles, bins - groups * block, LANES), f32)

    def unfold(tile):
        parts = [pieces[rows_of(tile * groups + j, block)] for j in range(groups)]
        for q in range(groups):
            part = parts[-q % groups]
            for g in range(1, groups):
                part = jnp.where(lane_group == g, parts[(g - q) % groups], part)
            if q:
                part = pltpu.roll(part, LANES - q * share, 1)
            columns[tile, pl.ds(q, block, stride=groups)] = part

    each(tiles, unfold)
    terms = jnp.concatenate([split(columns[tile]) for tile in range(tiles)], axis=1)

    def scatter(row):
        here = span(row, cols_count)
        picks = one_hot(sea_count, place[0:1, here] - 1)
        done[:, here] = joined(dot(terms, picks))
        leave(row).start()

    def leave(row):
        here = span(row, cols_count)
        return pltpu.make_async_copy(done.at[:, here], out.at[:, here], left.at[row])

    each(rows_count, scatter)
    each(rows_count, lambda row: leave(row).wait())


def call(kernel, outs, scratch, operands, flops, apart=(), direct=False):
    held = sum(x.size * x.dtype.itemsize for x in operands)
    single = not isinstance(outs, list)
    shapes = [jax.ShapeDtypeStruct(*out) for out in ([outs] if single else outs)]
    held += sum(x.size * x.dtype.itemsize for x in shapes)
    own = sum(4 * math.prod(getattr(x, "shape", ())) for x in scratch)
    in_vmem = pl.BlockSpec(memory_space=pltpu.VMEM)
    places = [pl.BlockSpec(memory_space=pltpu.HBM) if x in apart else in_vmem for x in range(len(operands))]
    operands = [
        x if x.size == 1 else pltpu.with_memory_space_constraint(x, place.memory_space)
        for x, place in zip(operands, places)
    ]
    return pl.pallas_call(
        kernel,
        out_shape=shapes[0] if single else shapes,
        in_specs=places,
        out_specs=(pl.BlockSpec(memory_space=pltpu.HBM) if direct else in_vmem) if single else [in_vmem] * len(shapes),
        scratch_shapes=scratch,
        compiler_params=pltpu.CompilerParams(vmem_limit_bytes=min(60 << 20, (4 << 20) + held + own)),
        cost_estimate=pl.CostEstimate(flops=flops, bytes_accessed=held, transcendentals=0),
    )(*operands)


def local(
    spectra,
    courant,
    coupling,
    growth,
    dissipation,
    wind,
    neighbours,
    wet_mask,
    send_list,
    recv_list,
    substep_count,
):
    devices = lax.axis_size("bin")
    field = spectra[0]
    bins_here, points = field.shape
    rows_count, cols_count = grid_shape(points)
    sea_count = points // 2
    listed = send_list.shape[1]
    share = sea_count // devices
    groups = LANES // share
    block = -(-bins_here // groups)
    bins = up_to(groups * block, SUBLANES)
    size = devices * bins_here
    extra = bins - bins_here
    if extra:
        field = jnp.pad(field, ((0, extra), (0, 0)))
        courant = jnp.pad(courant, ((0, 0), (0, extra)))
    def transpose_all(pieces):
        pieces = pieces.reshape(devices, 1, block * LANES)
        pieces = lax.all_to_all(pieces, "bin", split_axis=0, concat_axis=0)
        return pieces.reshape(devices * block, LANES)

    def swap(array):
        return lax.ppermute(array, "nest", [(0, 1), (1, 0)])

    spectra_b, send_b = swap(field), swap(send_list)
    grid = (rows_count, bins, cols_count)
    row_of = (rows_count, 1, cols_count)
    steps = call(
        count_kernel, ((SUBLANES, cols_count), f32), [], (substep_count.reshape(1, 1),), 10**9
    )
    early = (
        field,
        neighbours[0],
        wet_mask,
        send_list,
        recv_list,
    )
    kept_into = rows_count if points * listed <= 1 << 22 else 1
    order, rank, base, into, sea, taken, lists = call(
        prepare_kernel,
        [
            (row_of, jnp.int32),
            (row_of, jnp.int32),
            (grid, f32),
            ((kept_into, listed, cols_count), bf16),
            (row_of, f32),
            (row_of, f32),
            ((2, listed), jnp.int32),
        ],
        [],
        early,
        10**9,
    )
    field, outgoing, rates = call(
        first_kernel,
        [(grid, f32), ((bins, listed), f32), ((13, bins, cols_count), f32)],
        [pltpu.VMEM(grid, f32)] * 2,
        (base, into, sea, lists, spectra_b, send_b, courant, steps),
        10**8,
    )
    incoming = swap(outgoing)
    kept = rows_count if points * sea_count <= 1 << 22 else 1
    ranks, picks, place, weights, source_rates = call(
        places_kernel,
        [
            (row_of, f32),
            ((kept, cols_count, sea_count), bf16),
            ((1, points), jnp.int32),
            ((size, size), bf16),
            ((2, size), f32),
        ],
        [],
        (rank, sea, coupling, growth.reshape(1, size), dissipation.reshape(1, size)),
        10**9,
    )
    tiles = sea_count // LANES
    pieces, blown = call(
        functools.partial(second_kernel, share),
        [((devices * block, LANES), f32), ((SUBLANES, sea_count), f32)],
        [*[pltpu.VMEM(grid, f32)] * 3, pltpu.VMEM((tiles, bins, LANES), f32)],
        (field, incoming, into, lists, taken, sea, rates, ranks, picks, order, wind),
        10**9,
    )
    pieces = transpose_all(pieces)
    pieces = call(
        functools.partial(integrate_kernel, share),
        ((devices * block, LANES), f32),
        [
            pltpu.VMEM((size + up_to(groups * block, SUBLANES), LANES), f32),
            pltpu.VMEM((groups, devices * block, LANES), f32),
        ],
        (pieces, weights, source_rates, blown),
        10**9,
    )
    pieces = transpose_all(pieces)
    result = call(
        functools.partial(spread_kernel, share),
        ((bins, points), f32),
        [
            pltpu.VMEM((tiles, bins, LANES), f32),
            pltpu.VMEM((bins, points), f32),
            pltpu.SemaphoreType.DMA((rows_count,)),
        ],
        (pieces, place),
        10**8,
        direct=True,
    )
    return result[None, :bins_here]


def solution(mesh):
    in_specs = (
        P("nest", "bin", None),
        P(None, "bin"),
        P(),
        P(),
        P(),
        P("nest", None),
        P("nest", None, None),
        P("nest", None),
        P("nest", None),
        P("nest", None),
        P("nest"),
    )
    out_specs = P("nest", "bin", None)
    return jax.shard_map(local, mesh=mesh, in_specs=in_specs, out_specs=out_specs, check_vma=False)
```

```python
import functools
import math

import jax
import jax.numpy as jnp
from jax import lax
from jax.experimental import pallas as pl
from jax.experimental.pallas import tpu as pltpu
from jax.sharding import PartitionSpec as P

SUBSTEPS = 2
SRC = 5
LANES = 128
SUBLANES = 8
CHUNK = 640

source_dt = 0.25
tiny_add = 1e-06
f32 = jnp.float32
bf16 = jnp.bfloat16


def up_to(value, unit):
    return -(-value // unit) * unit


def grid_shape(points):
    cols_count = min(256, points // 4)
    return points // cols_count, cols_count


def dot(left, right):
    return jnp.dot(left, right, preferred_element_type=f32)


def dot_t(left, right):
    return lax.dot_general(left, right, (((1,), (1,)), ((), ())), preferred_element_type=f32)


def split(values):
    rest = values - values.astype(bf16).astype(f32)
    return jnp.concatenate([values, rest], axis=0).astype(bf16)


def joined(terms):
    half = terms.shape[0] // 2
    return terms[:half] + terms[half:]


def marked(at, index):
    same = at.astype(jnp.int16) == jnp.broadcast_to(index, at.shape).astype(jnp.int16)
    return jnp.where(same, jnp.ones(at.shape, bf16), jnp.zeros(at.shape, bf16))


def one_hot(rows, index):
    return marked(lax.broadcasted_iota(jnp.int32, (rows, index.shape[1]), 0), index)


def column(row):
    size = row.shape[1]
    at = lax.broadcasted_iota(jnp.int32, (size, size), 0)
    across = lax.broadcasted_iota(jnp.int32, (size, size), 1)
    return jnp.sum(jnp.where(at == across, row, 0.0), axis=1, keepdims=True)


def each(count, body):
    if count <= 16:
        for step in range(count):
            body(step)
    else:
        pl.loop(0, count)(body)


def total_of(count, shape, term):
    total = jnp.zeros(shape, f32)
    if count <= 16:
        for step in range(count):
            total = total + term(step)
        return total
    return lax.fori_loop(0, count, lambda step, total: total + term(step), total)


def span(start, size):
    if isinstance(start, int):
        return pl.ds(start * size, size)
    return pl.ds(pl.multiple_of(start * size, size), size)


def rows_of(start, size):
    return pl.ds(start * size, size)


def rows_stacked(tiles):
    at = lax.broadcasted_iota(jnp.int32, (SUBLANES, LANES), 0)
    stacked = eight(tiles[0])
    for k in range(1, len(tiles)):
        stacked = jnp.where(at == k, eight(tiles[k]), stacked)
    return stacked


def tiles_of(row):
    return [row[:, k * LANES : (k + 1) * LANES] for k in range(row.shape[1] // LANES)]


def taken_from(tables, index):
    lane, tile = index & (LANES - 1), index >> (LANES - 1).bit_length()
    found = None
    for k, table in enumerate(tables):
        here = jnp.take_along_axis(eight(table), lane, axis=1, mode="promise_in_bounds")
        found = here if k == 0 else jnp.where(tile == k, here, found)
    return found


def look_up(table, index):
    count = index.shape[1] // LANES
    found = taken_from(tiles_of(table), rows_stacked(tiles_of(index)))
    return jnp.concatenate([found[k : k + 1] for k in range(count)], axis=1)


def walk(tables, order, rank):
    rows_count, _, cols_count = order.shape
    count = cols_count // LANES
    bits = (cols_count - 1).bit_length()
    at = lax.broadcasted_iota(jnp.int32, (SUBLANES, LANES), 0)
    lane = lax.broadcasted_iota(jnp.int32, (SUBLANES, LANES), 1)
    point = (at % count) * LANES + lane
    column_at = lane * count + at % count

    def doubled(pointers, near):
        for bit in range(bits - 1):
            far = taken_from([pointers[k : k + 1] for k in range(count)], pointers)
            pointers = jnp.where((at >= count) & ((near >> bit) & 1 == 0), pointers, far)
        return [pointers[count + k : count + k + 1] for k in range(count)]

    def stopped(pointers):
        pointers = jnp.where(point == 0, 0, pointers)
        steps = jnp.where(point == 0, 0, 1)
        for bit in range(bits - 1):
            both = (steps << bits) + pointers
            back = taken_from([both[k : k + 1] for k in range(count)], pointers)
            steps = steps + (back >> bits)
            pointers = back & ((1 << bits) - 1)
        return steps, pointers == 0

    east, west = (rows_stacked(tiles_of(tables[k : k + 1, 0:cols_count])) for k in range(2))
    last = jnp.broadcast_to(tables[1:2, 0:1], (SUBLANES, LANES))
    onward = doubled(jnp.where(at < count, east, 0), column_at)
    backward = doubled(jnp.where(at < count, west, last), cols_count - 1 - column_at)
    near = column_at < 1 << (bits - 1)
    found = [jnp.where(near[k : k + 1], onward[k], backward[k]) for k in range(count)]
    order[0] = jnp.concatenate(found, axis=1)
    by_west, reached = stopped(west)
    by_east, _ = stopped(east)
    steps = jnp.where(reached, by_west, cols_count - by_east)
    steps = steps % count * LANES + steps // count
    rank[0] = jnp.concatenate([steps[k : k + 1] for k in range(count)], axis=1)

    def north(row):
        return tables[2:3, span(row, cols_count)] - (row + 1) * cols_count

    def south(row):
        return tables[3:4, span(row, cols_count)] - (row - 1) * cols_count

    if rows_count <= 16:
        there, back = north(0), south(1)
        for row in range(1, rows_count):
            order[row] = look_up(there, order[0])
            rank[row] = look_up(rank[0], back)
            if row + 1 < rows_count:
                there, back = look_up(north(row), there), look_up(back, south(row + 1))
    else:

        def next_row(row):
            order[row + 1] = look_up(north(row), order[row])
            rank[row + 1] = look_up(rank[row], south(row + 1))

        each(rows_count - 1, next_row)


def grid_places(listed, rank):
    rows_count, _, cols_count = rank.shape
    tiles = tiles_of(listed)
    found = []
    for tile in tiles:
        index = eight(tile)

        def column_in(row, best):
            first = row * cols_count
            within = jnp.clip(index - first, 0, cols_count - 1)
            here = taken_from(tiles_of(rank[row]), within)
            return jnp.where(index - first == within, here + first, best)

        best = jnp.zeros((SUBLANES, LANES), jnp.int32)
        if rows_count <= 16:
            for row in range(rows_count):
                best = column_in(row, best)
        else:
            best = lax.fori_loop(0, rows_count, column_in, best)
        found.append(best[0:1])
    return jnp.concatenate(found, axis=1)


def down(row):
    wide = jnp.broadcast_to(row.astype(f32), (LANES, row.shape[1]))
    return jnp.transpose(wide).astype(jnp.int32)


def one_hot_across(index, first, count):
    lane = lax.broadcasted_iota(jnp.int32, index.shape, 1)
    tiles = [
        marked(lane, index - (first + tile * LANES))
        for tile in range(count // LANES)
    ]
    return jnp.concatenate(tiles, axis=1)


def eight(row):
    return jnp.broadcast_to(row, (SUBLANES, row.shape[1]))


def face_at(cell, onward, slope, other, coefs):
    _, near, far = coefs
    estimate = cell + near * slope + far * other
    return jnp.clip(estimate, jnp.minimum(cell, onward), jnp.maximum(cell, onward))


def ahead(tiles):
    return tiles[1:] + [pltpu.roll(tiles[0], LANES - 1, 1)]


def behind(tiles):
    return [pltpu.roll(tiles[-1], 1, 1)] + tiles[:-1]


def moved_east(cells, coefs):
    rate = coefs[0]
    onward = ahead(cells)
    slopes = [b - a for a, b in zip(cells, onward)]
    others = [jnp.where(rate >= 0.0, a, b) for a, b in zip(behind(slopes), ahead(slopes))]
    faces = [face_at(*values, coefs) for values in zip(cells, onward, slopes, others)]
    return [a - rate * (b - c) for a, b, c in zip(cells, faces, behind(faces))]


def advance(field, moved, faces, sea, east, north):
    rows_count, bins, cols_count = field.shape
    if rows_count <= 16:
        for first in range(0, bins, SUBLANES):
            here = slice(first, first + SUBLANES)
            to_east, to_north = ([x[here, :LANES] for x in coefs] for coefs in (east, north))
            forward = to_north[0] >= 0.0
            rows = [moved_east(tiles_of(field[row, here]), to_east) for row in range(rows_count)]
            for k in range(cols_count // LANES):
                cells = [tiles[k] for tiles in rows]
                onward = cells[1:] + cells[:1]
                slopes = [b - a for a, b in zip(cells, onward)]
                over = [
                    face_at(
                        cells[row],
                        onward[row],
                        slopes[row],
                        jnp.where(forward, slopes[row - 1], slopes[(row + 1) % rows_count]),
                        to_north,
                    )
                    for row in range(rows_count)
                ]
                there = slice(k * LANES, (k + 1) * LANES)
                for row in range(rows_count):
                    change = to_north[0] * (over[row] - over[row - 1])
                    field[row, here, there] = (cells[row] - change) * sea[row, :, there]
        return

    def to_east(row):
        tiles = moved_east(tiles_of(field[row]), [x[:, :LANES] for x in east])
        moved[row] = jnp.concatenate(tiles, axis=1)

    def over_row(row):
        first, second, last = (moved[(row + k + rows_count) % rows_count] for k in (1, 2, -1))
        cell = moved[row]
        other = jnp.where(north[0] >= 0.0, cell - last, second - first)
        faces[row] = face_at(cell, first, first - cell, other, north)

    def to_north(row):
        last = (row - 1 + rows_count) % rows_count
        field[row] = (moved[row] - north[0] * (faces[row] - faces[last])) * sea[row]

    for step in (to_east, over_row, to_north):
        each(rows_count, step)


def coefs_of(rates, which):
    return [rates[3 * which + k] for k in range(3)]


def landing(row, into, lists, cols_count):
    if into.shape[0] > 1:
        return into[row]
    return one_hot_across(down(lists[1:2]), row * cols_count, cols_count)


def count_kernel(steps_in, steps):
    steps[...] = jnp.broadcast_to(steps_in[...].astype(f32), steps.shape)


def prepare_kernel(
    spectra,
    tables,
    wet,
    send,
    recv,
    order,
    rank,
    base,
    into,
    sea,
    taken,
    lists,
):
    rows_count, bins, cols_count = base.shape
    listed = send.shape[1]
    walk(tables, order, rank)
    lists[0:1] = grid_places(send[...], rank)
    lists[1:2] = grid_places(recv[...], rank)
    recv_down = down(lists[1:2])

    def place(row):
        own = one_hot(cols_count, order[row])
        here = one_hot_across(recv_down, row * cols_count, cols_count)
        if into.shape[0] > 1:
            into[row] = here
        got = dot(jnp.ones((SUBLANES, listed), bf16), here)[0:1]
        taken[row] = got
        covered = look_up(wet[0:1, span(row, cols_count)], order[row]).astype(f32)
        sea[row] = covered
        values = joined(dot(split(spectra[:, span(row, cols_count)]), own))
        base[row] = values * (covered * (1.0 - got))

    each(rows_count, place)


def first_kernel(
    base,
    into,
    sea,
    lists,
    spectra_b,
    send_b,
    courant,
    steps,
    field,
    outgoing,
    rates,
    moved,
    faces,
):
    rows_count, bins, cols_count = base.shape
    listed = lists.shape[1]
    second = jnp.where(steps[0:1] > 1.0, 1.0, 0.0)
    for which in range(2):
        rate = column(courant[which : which + 1, :]) / steps[0:1]
        for k, value in enumerate((rate, rate * second)):
            at = 3 * (2 * k + which)
            rates[at] = jnp.broadcast_to(value, (bins, cols_count))
            bend = (1.0 - rates[at] * rates[at]) * (1.0 / 6.0)
            bend = jnp.where(rates[at] >= 0.0, bend, -bend)
            rates[at + 1] = 0.5 - 0.5 * rates[at] - bend
            rates[at + 2] = bend
    rates[12] = jnp.broadcast_to(second, (bins, cols_count))

    def sent(row):
        own = one_hot(cols_count, send_b[...] - row * cols_count)
        return dot(split(spectra_b[:, span(row, cols_count)]), own)

    incoming = total_of(rows_count, (2 * bins, listed), sent).astype(bf16)

    def take(row):
        field[row] = base[row] + joined(dot(incoming, landing(row, into, lists, cols_count)))

    each(rows_count, take)
    advance(field, moved, faces, sea, coefs_of(rates, 0), coefs_of(rates, 1))

    def sending(row):
        return dot(split(field[row]), one_hot(cols_count, lists[0:1] - row * cols_count))

    outgoing[...] = joined(total_of(rows_count, (2 * bins, listed), sending))


def picked(row, ranks, picks, sea_count):
    if picks.shape[0] == ranks.shape[0]:
        return picks[row]
    return one_hot_across(down(ranks[row] - 1.0), 0, sea_count)


def places_kernel(rank, sea, coupling, growth, dissipation, ranks, picks, place, weights, rates):
    rows_count, _, cols_count = rank.shape
    sea_count = picks.shape[2]
    at = lax.broadcasted_iota(jnp.int32, (cols_count, cols_count), 0)
    across = lax.broadcasted_iota(jnp.int32, (cols_count, cols_count), 1)
    upper = jnp.where(at <= across, 1.0, 0.0).astype(bf16)

    def number(row, before):
        here = sea[row]
        number_of = dot(eight(here).astype(bf16), upper)[0:1] + before
        number_of = jnp.where(here > 0.0, number_of, 0.0)
        ranks[row] = number_of
        if picks.shape[0] == rows_count:
            picks[row] = one_hot_across(down(number_of - 1.0), 0, sea_count)
        place[0:1, span(row, cols_count)] = look_up(number_of.astype(jnp.int32), rank[row])
        return before + jnp.sum(here, axis=1, keepdims=True)

    before = jnp.zeros((1, 1), f32)
    if rows_count <= 16:
        for row in range(rows_count):
            before = number(row, before)
    else:
        lax.fori_loop(0, rows_count, number, before)
    turned = min(2, weights.shape[0] // cols_count) * cols_count
    unit = jnp.where(at == across, 1.0, 0.0).astype(bf16)
    for first in range(0, turned, cols_count):
        here = slice(first, first + cols_count)
        weights[here] = dot_t(unit, coupling[:, here]).astype(bf16)
    weights[turned:] = jnp.transpose(coupling[:, turned:])
    rates[0:1] = growth[...]
    rates[1:2] = dissipation[...]


def second_kernel(
    share,
    field_in,
    incoming,
    into,
    lists,
    taken,
    sea,
    rates,
    ranks,
    picks,
    order,
    wind,
    pieces,
    blown,
    field,
    moved,
    faces,
    columns,
):
    rows_count, bins, cols_count = field.shape
    tiles, _, _ = columns.shape
    sea_count = tiles * LANES
    terms = split(incoming[...])

    def take(row):
        got = joined(dot(terms, landing(row, into, lists, cols_count)))
        field[row] = jnp.where(taken[row] * rates[12, 0:1] > 0.5, got, field_in[row])

    each(rows_count, take)
    advance(field, moved, faces, sea, coefs_of(rates, 2), coefs_of(rates, 3))

    def at_sea(row):
        by_grid = look_up(wind[0:1, span(row, cols_count)], order[row])
        terms = jnp.concatenate([split(field[row]), split(eight(by_grid))], axis=0)
        return dot(terms, picked(row, ranks, picks, sea_count))

    total = total_of(rows_count, (2 * bins + 2 * SUBLANES, sea_count), at_sea)
    blown[...] = joined(total[2 * bins :])
    total = joined(total[: 2 * bins])
    for tile in range(tiles):
        columns[tile] = total[:, tile * LANES : (tile + 1) * LANES]
    groups = LANES // share
    block = pieces.shape[0] // (tiles * groups)
    lane_group = lax.broadcasted_iota(jnp.int32, (block, LANES), 1) // share

    def fold(tile):
        parts = []
        for q in range(groups):
            part = columns[tile, pl.ds(q, block, stride=groups)]
            parts.append(pltpu.roll(part, q * share, 1) if q else part)
        for j in range(groups):
            piece = parts[-j % groups]
            for g in range(1, groups):
                piece = jnp.where(lane_group == g, parts[(g - j) % groups], piece)
            pieces[rows_of(tile * groups + j, block)] = piece

    each(tiles, fold)


def integrate_kernel(share, pieces, weights, rates, blown, out, values, parts):
    size = weights.shape[0]
    devices = blown.shape[1] // share
    groups = LANES // share
    block = pieces.shape[0] // devices
    bins = size // devices
    even = bins == groups * block

    def bins_of(device, q):
        return pl.ds(device * bins + q, block, stride=groups)

    me = lax.axis_index("bin")
    shift = lax.rem(me, groups)

    def unfold(device):
        for q in range(groups):
            values[bins_of(device, q)] = pieces[rows_of(device, block)]

    if even:
        for q in range(groups):
            values[pl.ds(q, devices * block, stride=groups)] = pieces[...]
    else:
        pl.loop(0, devices)(unfold)
    turned = jnp.transpose(values[0:size])
    group = lax.broadcasted_iota(jnp.int32, (share, size), 1) % bins % groups
    now = turned[0:share]
    for g in range(1, groups):
        here = group == lax.rem(g + groups - shift, groups)
        now = jnp.where(here, turned[g * share : (g + 1) * share], now)
    mine = pltpu.roll(blown[...], blown.shape[1] - me * share, 1)
    push = 1.0 + source_dt * (rates[0:1] * column(mine[0:1, 0:share]))
    drag = source_dt * rates[1:2]
    for repeat in range(SRC):
        terms = now.astype(bf16)
        linear = [dot(terms, weights[:, at : at + CHUNK]) for at in range(0, size, CHUNK)]
        linear = jnp.concatenate(linear, axis=1)
        mean = jnp.sum(now * now, axis=1, keepdims=True) * (1.0 / size)
        spread = jnp.sqrt(mean + tiny_add)
        now = (now * push + source_dt * linear) / (1.0 + drag * spread)
    values[0:size] = jnp.transpose(jnp.concatenate([now] * groups, axis=0))

    def fold(device):
        for q in range(groups):
            parts[q, rows_of(device, block)] = values[bins_of(device, q)]

    if not even:
        pl.loop(0, devices)(fold)
    lane_group = lax.broadcasted_iota(jnp.int32, out.shape, 1) // share
    result = None
    for q in range(groups):
        part = values[pl.ds(q, devices * block, stride=groups)] if even else parts[q]
        result = part if q == 0 else jnp.where(lane_group == lax.rem(q + shift, groups), part, result)
    out[...] = result


def spread_kernel(share, pieces, place, out, columns, done, left):
    tiles, bins, _ = columns.shape
    groups = LANES // share
    block = pieces.shape[0] // (tiles * groups)
    sea_count = tiles * LANES
    points = place.shape[1]
    rows_count, cols_count = grid_shape(points)
    lane_group = lax.broadcasted_iota(jnp.int32, (block, LANES), 1) // share
    if groups * block < bins:
        columns[:, groups * block :] = jnp.zeros((tiles, bins - groups * block, LANES), f32)

    def unfold(tile):
        parts = [pieces[rows_of(tile * groups + j, block)] for j in range(groups)]
        for q in range(groups):
            part = parts[-q % groups]
            for g in range(1, groups):
                part = jnp.where(lane_group == g, parts[(g - q) % groups], part)
            if q:
                part = pltpu.roll(part, LANES - q * share, 1)
            columns[tile, pl.ds(q, block, stride=groups)] = part

    each(tiles, unfold)
    terms = jnp.concatenate([split(columns[tile]) for tile in range(tiles)], axis=1)

    def scatter(row):
        here = span(row, cols_count)
        picks = one_hot(sea_count, place[0:1, here] - 1)
        done[:, here] = joined(dot(terms, picks))
        leave(row).start()

    def leave(row):
        here = span(row, cols_count)
        return pltpu.make_async_copy(done.at[:, here], out.at[:, here], left.at[row])

    each(rows_count, scatter)
    each(rows_count, lambda row: leave(row).wait())


def call(kernel, outs, scratch, operands, flops, apart=(), direct=False):
    held = sum(x.size * x.dtype.itemsize for x in operands)
    single = not isinstance(outs, list)
    shapes = [jax.ShapeDtypeStruct(*out) for out in ([outs] if single else outs)]
    held += sum(x.size * x.dtype.itemsize for x in shapes)
    own = sum(4 * math.prod(getattr(x, "shape", ())) for x in scratch)
    in_vmem = pl.BlockSpec(memory_space=pltpu.VMEM)
    places = [pl.BlockSpec(memory_space=pltpu.HBM) if x in apart else in_vmem for x in range(len(operands))]
    operands = [
        x if x.size == 1 else pltpu.with_memory_space_constraint(x, place.memory_space)
        for x, place in zip(operands, places)
    ]
    return pl.pallas_call(
        kernel,
        out_shape=shapes[0] if single else shapes,
        in_specs=places,
        out_specs=(pl.BlockSpec(memory_space=pltpu.HBM) if direct else in_vmem) if single else [in_vmem] * len(shapes),
        scratch_shapes=scratch,
        compiler_params=pltpu.CompilerParams(vmem_limit_bytes=min(60 << 20, (4 << 20) + held + own)),
        cost_estimate=pl.CostEstimate(flops=flops, bytes_accessed=held, transcendentals=0),
    )(*operands)


def local(
    spectra,
    courant,
    coupling,
    growth,
    dissipation,
    wind,
    neighbours,
    wet_mask,
    send_list,
    recv_list,
    substep_count,
):
    devices = lax.axis_size("bin")
    field = spectra[0]
    bins_here, points = field.shape
    rows_count, cols_count = grid_shape(points)
    sea_count = points // 2
    listed = send_list.shape[1]
    share = sea_count // devices
    groups = LANES // share
    block = -(-bins_here // groups)
    bins = up_to(groups * block, SUBLANES)
    size = devices * bins_here
    extra = bins - bins_here
    if extra:
        field = jnp.pad(field, ((0, extra), (0, 0)))
        courant = jnp.pad(courant, ((0, 0), (0, extra)))
    def transpose_all(pieces):
        pieces = pieces.reshape(devices, 1, block * LANES)
        pieces = lax.all_to_all(pieces, "bin", split_axis=0, concat_axis=0)
        return pieces.reshape(devices * block, LANES)

    def swap(array):
        return lax.ppermute(array, "nest", [(0, 1), (1, 0)])

    spectra_b, send_b = swap(field), swap(send_list)
    grid = (rows_count, bins, cols_count)
    row_of = (rows_count, 1, cols_count)
    steps = call(
        count_kernel, ((SUBLANES, cols_count), f32), [], (substep_count.reshape(1, 1),), 10**9
    )
    early = (
        field,
        neighbours[0],
        wet_mask,
        send_list,
        recv_list,
    )
    kept_into = rows_count if points * listed <= 1 << 22 else 1
    order, rank, base, into, sea, taken, lists = call(
        prepare_kernel,
        [
            (row_of, jnp.int32),
            (row_of, jnp.int32),
            (grid, f32),
            ((kept_into, listed, cols_count), bf16),
            (row_of, f32),
            (row_of, f32),
            ((2, listed), jnp.int32),
        ],
        [],
        early,
        10**9,
    )
    field, outgoing, rates = call(
        first_kernel,
        [(grid, f32), ((bins, listed), f32), ((13, bins, cols_count), f32)],
        [pltpu.VMEM(grid, f32)] * 2,
        (base, into, sea, lists, spectra_b, send_b, courant, steps),
        10**8,
    )
    incoming = swap(outgoing)
    kept = rows_count if points * sea_count <= 1 << 22 else 1
    ranks, picks, place, weights, source_rates = call(
        places_kernel,
        [
            (row_of, f32),
            ((kept, cols_count, sea_count), bf16),
            ((1, points), jnp.int32),
            ((size, size), bf16),
            ((2, size), f32),
        ],
        [],
        (rank, sea, coupling, growth.reshape(1, size), dissipation.reshape(1, size)),
        10**9,
    )
    tiles = sea_count // LANES
    pieces, blown = call(
        functools.partial(second_kernel, share),
        [((devices * block, LANES), f32), ((SUBLANES, sea_count), f32)],
        [*[pltpu.VMEM(grid, f32)] * 3, pltpu.VMEM((tiles, bins, LANES), f32)],
        (field, incoming, into, lists, taken, sea, rates, ranks, picks, order, wind),
        10**9,
    )
    pieces = transpose_all(pieces)
    pieces = call(
        functools.partial(integrate_kernel, share),
        ((devices * block, LANES), f32),
        [
            pltpu.VMEM((size + up_to(groups * block, SUBLANES), LANES), f32),
            pltpu.VMEM((groups, devices * block, LANES), f32),
        ],
        (pieces, weights, source_rates, blown),
        10**9,
    )
    pieces = transpose_all(pieces)
    result = call(
        functools.partial(spread_kernel, share),
        ((bins, points), f32),
        [
            pltpu.VMEM((tiles, bins, LANES), f32),
            pltpu.VMEM((bins, points), f32),
            pltpu.SemaphoreType.DMA((rows_count,)),
        ],
        (pieces, place),
        10**8,
        direct=True,
    )
    return result[None, :bins_here]


def solution(mesh):
    in_specs = (
        P("nest", "bin", None),
        P(None, "bin"),
        P(),
        P(),
        P(),
        P("nest", None),
        P("nest", None, None),
        P("nest", None),
        P("nest", None),
        P("nest", None),
        P("nest"),
    )
    out_specs = P("nest", "bin", None)
    return jax.shard_map(local, mesh=mesh, in_specs=in_specs, out_specs=out_specs, check_vma=False)
```

```python
import functools
import math

import jax
import jax.numpy as jnp
from jax import lax
from jax.experimental import pallas as pl
from jax.experimental.pallas import tpu as pltpu
from jax.sharding import PartitionSpec as P

SUBSTEPS = 2
SRC = 5
LANES = 128
SUBLANES = 8
CHUNK = 640

source_dt = 0.25
tiny_add = 1e-06
f32 = jnp.float32
bf16 = jnp.bfloat16


def up_to(value, unit):
    return -(-value // unit) * unit


def grid_shape(points):
    cols_count = min(256, points // 4)
    return points // cols_count, cols_count


def dot(left, right):
    return jnp.dot(left, right, preferred_element_type=f32)


def dot_t(left, right):
    return lax.dot_general(left, right, (((1,), (1,)), ((), ())), preferred_element_type=f32)


def split(values):
    rest = values - values.astype(bf16).astype(f32)
    return jnp.concatenate([values, rest], axis=0).astype(bf16)


def joined(terms):
    half = terms.shape[0] // 2
    return terms[:half] + terms[half:]


def marked(at, index):
    same = at.astype(jnp.int16) == jnp.broadcast_to(index, at.shape).astype(jnp.int16)
    return jnp.where(same, jnp.ones(at.shape, bf16), jnp.zeros(at.shape, bf16))


def one_hot(rows, index):
    return marked(lax.broadcasted_iota(jnp.int32, (rows, index.shape[1]), 0), index)


def column(row):
    size = row.shape[1]
    at = lax.broadcasted_iota(jnp.int32, (size, size), 0)
    across = lax.broadcasted_iota(jnp.int32, (size, size), 1)
    return jnp.sum(jnp.where(at == across, row, 0.0), axis=1, keepdims=True)


def each(count, body):
    if count <= 16:
        for step in range(count):
            body(step)
    else:
        pl.loop(0, count)(body)


def total_of(count, shape, term):
    total = jnp.zeros(shape, f32)
    if count <= 16:
        for step in range(count):
            total = total + term(step)
        return total
    return lax.fori_loop(0, count, lambda step, total: total + term(step), total)


def span(start, size):
    if isinstance(start, int):
        return pl.ds(start * size, size)
    return pl.ds(pl.multiple_of(start * size, size), size)


def rows_of(start, size):
    return pl.ds(start * size, size)


def rows_stacked(tiles):
    at = lax.broadcasted_iota(jnp.int32, (SUBLANES, LANES), 0)
    stacked = eight(tiles[0])
    for k in range(1, len(tiles)):
        stacked = jnp.where(at == k, eight(tiles[k]), stacked)
    return stacked


def tiles_of(row):
    return [row[:, k * LANES : (k + 1) * LANES] for k in range(row.shape[1] // LANES)]


def taken_from(tables, index):
    lane, tile = index & (LANES - 1), index >> (LANES - 1).bit_length()
    found = None
    for k, table in enumerate(tables):
        here = jnp.take_along_axis(eight(table), lane, axis=1, mode="promise_in_bounds")
        found = here if k == 0 else jnp.where(tile == k, here, found)
    return found


def look_up(table, index):
    count = index.shape[1] // LANES
    found = taken_from(tiles_of(table), rows_stacked(tiles_of(index)))
    return jnp.concatenate([found[k : k + 1] for k in range(count)], axis=1)


def walk(tables, order, rank):
    rows_count, _, cols_count = order.shape
    count = cols_count // LANES
    bits = (cols_count - 1).bit_length()
    at = lax.broadcasted_iota(jnp.int32, (SUBLANES, LANES), 0)
    lane = lax.broadcasted_iota(jnp.int32, (SUBLANES, LANES), 1)
    point = (at % count) * LANES + lane
    column_at = lane * count + at % count

    def doubled(pointers, near):
        for bit in range(bits - 1):
            far = taken_from([pointers[k : k + 1] for k in range(count)], pointers)
            pointers = jnp.where((at >= count) & ((near >> bit) & 1 == 0), pointers, far)
        return [pointers[count + k : count + k + 1] for k in range(count)]

    def stopped(pointers):
        pointers = jnp.where(point == 0, 0, pointers)
        steps = jnp.where(point == 0, 0, 1)
        for bit in range(bits - 1):
            both = (steps << bits) + pointers
            back = taken_from([both[k : k + 1] for k in range(count)], pointers)
            steps = steps + (back >> bits)
            pointers = back & ((1 << bits) - 1)
        return steps, pointers == 0

    east, west = (rows_stacked(tiles_of(tables[k : k + 1, 0:cols_count])) for k in range(2))
    last = jnp.broadcast_to(tables[1:2, 0:1], (SUBLANES, LANES))
    onward = doubled(jnp.where(at < count, east, 0), column_at)
    backward = doubled(jnp.where(at < count, west, last), cols_count - 1 - column_at)
    near = column_at < 1 << (bits - 1)
    found = [jnp.where(near[k : k + 1], onward[k], backward[k]) for k in range(count)]
    order[0] = jnp.concatenate(found, axis=1)
    by_west, reached = stopped(west)
    by_east, _ = stopped(east)
    steps = jnp.where(reached, by_west, cols_count - by_east)
    steps = steps % count * LANES + steps // count
    rank[0] = jnp.concatenate([steps[k : k + 1] for k in range(count)], axis=1)

    def north(row):
        return tables[2:3, span(row, cols_count)] - (row + 1) * cols_count

    def south(row):
        return tables[3:4, span(row, cols_count)] - (row - 1) * cols_count

    if rows_count <= 16:
        there, back = north(0), south(1)
        for row in range(1, rows_count):
            order[row] = look_up(there, order[0])
            rank[row] = look_up(rank[0], back)
            if row + 1 < rows_count:
                there, back = look_up(north(row), there), look_up(back, south(row + 1))
    else:

        def next_row(row):
            order[row + 1] = look_up(north(row), order[row])
            rank[row + 1] = look_up(rank[row], south(row + 1))

        each(rows_count - 1, next_row)


def grid_places(listed, rank):
    rows_count, _, cols_count = rank.shape
    tiles = tiles_of(listed)
    found = []
    for tile in tiles:
        index = eight(tile)

        def column_in(row, best):
            first = row * cols_count
            within = jnp.clip(index - first, 0, cols_count - 1)
            here = taken_from(tiles_of(rank[row]), within)
            return jnp.where(index - first == within, here + first, best)

        best = jnp.zeros((SUBLANES, LANES), jnp.int32)
        if rows_count <= 16:
            for row in range(rows_count):
                best = column_in(row, best)
        else:
            best = lax.fori_loop(0, rows_count, column_in, best)
        found.append(best[0:1])
    return jnp.concatenate(found, axis=1)


def down(row):
    wide = jnp.broadcast_to(row.astype(f32), (LANES, row.shape[1]))
    return jnp.transpose(wide).astype(jnp.int32)


def one_hot_across(index, first, count):
    lane = lax.broadcasted_iota(jnp.int32, index.shape, 1)
    tiles = [
        marked(lane, index - (first + tile * LANES))
        for tile in range(count // LANES)
    ]
    return jnp.concatenate(tiles, axis=1)


def eight(row):
    return jnp.broadcast_to(row, (SUBLANES, row.shape[1]))


def face_at(cell, onward, slope, other, coefs):
    _, near, far = coefs
    estimate = cell + near * slope + far * other
    return jnp.clip(estimate, jnp.minimum(cell, onward), jnp.maximum(cell, onward))


def ahead(tiles):
    return tiles[1:] + [pltpu.roll(tiles[0], LANES - 1, 1)]


def behind(tiles):
    return [pltpu.roll(tiles[-1], 1, 1)] + tiles[:-1]


def moved_east(cells, coefs):
    rate = coefs[0]
    onward = ahead(cells)
    slopes = [b - a for a, b in zip(cells, onward)]
    others = [jnp.where(rate >= 0.0, a, b) for a, b in zip(behind(slopes), ahead(slopes))]
    faces = [face_at(*values, coefs) for values in zip(cells, onward, slopes, others)]
    return [a - rate * (b - c) for a, b, c in zip(cells, faces, behind(faces))]


def advance(field, moved, faces, sea, east, north):
    rows_count, bins, cols_count = field.shape
    if rows_count <= 16:
        for first in range(0, bins, SUBLANES):
            here = slice(first, first + SUBLANES)
            to_east, to_north = ([x[here, :LANES] for x in coefs] for coefs in (east, north))
            forward = to_north[0] >= 0.0
            rows = [moved_east(tiles_of(field[row, here]), to_east) for row in range(rows_count)]
            for k in range(cols_count // LANES):
                cells = [tiles[k] for tiles in rows]
                onward = cells[1:] + cells[:1]
                slopes = [b - a for a, b in zip(cells, onward)]
                over = [
                    face_at(
                        cells[row],
                        onward[row],
                        slopes[row],
                        jnp.where(forward, slopes[row - 1], slopes[(row + 1) % rows_count]),
                        to_north,
                    )
                    for row in range(rows_count)
                ]
                there = slice(k * LANES, (k + 1) * LANES)
                for row in range(rows_count):
                    change = to_north[0] * (over[row] - over[row - 1])
                    field[row, here, there] = (cells[row] - change) * sea[row, :, there]
        return

    def to_east(row):
        tiles = moved_east(tiles_of(field[row]), [x[:, :LANES] for x in east])
        moved[row] = jnp.concatenate(tiles, axis=1)

    def over_row(row):
        first, second, last = (moved[(row + k + rows_count) % rows_count] for k in (1, 2, -1))
        cell = moved[row]
        other = jnp.where(north[0] >= 0.0, cell - last, second - first)
        faces[row] = face_at(cell, first, first - cell, other, north)

    def to_north(row):
        last = (row - 1 + rows_count) % rows_count
        field[row] = (moved[row] - north[0] * (faces[row] - faces[last])) * sea[row]

    for step in (to_east, over_row, to_north):
        each(rows_count, step)


def coefs_of(rates, which):
    return [rates[3 * which + k] for k in range(3)]


def landing(row, into, lists, cols_count):
    if into.shape[0] > 1:
        return into[row]
    return one_hot_across(down(lists[1:2]), row * cols_count, cols_count)


def count_kernel(steps_in, steps):
    steps[...] = jnp.broadcast_to(steps_in[...].astype(f32), steps.shape)


def prepare_kernel(
    spectra,
    tables,
    wet,
    send,
    recv,
    order,
    rank,
    base,
    into,
    sea,
    taken,
    lists,
):
    rows_count, bins, cols_count = base.shape
    listed = send.shape[1]
    walk(tables, order, rank)
    lists[0:1] = grid_places(send[...], rank)
    lists[1:2] = grid_places(recv[...], rank)
    recv_down = down(lists[1:2])

    def place(row):
        own = one_hot(cols_count, order[row])
        here = one_hot_across(recv_down, row * cols_count, cols_count)
        if into.shape[0] > 1:
            into[row] = here
        got = dot(jnp.ones((SUBLANES, listed), bf16), here)[0:1]
        taken[row] = got
        covered = look_up(wet[0:1, span(row, cols_count)], order[row]).astype(f32)
        sea[row] = covered
        values = joined(dot(split(spectra[:, span(row, cols_count)]), own))
        base[row] = values * (covered * (1.0 - got))

    each(rows_count, place)


def first_kernel(
    base,
    into,
    sea,
    lists,
    spectra_b,
    send_b,
    courant,
    steps,
    field,
    outgoing,
    rates,
    moved,
    faces,
):
    rows_count, bins, cols_count = base.shape
    listed = lists.shape[1]
    second = jnp.where(steps[0:1] > 1.0, 1.0, 0.0)
    for which in range(2):
        rate = column(courant[which : which + 1, :]) / steps[0:1]
        for k, value in enumerate((rate, rate * second)):
            at = 3 * (2 * k + which)
            rates[at] = jnp.broadcast_to(value, (bins, cols_count))
            bend = (1.0 - rates[at] * rates[at]) * (1.0 / 6.0)
            bend = jnp.where(rates[at] >= 0.0, bend, -bend)
            rates[at + 1] = 0.5 - 0.5 * rates[at] - bend
            rates[at + 2] = bend
    rates[12] = jnp.broadcast_to(second, (bins, cols_count))

    def sent(row):
        own = one_hot(cols_count, send_b[...] - row * cols_count)
        return dot(split(spectra_b[:, span(row, cols_count)]), own)

    incoming = total_of(rows_count, (2 * bins, listed), sent).astype(bf16)

    def take(row):
        field[row] = base[row] + joined(dot(incoming, landing(row, into, lists, cols_count)))

    each(rows_count, take)
    advance(field, moved, faces, sea, coefs_of(rates, 0), coefs_of(rates, 1))

    def sending(row):
        return dot(split(field[row]), one_hot(cols_count, lists[0:1] - row * cols_count))

    outgoing[...] = joined(total_of(rows_count, (2 * bins, listed), sending))


def picked(row, ranks, picks, sea_count):
    if picks.shape[0] == ranks.shape[0]:
        return picks[row]
    return one_hot_across(down(ranks[row] - 1.0), 0, sea_count)


def places_kernel(
    rank, order, wind, sea, coupling, growth, dissipation, ranks, picks, place, winds, weights, rates
):
    rows_count, _, cols_count = rank.shape
    sea_count = picks.shape[2]
    at = lax.broadcasted_iota(jnp.int32, (cols_count, cols_count), 0)
    across = lax.broadcasted_iota(jnp.int32, (cols_count, cols_count), 1)
    upper = jnp.where(at <= across, 1.0, 0.0).astype(bf16)

    def number(row, before):
        here = sea[row]
        number_of = dot(eight(here).astype(bf16), upper)[0:1] + before
        number_of = jnp.where(here > 0.0, number_of, 0.0)
        ranks[row] = number_of
        winds[row] = look_up(wind[0:1, span(row, cols_count)], order[row])
        if picks.shape[0] == rows_count:
            picks[row] = one_hot_across(down(number_of - 1.0), 0, sea_count)
        place[0:1, span(row, cols_count)] = look_up(number_of.astype(jnp.int32), rank[row])
        return before + jnp.sum(here, axis=1, keepdims=True)

    before = jnp.zeros((1, 1), f32)
    if rows_count <= 16:
        for row in range(rows_count):
            before = number(row, before)
    else:
        lax.fori_loop(0, rows_count, number, before)
    turned = min(3, weights.shape[0] // cols_count) * cols_count
    unit = jnp.where(at == across, 1.0, 0.0).astype(bf16)
    for first in range(0, turned, cols_count):
        here = slice(first, first + cols_count)
        weights[here] = dot_t(unit, coupling[:, here]).astype(bf16)
    weights[turned:] = jnp.transpose(coupling[:, turned:])
    rates[0:1] = growth[...]
    rates[1:2] = dissipation[...]


def second_kernel(
    share,
    field_in,
    incoming,
    into,
    lists,
    taken,
    sea,
    rates,
    ranks,
    picks,
    winds,
    pieces,
    blown,
    field,
    moved,
    faces,
    columns,
):
    rows_count, bins, cols_count = field.shape
    tiles, _, _ = columns.shape
    sea_count = tiles * LANES
    terms = split(incoming[...])

    def take(row):
        got = joined(dot(terms, landing(row, into, lists, cols_count)))
        field[row] = jnp.where(taken[row] * rates[12, 0:1] > 0.5, got, field_in[row])

    each(rows_count, take)
    advance(field, moved, faces, sea, coefs_of(rates, 2), coefs_of(rates, 3))

    def at_sea(row):
        terms = jnp.concatenate([split(field[row]), split(eight(winds[row]))], axis=0)
        return dot(terms, picked(row, ranks, picks, sea_count))

    total = total_of(rows_count, (2 * bins + 2 * SUBLANES, sea_count), at_sea)
    blown[...] = joined(total[2 * bins :])
    total = joined(total[: 2 * bins])
    for tile in range(tiles):
        columns[tile] = total[:, tile * LANES : (tile + 1) * LANES]
    groups = LANES // share
    block = pieces.shape[0] // (tiles * groups)
    lane_group = lax.broadcasted_iota(jnp.int32, (block, LANES), 1) // share

    def fold(tile):
        parts = []
        for q in range(groups):
            part = columns[tile, pl.ds(q, block, stride=groups)]
            parts.append(pltpu.roll(part, q * share, 1) if q else part)
        for j in range(groups):
            piece = parts[-j % groups]
            for g in range(1, groups):
                piece = jnp.where(lane_group == g, parts[(g - j) % groups], piece)
            pieces[rows_of(tile * groups + j, block)] = piece

    each(tiles, fold)


def integrate_kernel(share, pieces, weights, rates, blown, out, values, parts):
    size = weights.shape[0]
    devices = blown.shape[1] // share
    groups = LANES // share
    block = pieces.shape[0] // devices
    bins = size // devices
    even = bins == groups * block

    def bins_of(device, q):
        return pl.ds(device * bins + q, block, stride=groups)

    me = lax.axis_index("bin")
    shift = lax.rem(me, groups)

    def unfold(device):
        for q in range(groups):
            values[bins_of(device, q)] = pieces[rows_of(device, block)]

    if even:
        for q in range(groups):
            values[pl.ds(q, devices * block, stride=groups)] = pieces[...]
    else:
        pl.loop(0, devices)(unfold)
    turned = jnp.transpose(values[0:size])
    group = lax.broadcasted_iota(jnp.int32, (share, size), 1) % bins % groups
    now = turned[0:share]
    for g in range(1, groups):
        here = group == lax.rem(g + groups - shift, groups)
        now = jnp.where(here, turned[g * share : (g + 1) * share], now)
    mine = pltpu.roll(blown[...], blown.shape[1] - me * share, 1)
    push = 1.0 + source_dt * (rates[0:1] * column(mine[0:1, 0:share]))
    drag = source_dt * rates[1:2]
    for repeat in range(SRC):
        terms = now.astype(bf16)
        linear = [dot(terms, weights[:, at : at + CHUNK]) for at in range(0, size, CHUNK)]
        linear = jnp.concatenate(linear, axis=1)
        mean = jnp.sum(now * now, axis=1, keepdims=True) * (1.0 / size)
        spread = jnp.sqrt(mean + tiny_add)
        now = (now * push + source_dt * linear) / (1.0 + drag * spread)
    values[0:size] = jnp.transpose(jnp.concatenate([now] * groups, axis=0))

    def fold(device):
        for q in range(groups):
            parts[q, rows_of(device, block)] = values[bins_of(device, q)]

    if not even:
        pl.loop(0, devices)(fold)
    lane_group = lax.broadcasted_iota(jnp.int32, out.shape, 1) // share
    result = None
    for q in range(groups):
        part = values[pl.ds(q, devices * block, stride=groups)] if even else parts[q]
        result = part if q == 0 else jnp.where(lane_group == lax.rem(q + shift, groups), part, result)
    out[...] = result


def spread_kernel(share, pieces, place, out, columns, done, left):
    tiles, bins, _ = columns.shape
    groups = LANES // share
    block = pieces.shape[0] // (tiles * groups)
    sea_count = tiles * LANES
    points = place.shape[1]
    rows_count, cols_count = grid_shape(points)
    lane_group = lax.broadcasted_iota(jnp.int32, (block, LANES), 1) // share
    if groups * block < bins:
        columns[:, groups * block :] = jnp.zeros((tiles, bins - groups * block, LANES), f32)

    def unfold(tile):
        parts = [pieces[rows_of(tile * groups + j, block)] for j in range(groups)]
        for q in range(groups):
            part = parts[-q % groups]
            for g in range(1, groups):
                part = jnp.where(lane_group == g, parts[(g - q) % groups], part)
            if q:
                part = pltpu.roll(part, LANES - q * share, 1)
            columns[tile, pl.ds(q, block, stride=groups)] = part

    each(tiles, unfold)
    terms = jnp.concatenate([split(columns[tile]) for tile in range(tiles)], axis=1)

    def scatter(row):
        here = span(row, cols_count)
        picks = one_hot(sea_count, place[0:1, here] - 1)
        done[:, here] = joined(dot(terms, picks))
        leave(row).start()

    def leave(row):
        here = span(row, cols_count)
        return pltpu.make_async_copy(done.at[:, here], out.at[:, here], left.at[row])

    each(rows_count, scatter)
    each(rows_count, lambda row: leave(row).wait())


def call(kernel, outs, scratch, operands, flops, apart=(), direct=False):
    held = sum(x.size * x.dtype.itemsize for x in operands)
    single = not isinstance(outs, list)
    shapes = [jax.ShapeDtypeStruct(*out) for out in ([outs] if single else outs)]
    held += sum(x.size * x.dtype.itemsize for x in shapes)
    own = sum(4 * math.prod(getattr(x, "shape", ())) for x in scratch)
    in_vmem = pl.BlockSpec(memory_space=pltpu.VMEM)
    places = [pl.BlockSpec(memory_space=pltpu.HBM) if x in apart else in_vmem for x in range(len(operands))]
    operands = [
        x if x.size == 1 else pltpu.with_memory_space_constraint(x, place.memory_space)
        for x, place in zip(operands, places)
    ]
    return pl.pallas_call(
        kernel,
        out_shape=shapes[0] if single else shapes,
        in_specs=places,
        out_specs=(pl.BlockSpec(memory_space=pltpu.HBM) if direct else in_vmem) if single else [in_vmem] * len(shapes),
        scratch_shapes=scratch,
        compiler_params=pltpu.CompilerParams(vmem_limit_bytes=min(60 << 20, (4 << 20) + held + own)),
        cost_estimate=pl.CostEstimate(flops=flops, bytes_accessed=held, transcendentals=0),
    )(*operands)


def local(
    spectra,
    courant,
    coupling,
    growth,
    dissipation,
    wind,
    neighbours,
    wet_mask,
    send_list,
    recv_list,
    substep_count,
):
    devices = lax.axis_size("bin")
    field = spectra[0]
    bins_here, points = field.shape
    rows_count, cols_count = grid_shape(points)
    sea_count = points // 2
    listed = send_list.shape[1]
    share = sea_count // devices
    groups = LANES // share
    block = -(-bins_here // groups)
    bins = up_to(groups * block, SUBLANES)
    size = devices * bins_here
    extra = bins - bins_here
    if extra:
        field = jnp.pad(field, ((0, extra), (0, 0)))
        courant = jnp.pad(courant, ((0, 0), (0, extra)))
    def transpose_all(pieces):
        pieces = pieces.reshape(devices, 1, block * LANES)
        pieces = lax.all_to_all(pieces, "bin", split_axis=0, concat_axis=0)
        return pieces.reshape(devices * block, LANES)

    def swap(array):
        return lax.ppermute(array, "nest", [(0, 1), (1, 0)])

    spectra_b, send_b = swap(field), swap(send_list)
    grid = (rows_count, bins, cols_count)
    row_of = (rows_count, 1, cols_count)
    steps = call(
        count_kernel, ((SUBLANES, cols_count), f32), [], (substep_count.reshape(1, 1),), 10**9
    )
    early = (
        field,
        neighbours[0],
        wet_mask,
        send_list,
        recv_list,
    )
    kept_into = rows_count if points * listed <= 1 << 22 else 1
    order, rank, base, into, sea, taken, lists = call(
        prepare_kernel,
        [
            (row_of, jnp.int32),
            (row_of, jnp.int32),
            (grid, f32),
            ((kept_into, listed, cols_count), bf16),
            (row_of, f32),
            (row_of, f32),
            ((2, listed), jnp.int32),
        ],
        [],
        early,
        10**9,
    )
    field, outgoing, rates = call(
        first_kernel,
        [(grid, f32), ((bins, listed), f32), ((13, bins, cols_count), f32)],
        [pltpu.VMEM(grid, f32)] * 2,
        (base, into, sea, lists, spectra_b, send_b, courant, steps),
        10**8,
    )
    incoming = swap(outgoing)
    kept = rows_count if points * sea_count <= 1 << 22 else 1
    ranks, picks, place, winds, weights, source_rates = call(
        places_kernel,
        [
            (row_of, f32),
            ((kept, cols_count, sea_count), bf16),
            ((1, points), jnp.int32),
            (row_of, f32),
            ((size, size), bf16),
            ((2, size), f32),
        ],
        [],
        (rank, order, wind, sea, coupling, growth.reshape(1, size), dissipation.reshape(1, size)),
        10**9,
    )
    tiles = sea_count // LANES
    pieces, blown = call(
        functools.partial(second_kernel, share),
        [((devices * block, LANES), f32), ((SUBLANES, sea_count), f32)],
        [*[pltpu.VMEM(grid, f32)] * 3, pltpu.VMEM((tiles, bins, LANES), f32)],
        (field, incoming, into, lists, taken, sea, rates, ranks, picks, winds),
        10**9,
    )
    pieces = transpose_all(pieces)
    pieces = call(
        functools.partial(integrate_kernel, share),
        ((devices * block, LANES), f32),
        [
            pltpu.VMEM((size + up_to(groups * block, SUBLANES), LANES), f32),
            pltpu.VMEM((groups, devices * block, LANES), f32),
        ],
        (pieces, weights, source_rates, blown),
        10**9,
    )
    pieces = transpose_all(pieces)
    result = call(
        functools.partial(spread_kernel, share),
        ((bins, points), f32),
        [
            pltpu.VMEM((tiles, bins, LANES), f32),
            pltpu.VMEM((bins, points), f32),
            pltpu.SemaphoreType.DMA((rows_count,)),
        ],
        (pieces, place),
        10**8,
        direct=True,
    )
    return result[None, :bins_here]


def solution(mesh):
    in_specs = (
        P("nest", "bin", None),
        P(None, "bin"),
        P(),
        P(),
        P(),
        P("nest", None),
        P("nest", None, None),
        P("nest", None),
        P("nest", None),
        P("nest", None),
        P("nest"),
    )
    out_specs = P("nest", "bin", None)
    return jax.shard_map(local, mesh=mesh, in_specs=in_specs, out_specs=out_specs, check_vma=False)
```

```python
import functools
import math

import jax
import jax.numpy as jnp
from jax import lax
from jax.experimental import pallas as pl
from jax.experimental.pallas import tpu as pltpu
from jax.sharding import PartitionSpec as P

SUBSTEPS = 2
SRC = 5
LANES = 128
SUBLANES = 8
CHUNK = 640

source_dt = 0.25
tiny_add = 1e-06
f32 = jnp.float32
bf16 = jnp.bfloat16


def up_to(value, unit):
    return -(-value // unit) * unit


def grid_shape(points):
    cols_count = min(256, points // 4)
    return points // cols_count, cols_count


def dot(left, right):
    return jnp.dot(left, right, preferred_element_type=f32)


def dot_t(left, right):
    return lax.dot_general(left, right, (((1,), (1,)), ((), ())), preferred_element_type=f32)


def split(values):
    rest = values - values.astype(bf16).astype(f32)
    return jnp.concatenate([values, rest], axis=0).astype(bf16)


def joined(terms):
    half = terms.shape[0] // 2
    return terms[:half] + terms[half:]


def marked(at, index):
    same = at.astype(jnp.int16) == jnp.broadcast_to(index, at.shape).astype(jnp.int16)
    return jnp.where(same, jnp.ones(at.shape, bf16), jnp.zeros(at.shape, bf16))


def one_hot(rows, index):
    return marked(lax.broadcasted_iota(jnp.int32, (rows, index.shape[1]), 0), index)


def column(row):
    size = row.shape[1]
    at = lax.broadcasted_iota(jnp.int32, (size, size), 0)
    across = lax.broadcasted_iota(jnp.int32, (size, size), 1)
    return jnp.sum(jnp.where(at == across, row, 0.0), axis=1, keepdims=True)


def each(count, body):
    if count <= 16:
        for step in range(count):
            body(step)
    else:
        pl.loop(0, count)(body)


def total_of(count, shape, term):
    total = jnp.zeros(shape, f32)
    if count <= 16:
        for step in range(count):
            total = total + term(step)
        return total
    return lax.fori_loop(0, count, lambda step, total: total + term(step), total)


def span(start, size):
    if isinstance(start, int):
        return pl.ds(start * size, size)
    return pl.ds(pl.multiple_of(start * size, size), size)


def rows_of(start, size):
    return pl.ds(start * size, size)


def rows_stacked(tiles):
    at = lax.broadcasted_iota(jnp.int32, (SUBLANES, LANES), 0)
    stacked = eight(tiles[0])
    for k in range(1, len(tiles)):
        stacked = jnp.where(at == k, eight(tiles[k]), stacked)
    return stacked


def tiles_of(row):
    return [row[:, k * LANES : (k + 1) * LANES] for k in range(row.shape[1] // LANES)]


def taken_from(tables, index):
    lane, tile = index & (LANES - 1), index >> (LANES - 1).bit_length()
    found = None
    for k, table in enumerate(tables):
        here = jnp.take_along_axis(eight(table), lane, axis=1, mode="promise_in_bounds")
        found = here if k == 0 else jnp.where(tile == k, here, found)
    return found


def look_up(table, index):
    count = index.shape[1] // LANES
    found = taken_from(tiles_of(table), rows_stacked(tiles_of(index)))
    return jnp.concatenate([found[k : k + 1] for k in range(count)], axis=1)


def walk(tables, order, rank):
    rows_count, _, cols_count = order.shape
    count = cols_count // LANES
    bits = (cols_count - 1).bit_length()
    at = lax.broadcasted_iota(jnp.int32, (SUBLANES, LANES), 0)
    lane = lax.broadcasted_iota(jnp.int32, (SUBLANES, LANES), 1)
    point = (at % count) * LANES + lane
    column_at = lane * count + at % count

    def doubled(pointers, near):
        for bit in range(bits - 1):
            far = taken_from([pointers[k : k + 1] for k in range(count)], pointers)
            pointers = jnp.where((at >= count) & ((near >> bit) & 1 == 0), pointers, far)
        return [pointers[count + k : count + k + 1] for k in range(count)]

    def stopped(pointers):
        pointers = jnp.where(point == 0, 0, pointers)
        steps = jnp.where(point == 0, 0, 1)
        for bit in range(bits - 1):
            both = (steps << bits) + pointers
            back = taken_from([both[k : k + 1] for k in range(count)], pointers)
            steps = steps + (back >> bits)
            pointers = back & ((1 << bits) - 1)
        return steps, pointers == 0

    east, west = (rows_stacked(tiles_of(tables[k : k + 1, 0:cols_count])) for k in range(2))
    last = jnp.broadcast_to(tables[1:2, 0:1], (SUBLANES, LANES))
    onward = doubled(jnp.where(at < count, east, 0), column_at)
    backward = doubled(jnp.where(at < count, west, last), cols_count - 1 - column_at)
    near = column_at < 1 << (bits - 1)
    found = [jnp.where(near[k : k + 1], onward[k], backward[k]) for k in range(count)]
    order[0] = jnp.concatenate(found, axis=1)
    by_west, reached = stopped(west)
    by_east, _ = stopped(east)
    steps = jnp.where(reached, by_west, cols_count - by_east)
    steps = steps % count * LANES + steps // count
    rank[0] = jnp.concatenate([steps[k : k + 1] for k in range(count)], axis=1)

    def north(row):
        return tables[2:3, span(row, cols_count)] - (row + 1) * cols_count

    def south(row):
        return tables[3:4, span(row, cols_count)] - (row - 1) * cols_count

    if rows_count <= 16:
        there, back = north(0), south(1)
        for row in range(1, rows_count):
            order[row] = look_up(there, order[0])
            rank[row] = look_up(rank[0], back)
            if row + 1 < rows_count:
                there, back = look_up(north(row), there), look_up(back, south(row + 1))
    else:

        def next_row(row):
            order[row + 1] = look_up(north(row), order[row])
            rank[row + 1] = look_up(rank[row], south(row + 1))

        each(rows_count - 1, next_row)


def grid_places(listed, rank):
    rows_count, _, cols_count = rank.shape
    tiles = tiles_of(listed)
    found = []
    for tile in tiles:
        index = eight(tile)

        def column_in(row, best):
            first = row * cols_count
            within = jnp.clip(index - first, 0, cols_count - 1)
            here = taken_from(tiles_of(rank[row]), within)
            return jnp.where(index - first == within, here + first, best)

        best = jnp.zeros((SUBLANES, LANES), jnp.int32)
        if rows_count <= 16:
            for row in range(rows_count):
                best = column_in(row, best)
        else:
            best = lax.fori_loop(0, rows_count, column_in, best)
        found.append(best[0:1])
    return jnp.concatenate(found, axis=1)


def down(row):
    wide = jnp.broadcast_to(row.astype(f32), (LANES, row.shape[1]))
    return jnp.transpose(wide).astype(jnp.int32)


def one_hot_across(index, first, count):
    lane = lax.broadcasted_iota(jnp.int32, index.shape, 1)
    tiles = [
        marked(lane, index - (first + tile * LANES))
        for tile in range(count // LANES)
    ]
    return jnp.concatenate(tiles, axis=1)


def eight(row):
    return jnp.broadcast_to(row, (SUBLANES, row.shape[1]))


def face_at(cell, onward, slope, other, coefs):
    _, near, far = coefs
    estimate = cell + near * slope + far * other
    return jnp.clip(estimate, jnp.minimum(cell, onward), jnp.maximum(cell, onward))


def ahead(tiles):
    return tiles[1:] + [pltpu.roll(tiles[0], LANES - 1, 1)]


def behind(tiles):
    return [pltpu.roll(tiles[-1], 1, 1)] + tiles[:-1]


def moved_east(cells, coefs):
    rate = coefs[0]
    onward = ahead(cells)
    slopes = [b - a for a, b in zip(cells, onward)]
    others = [jnp.where(rate >= 0.0, a, b) for a, b in zip(behind(slopes), ahead(slopes))]
    faces = [face_at(*values, coefs) for values in zip(cells, onward, slopes, others)]
    return [a - rate * (b - c) for a, b, c in zip(cells, faces, behind(faces))]


def advance(field, moved, faces, sea, east, north):
    rows_count, bins, cols_count = field.shape
    if rows_count <= 16:
        for first in range(0, bins, SUBLANES):
            here = slice(first, first + SUBLANES)
            to_east, to_north = ([x[here, :LANES] for x in coefs] for coefs in (east, north))
            forward = to_north[0] >= 0.0
            rows = [moved_east(tiles_of(field[row, here]), to_east) for row in range(rows_count)]
            for k in range(cols_count // LANES):
                cells = [tiles[k] for tiles in rows]
                onward = cells[1:] + cells[:1]
                slopes = [b - a for a, b in zip(cells, onward)]
                over = [
                    face_at(
                        cells[row],
                        onward[row],
                        slopes[row],
                        jnp.where(forward, slopes[row - 1], slopes[(row + 1) % rows_count]),
                        to_north,
                    )
                    for row in range(rows_count)
                ]
                there = slice(k * LANES, (k + 1) * LANES)
                for row in range(rows_count):
                    change = to_north[0] * (over[row] - over[row - 1])
                    field[row, here, there] = (cells[row] - change) * sea[row, :, there]
        return

    def to_east(row):
        tiles = moved_east(tiles_of(field[row]), [x[:, :LANES] for x in east])
        moved[row] = jnp.concatenate(tiles, axis=1)

    def over_row(row):
        first, second, last = (moved[(row + k + rows_count) % rows_count] for k in (1, 2, -1))
        cell = moved[row]
        other = jnp.where(north[0] >= 0.0, cell - last, second - first)
        faces[row] = face_at(cell, first, first - cell, other, north)

    def to_north(row):
        last = (row - 1 + rows_count) % rows_count
        field[row] = (moved[row] - north[0] * (faces[row] - faces[last])) * sea[row]

    for step in (to_east, over_row, to_north):
        each(rows_count, step)


def coefs_of(rates, which):
    return [rates[3 * which + k] for k in range(3)]


def landing(row, into, lists, cols_count):
    if into.shape[0] > 1:
        return into[row]
    return one_hot_across(down(lists[1:2]), row * cols_count, cols_count)


def count_kernel(steps_in, steps):
    steps[...] = jnp.broadcast_to(steps_in[...].astype(f32), steps.shape)


def prepare_kernel(
    spectra,
    tables,
    wet,
    send,
    recv,
    order,
    rank,
    base,
    into,
    sea,
    taken,
    lists,
):
    rows_count, bins, cols_count = base.shape
    listed = send.shape[1]
    walk(tables, order, rank)
    lists[0:1] = grid_places(send[...], rank)
    lists[1:2] = grid_places(recv[...], rank)
    recv_down = down(lists[1:2])

    def place(row):
        own = one_hot(cols_count, order[row])
        here = one_hot_across(recv_down, row * cols_count, cols_count)
        if into.shape[0] > 1:
            into[row] = here
        got = dot(jnp.ones((SUBLANES, listed), bf16), here)[0:1]
        taken[row] = got
        covered = look_up(wet[0:1, span(row, cols_count)], order[row]).astype(f32)
        sea[row] = covered
        values = joined(dot(split(spectra[:, span(row, cols_count)]), own))
        base[row] = values * (covered * (1.0 - got))

    each(rows_count, place)


def first_kernel(
    base,
    into,
    sea,
    lists,
    spectra_b,
    send_b,
    courant,
    steps,
    field,
    outgoing,
    rates,
    moved,
    faces,
):
    rows_count, bins, cols_count = base.shape
    listed = lists.shape[1]
    second = jnp.where(steps[0:1] > 1.0, 1.0, 0.0)
    for which in range(2):
        rate = column(courant[which : which + 1, :]) / steps[0:1]
        for k, value in enumerate((rate, rate * second)):
            at = 3 * (2 * k + which)
            rates[at] = jnp.broadcast_to(value, (bins, cols_count))
            bend = (1.0 - rates[at] * rates[at]) * (1.0 / 6.0)
            bend = jnp.where(rates[at] >= 0.0, bend, -bend)
            rates[at + 1] = 0.5 - 0.5 * rates[at] - bend
            rates[at + 2] = bend
    rates[12] = jnp.broadcast_to(second, (bins, cols_count))

    def sent(row):
        own = one_hot(cols_count, send_b[...] - row * cols_count)
        return dot(split(spectra_b[:, span(row, cols_count)]), own)

    incoming = total_of(rows_count, (2 * bins, listed), sent).astype(bf16)

    def take(row):
        field[row] = base[row] + joined(dot(incoming, landing(row, into, lists, cols_count)))

    each(rows_count, take)
    advance(field, moved, faces, sea, coefs_of(rates, 0), coefs_of(rates, 1))

    def sending(row):
        return dot(split(field[row]), one_hot(cols_count, lists[0:1] - row * cols_count))

    outgoing[...] = joined(total_of(rows_count, (2 * bins, listed), sending))


def picked(row, ranks, picks, sea_count):
    if picks.shape[0] == ranks.shape[0]:
        return picks[row]
    return one_hot_across(down(ranks[row] - 1.0), 0, sea_count)


def places_kernel(rank, sea, coupling, growth, dissipation, ranks, picks, place, weights, rates):
    rows_count, _, cols_count = rank.shape
    sea_count = picks.shape[2]
    at = lax.broadcasted_iota(jnp.int32, (cols_count, cols_count), 0)
    across = lax.broadcasted_iota(jnp.int32, (cols_count, cols_count), 1)
    upper = jnp.where(at <= across, 1.0, 0.0).astype(bf16)

    def number(row, before):
        here = sea[row]
        number_of = dot(eight(here).astype(bf16), upper)[0:1] + before
        number_of = jnp.where(here > 0.0, number_of, 0.0)
        ranks[row] = number_of
        if picks.shape[0] == rows_count:
            picks[row] = one_hot_across(down(number_of - 1.0), 0, sea_count)
        place[0:1, span(row, cols_count)] = look_up(number_of.astype(jnp.int32), rank[row])
        return before + jnp.sum(here, axis=1, keepdims=True)

    before = jnp.zeros((1, 1), f32)
    if rows_count <= 16:
        for row in range(rows_count):
            before = number(row, before)
    else:
        lax.fori_loop(0, rows_count, number, before)
    turned = min(2, weights.shape[0] // cols_count) * cols_count
    unit = jnp.where(at == across, 1.0, 0.0).astype(bf16)
    for first in range(0, turned, cols_count):
        here = slice(first, first + cols_count)
        weights[here] = dot_t(unit, coupling[:, here]).astype(bf16)
    weights[turned:] = jnp.transpose(coupling[:, turned:])
    rates[0:1] = growth[...].reshape(1, growth.shape[0])
    rates[1:2] = dissipation[...].reshape(1, growth.shape[0])


def second_kernel(
    share,
    field_in,
    incoming,
    into,
    lists,
    taken,
    sea,
    rates,
    ranks,
    picks,
    order,
    wind,
    pieces,
    blown,
    field,
    moved,
    faces,
    columns,
):
    rows_count, bins, cols_count = field.shape
    tiles, _, _ = columns.shape
    sea_count = tiles * LANES
    terms = split(incoming[...])

    def take(row):
        got = joined(dot(terms, landing(row, into, lists, cols_count)))
        field[row] = jnp.where(taken[row] * rates[12, 0:1] > 0.5, got, field_in[row])

    each(rows_count, take)
    advance(field, moved, faces, sea, coefs_of(rates, 2), coefs_of(rates, 3))

    def at_sea(row):
        by_grid = look_up(wind[0:1, span(row, cols_count)], order[row])
        terms = jnp.concatenate([split(field[row]), split(eight(by_grid))], axis=0)
        return dot(terms, picked(row, ranks, picks, sea_count))

    total = total_of(rows_count, (2 * bins + 2 * SUBLANES, sea_count), at_sea)
    blown[...] = joined(total[2 * bins :])
    total = joined(total[: 2 * bins])
    for tile in range(tiles):
        columns[tile] = total[:, tile * LANES : (tile + 1) * LANES]
    groups = LANES // share
    block = pieces.shape[0] // (tiles * groups)
    lane_group = lax.broadcasted_iota(jnp.int32, (block, LANES), 1) // share

    def fold(tile):
        parts = []
        for q in range(groups):
            part = columns[tile, pl.ds(q, block, stride=groups)]
            parts.append(pltpu.roll(part, q * share, 1) if q else part)
        for j in range(groups):
            piece = parts[-j % groups]
            for g in range(1, groups):
                piece = jnp.where(lane_group == g, parts[(g - j) % groups], piece)
            pieces[rows_of(tile * groups + j, block)] = piece

    each(tiles, fold)


def integrate_kernel(share, pieces, weights, rates, blown, out, values, parts):
    size = weights.shape[0]
    devices = blown.shape[1] // share
    groups = LANES // share
    block = pieces.shape[0] // devices
    bins = size // devices
    even = bins == groups * block

    def bins_of(device, q):
        return pl.ds(device * bins + q, block, stride=groups)

    me = lax.axis_index("bin")
    shift = lax.rem(me, groups)

    def unfold(device):
        for q in range(groups):
            values[bins_of(device, q)] = pieces[rows_of(device, block)]

    if even:
        for q in range(groups):
            values[pl.ds(q, devices * block, stride=groups)] = pieces[...]
    else:
        pl.loop(0, devices)(unfold)
    turned = jnp.transpose(values[0:size])
    group = lax.broadcasted_iota(jnp.int32, (share, size), 1) % bins % groups
    now = turned[0:share]
    for g in range(1, groups):
        here = group == lax.rem(g + groups - shift, groups)
        now = jnp.where(here, turned[g * share : (g + 1) * share], now)
    mine = pltpu.roll(blown[...], blown.shape[1] - me * share, 1)
    push = 1.0 + source_dt * (rates[0:1] * column(mine[0:1, 0:share]))
    drag = source_dt * rates[1:2]
    for repeat in range(SRC):
        terms = now.astype(bf16)
        linear = [dot(terms, weights[:, at : at + CHUNK]) for at in range(0, size, CHUNK)]
        linear = jnp.concatenate(linear, axis=1)
        mean = jnp.sum(now * now, axis=1, keepdims=True) * (1.0 / size)
        spread = jnp.sqrt(mean + tiny_add)
        now = (now * push + source_dt * linear) / (1.0 + drag * spread)
    values[0:size] = jnp.transpose(jnp.concatenate([now] * groups, axis=0))

    def fold(device):
        for q in range(groups):
            parts[q, rows_of(device, block)] = values[bins_of(device, q)]

    if not even:
        pl.loop(0, devices)(fold)
    lane_group = lax.broadcasted_iota(jnp.int32, out.shape, 1) // share
    result = None
    for q in range(groups):
        part = values[pl.ds(q, devices * block, stride=groups)] if even else parts[q]
        result = part if q == 0 else jnp.where(lane_group == lax.rem(q + shift, groups), part, result)
    out[...] = result


def spread_kernel(share, pieces, place, out, columns, done, left):
    tiles, bins, _ = columns.shape
    groups = LANES // share
    block = pieces.shape[0] // (tiles * groups)
    sea_count = tiles * LANES
    points = place.shape[1]
    rows_count, cols_count = grid_shape(points)
    lane_group = lax.broadcasted_iota(jnp.int32, (block, LANES), 1) // share
    if groups * block < bins:
        columns[:, groups * block :] = jnp.zeros((tiles, bins - groups * block, LANES), f32)

    def unfold(tile):
        parts = [pieces[rows_of(tile * groups + j, block)] for j in range(groups)]
        for q in range(groups):
            part = parts[-q % groups]
            for g in range(1, groups):
                part = jnp.where(lane_group == g, parts[(g - q) % groups], part)
            if q:
                part = pltpu.roll(part, LANES - q * share, 1)
            columns[tile, pl.ds(q, block, stride=groups)] = part

    each(tiles, unfold)
    terms = jnp.concatenate([split(columns[tile]) for tile in range(tiles)], axis=1)

    def scatter(row):
        here = span(row, cols_count)
        picks = one_hot(sea_count, place[0:1, here] - 1)
        done[:, here] = joined(dot(terms, picks))
        leave(row).start()

    def leave(row):
        here = span(row, cols_count)
        return pltpu.make_async_copy(done.at[:, here], out.at[:, here], left.at[row])

    each(rows_count, scatter)
    each(rows_count, lambda row: leave(row).wait())


def call(kernel, outs, scratch, operands, flops, apart=(), direct=False):
    held = sum(x.size * x.dtype.itemsize for x in operands)
    single = not isinstance(outs, list)
    shapes = [jax.ShapeDtypeStruct(*out) for out in ([outs] if single else outs)]
    held += sum(x.size * x.dtype.itemsize for x in shapes)
    own = sum(4 * math.prod(getattr(x, "shape", ())) for x in scratch)
    in_vmem = pl.BlockSpec(memory_space=pltpu.VMEM)
    places = [pl.BlockSpec(memory_space=pltpu.HBM) if x in apart else in_vmem for x in range(len(operands))]
    operands = [
        x if x.size == 1 else pltpu.with_memory_space_constraint(x, place.memory_space)
        for x, place in zip(operands, places)
    ]
    return pl.pallas_call(
        kernel,
        out_shape=shapes[0] if single else shapes,
        in_specs=places,
        out_specs=(pl.BlockSpec(memory_space=pltpu.HBM) if direct else in_vmem) if single else [in_vmem] * len(shapes),
        scratch_shapes=scratch,
        compiler_params=pltpu.CompilerParams(vmem_limit_bytes=min(60 << 20, (4 << 20) + held + own)),
        cost_estimate=pl.CostEstimate(flops=flops, bytes_accessed=held, transcendentals=0),
    )(*operands)


def local(
    spectra,
    courant,
    coupling,
    growth,
    dissipation,
    wind,
    neighbours,
    wet_mask,
    send_list,
    recv_list,
    substep_count,
):
    devices = lax.axis_size("bin")
    field = spectra[0]
    bins_here, points = field.shape
    rows_count, cols_count = grid_shape(points)
    sea_count = points // 2
    listed = send_list.shape[1]
    share = sea_count // devices
    groups = LANES // share
    block = -(-bins_here // groups)
    bins = up_to(groups * block, SUBLANES)
    size = devices * bins_here
    extra = bins - bins_here
    if extra:
        field = jnp.pad(field, ((0, extra), (0, 0)))
        courant = jnp.pad(courant, ((0, 0), (0, extra)))
    def transpose_all(pieces):
        pieces = pieces.reshape(devices, 1, block * LANES)
        pieces = lax.all_to_all(pieces, "bin", split_axis=0, concat_axis=0)
        return pieces.reshape(devices * block, LANES)

    def swap(array):
        return lax.ppermute(array, "nest", [(0, 1), (1, 0)])

    spectra_b, send_b = swap(field), swap(send_list)
    grid = (rows_count, bins, cols_count)
    row_of = (rows_count, 1, cols_count)
    steps = call(
        count_kernel, ((SUBLANES, cols_count), f32), [], (substep_count.reshape(1, 1),), 10**9
    )
    early = (
        field,
        neighbours[0],
        wet_mask,
        send_list,
        recv_list,
    )
    kept_into = rows_count if points * listed <= 1 << 22 else 1
    order, rank, base, into, sea, taken, lists = call(
        prepare_kernel,
        [
            (row_of, jnp.int32),
            (row_of, jnp.int32),
            (grid, f32),
            ((kept_into, listed, cols_count), bf16),
            (row_of, f32),
            (row_of, f32),
            ((2, listed), jnp.int32),
        ],
        [],
        early,
        10**9,
    )
    field, outgoing, rates = call(
        first_kernel,
        [(grid, f32), ((bins, listed), f32), ((13, bins, cols_count), f32)],
        [pltpu.VMEM(grid, f32)] * 2,
        (base, into, sea, lists, spectra_b, send_b, courant, steps),
        10**8,
    )
    incoming = swap(outgoing)
    kept = rows_count if points * sea_count <= 1 << 22 else 1
    ranks, picks, place, weights, source_rates = call(
        places_kernel,
        [
            (row_of, f32),
            ((kept, cols_count, sea_count), bf16),
            ((1, points), jnp.int32),
            ((size, size), bf16),
            ((2, size), f32),
        ],
        [],
        (rank, sea, coupling, growth, dissipation),
        10**9,
    )
    tiles = sea_count // LANES
    pieces, blown = call(
        functools.partial(second_kernel, share),
        [((devices * block, LANES), f32), ((SUBLANES, sea_count), f32)],
        [*[pltpu.VMEM(grid, f32)] * 3, pltpu.VMEM((tiles, bins, LANES), f32)],
        (field, incoming, into, lists, taken, sea, rates, ranks, picks, order, wind),
        10**9,
    )
    pieces = transpose_all(pieces)
    pieces = call(
        functools.partial(integrate_kernel, share),
        ((devices * block, LANES), f32),
        [
            pltpu.VMEM((size + up_to(groups * block, SUBLANES), LANES), f32),
            pltpu.VMEM((groups, devices * block, LANES), f32),
        ],
        (pieces, weights, source_rates, blown),
        10**9,
    )
    pieces = transpose_all(pieces)
    result = call(
        functools.partial(spread_kernel, share),
        ((bins, points), f32),
        [
            pltpu.VMEM((tiles, bins, LANES), f32),
            pltpu.VMEM((bins, points), f32),
            pltpu.SemaphoreType.DMA((rows_count,)),
        ],
        (pieces, place),
        10**8,
        direct=True,
    )
    return result[None, :bins_here]


def solution(mesh):
    in_specs = (
        P("nest", "bin", None),
        P(None, "bin"),
        P(),
        P(),
        P(),
        P("nest", None),
        P("nest", None, None),
        P("nest", None),
        P("nest", None),
        P("nest", None),
        P("nest"),
    )
    out_specs = P("nest", "bin", None)
    return jax.shard_map(local, mesh=mesh, in_specs=in_specs, out_specs=out_specs, check_vma=False)
```
